32 devices in a mesh: seq: 16 (over z, y, x), head: 2 (over core).
Axes of the slice: x: 2, y: 2, z: 4, core: 2. Of those that a mesh axis runs over, the one named last changes fastest.
Arguments:
- inputs: bfloat16 [2048, 2048], P('seq'), may hold values from -6.3 to 6.3
- doc_starts: int32 [2048], P('seq'), may hold values from 0 to 1, as said below
- decay_rate: float32 [2048, 16], P('seq', 'head'), may hold values from 0.4 to 1
- mixer_gain: bfloat16 [2048], P('seq'), may hold values from 0.5 to 1.5
- w_query: bfloat16 [2048, 2048], P('seq', 'head'), may hold values from -0.125 to 0.125
- w_key: bfloat16 [2048, 2048], P('seq', 'head'), may hold values from -0.125 to 0.125
- w_value: bfloat16 [2048, 4096], P('seq', 'head'), may hold values from -0.125 to 0.125
- w_beta: bfloat16 [2048, 16], P('seq', 'head'), may hold values from -1 to 1
- w_gating: bfloat16 [2048, 4096], P('seq', 'head'), may hold values from -0.125 to 0.125
- conv_query: bfloat16 [4, 2048], P(None, 'head'), may hold values from -3 to 3
- conv_key: bfloat16 [4, 2048], P(None, 'head'), may hold values from -3 to 3
- conv_value: bfloat16 [4, 4096], P(None, 'head'), may hold values from -3 to 3
- head_gain: bfloat16 [256], replicated, may hold values from 0.5 to 1.5
- w_output: bfloat16 [4096, 2048], P('head', 'seq'), may hold values from -0.1875 to 0.1875
- feed_gain: bfloat16 [2048], P('seq'), may hold values from 0.5 to 1.5
- w_gate: bfloat16 [2048, 5632], P('seq', 'head'), may hold values from -0.125 to 0.125
- w_up: bfloat16 [2048, 5632], P('seq', 'head'), may hold values from -0.125 to 0.125
- w_down: bfloat16 [5632, 2048], P('head', 'seq'), may hold values from -0.109375 to 0.109375
- cotangent: bfloat16 [2048, 2048], P('seq'), may hold values from -6 to 6
Outputs:
- block_out: bfloat16 [2048, 2048], P('seq')
- grad_inputs: float32 [2048, 2048], P('seq')
- grad_mixer_gain: float32 [2048], P('seq')
- grad_query: float32 [2048, 2048], P('seq', 'head')
- grad_key: float32 [2048, 2048], P('seq', 'head')
- grad_value: float32 [2048, 4096], P('seq', 'head')
- grad_beta: float32 [2048, 16], P('seq', 'head')
- grad_gating: float32 [2048, 4096], P('seq', 'head')
- grad_conv_query: float32 [4, 2048], P(None, 'head')
- grad_conv_key: float32 [4, 2048], P(None, 'head')
- grad_conv_value: float32 [4, 4096], P(None, 'head')
- grad_head_gain: float32 [256], replicated
- grad_output: float32 [4096, 2048], P('head', 'seq')
- grad_feed_gain: float32 [2048], P('seq')
- grad_gate: float32 [2048, 5632], P('seq', 'head')
- grad_up: float32 [2048, 5632], P('seq', 'head')
- grad_down: float32 [5632, 2048], P('head', 'seq')
The draws below stay inside these ranges and needn't reach their ends.
Inputs may be any that keep to these rules, and one draw needn't show every extreme that they name: `doc_starts`: document start flags; the first token of the stream always starts a document.
All inputs are finite; a program needn't handle non-finite values.
Results may differ from the reference program's by a relative error of at most 0.02.
Values may be sent and summed in bfloat16 or wider, within the bound.
No kernel may reach another device: no remote copies, remote signals or barrier semaphores. Data moves between devices by JAX's collectives and lax.ppermute only.
A program may use at most 384 MiB of HBM per device.

```python
import math
import jax
import jax.numpy as jnp
from jax import lax

D = 2048
MIXER_HEADS = 16
KEY_SIZE = 128
DV = 256
FF = 5632
CONV = 4
BLOCK = 64
TOK_DEV = 128
KDIM = 2048
VDIM = 4096
STREAM_TOKENS = 2048


def fast_heads_of(key, fast_count):
    order = jax.random.permutation(jax.random.fold_in(key, 5), MIXER_HEADS)
    return order < fast_count


def common_signs(key):
    flips = jax.random.randint(jax.random.fold_in(key, 7), (D,), 0, 2)
    return (2 * flips - 1).astype(jnp.float32)


def draw_inputs(key, part):
    signs = common_signs(key)
    key = jax.random.fold_in(key, 31)
    noise = jax.random.truncated_normal(key, -6.0, 6.0, (STREAM_TOKENS, D), jnp.float32)
    return (noise + 0.3 * signs[None, :]).astype(jnp.bfloat16)


def draw_w_beta(key, part):
    fast_count = MIXER_HEADS // 2
    fast_heads = fast_heads_of(key, fast_count)
    signs = common_signs(key)
    key = jax.random.fold_in(key, 37)
    noise = jax.random.truncated_normal(key, -4.0, 4.0, (D, MIXER_HEADS), jnp.float32) * (0.7 / math.sqrt(D))
    offset = jnp.where(fast_heads, 0.0, -24.0)
    return (noise + signs[:, None] * offset[None, :] / D).astype(jnp.bfloat16)


def draw_doc_starts(key, part):
    key = jax.random.fold_in(key, 11)
    random_keys_split = jax.random.split(key, 3)
    opening = jax.random.randint(random_keys_split[0], (), 1, TOK_DEV)
    closing = jax.random.randint(random_keys_split[1], (), STREAM_TOKENS - TOK_DEV + 1, STREAM_TOKENS)
    places = jnp.arange(STREAM_TOKENS)
    scattered = jax.random.randint(random_keys_split[2], (STREAM_TOKENS,), 0, 8) == 0
    outside = (places < opening) | (places > closing)
    start_flags = (places == 0) | (places == opening) | (places == closing) | scattered & outside
    return start_flags.astype(jnp.int32)


def draw_decay_rate(key, part):
    fast_count = MIXER_HEADS // 2
    fast_heads = fast_heads_of(key, fast_count)
    key = jax.random.fold_in(key, 23)
    random_keys_split = jax.random.split(key, 5)
    fast_rate = jax.random.uniform(random_keys_split[0], (MIXER_HEADS,), minval=1.0 / 50.0, maxval=1.0 / 30.0)
    slow_rate = math.log(2.0) / (2.0 * STREAM_TOKENS)
    baseline_decay = jnp.where(fast_heads, fast_rate, slow_rate)
    jitter_amount = jnp.exp(jax.random.uniform(random_keys_split[1], (STREAM_TOKENS // TOK_DEV, TOK_DEV, MIXER_HEADS), minval=-0.7, maxval=0.7))
    device_factor = jnp.exp(jax.random.uniform(random_keys_split[2], (STREAM_TOKENS // TOK_DEV, 1, MIXER_HEADS), minval=-0.7, maxval=0.7))
    jitter_amount = (jitter_amount * device_factor).reshape(STREAM_TOKENS, MIXER_HEADS)
    decay_spikes = jax.random.randint(random_keys_split[3], (STREAM_TOKENS, MIXER_HEADS), 0, max(STREAM_TOKENS // 2, 1)) == 0
    spike_keep_factor = jax.random.uniform(random_keys_split[4], (STREAM_TOKENS, MIXER_HEADS), minval=0.5, maxval=0.8)
    decay_values = jnp.exp(-baseline_decay * jitter_amount) * jnp.where(decay_spikes, spike_keep_factor, 1.0)
    return decay_values.astype(jnp.float32)


def raised(array, own_key, source, target, parts, factor):
    owner, partner = [(jnp.arange(array.shape[position]) // (array.shape[position] // parts)).reshape([-1 if axis == position else 1 for axis in range(array.ndim)]) for position in (source, target)]
    chosen = jax.random.permutation(own_key, parts)[partner]
    strong = (owner == chosen) | (owner == (partner + parts // 2) % parts)
    return jnp.where(strong, factor * array, array)


def levels(key, shape, cuts, low, top_value):
    level, own = 1.0, jax.random.fold_in(key, 6)
    for position, shards_of in cuts:
        heights = jnp.exp(jax.random.uniform(jax.random.fold_in(own, position), (shards_of,), jnp.float32, low / len(cuts), top_value / len(cuts)))
        level = level * jnp.repeat(heights, shape[position] // shards_of).reshape([-1 if axis == position else 1 for axis in range(len(shape))])
    return level


def normal_values(stream_key, dims, spread, bound, cuts=(), kind=jnp.bfloat16):
    level = levels(stream_key, dims, cuts, -0.22, 0.18) if cuts else 1.0
    entries = jax.random.normal(stream_key, dims, jnp.float32) * spread * level
    return jnp.minimum(jnp.maximum(entries, -bound), bound).astype(kind)


def bell_draw_with(rng, dims, deviation, most, cuts, heavy, dtype=jnp.bfloat16):
    array = deviation * jax.random.normal(rng, dims, jnp.float32)
    if cuts:
        array = array * levels(rng, dims, cuts, -0.22, 0.18)
    return jnp.clip(raised(array, jax.random.fold_in(rng, 3), *heavy), -most, most).astype(dtype)


def setup_inputs(seed: int = 0) -> dict:
    key_of = jax.random.split(jax.random.key(seed), 20)
    inputs = draw_inputs(jax.random.fold_in(key_of[19], 71), 0)
    doc_starts = draw_doc_starts(jax.random.fold_in(key_of[19], 71), 0)
    decay_rate = draw_decay_rate(jax.random.fold_in(key_of[19], 71), 0)
    mixer_gain = jnp.clip(1.0 + 0.1 * jax.random.normal(key_of[3], (D,), jnp.float32), 0.5, 1.5).astype(jnp.bfloat16)
    w_query = normal_values(key_of[4], (D, KDIM), D ** -0.5, 0.125, ((0, 16), (1, 2)))
    w_key = normal_values(key_of[5], (D, KDIM), D ** -0.5, 0.125, ((0, 16), (1, 2)))
    w_value = normal_values(key_of[6], (D, VDIM), D ** -0.5, 0.125, ((0, 16), (1, 2)))
    w_beta = draw_w_beta(jax.random.fold_in(key_of[19], 71), 0)
    w_gating = normal_values(key_of[8], (D, VDIM), D ** -0.5, 0.125, ((0, 16), (1, 2)))
    conv_query = normal_values(key_of[9], (CONV, KDIM), CONV ** -0.5, 3.0, ((1, 2),))
    conv_key = normal_values(key_of[10], (CONV, KDIM), CONV ** -0.5, 3.0, ((1, 2),))
    conv_value = normal_values(key_of[11], (CONV, VDIM), CONV ** -0.5, 3.0, ((1, 2),))
    head_gain = jnp.clip(1.0 + 0.1 * jax.random.normal(key_of[12], (DV,), jnp.float32), 0.5, 1.5).astype(jnp.bfloat16)
    w_output = normal_values(key_of[13], (VDIM, D), (VDIM // 4) ** -0.5, 0.1875, ((0, 2), (1, 16)))
    feed_gain = jnp.clip(1.0 + 0.1 * jax.random.normal(key_of[14], (D,), jnp.float32), 0.5, 1.5).astype(jnp.bfloat16)
    w_gate = normal_values(key_of[15], (D, FF), D ** -0.5, 0.125, ((0, 16), (1, 2)))
    w_up = normal_values(key_of[16], (D, FF), D ** -0.5, 0.125, ((0, 16), (1, 2)))
    w_down = normal_values(key_of[17], (FF, D), (FF // 2) ** -0.5, 0.109375, ((0, 2), (1, 16)))
    cotangent = bell_draw_with(key_of[18], (STREAM_TOKENS, D), 1.0, 6.0, ((0, 16),), (0, 1, 16, 2.0))
    return {"inputs": inputs, "doc_starts": doc_starts, "decay_rate": decay_rate, "mixer_gain": mixer_gain, "w_query": w_query, "w_key": w_key, "w_value": w_value, "w_beta": w_beta, "w_gating": w_gating, "conv_query": conv_query, "conv_key": conv_key, "conv_value": conv_value, "head_gain": head_gain, "w_output": w_output, "feed_gain": feed_gain, "w_gate": w_gate, "w_up": w_up, "w_down": w_down, "cotangent": cotangent}


EXACT_PRECISION = lax.Precision.HIGHEST
EPSILON = 1e-06

@jax.custom_vjp
def low(v):
    return lax.optimization_barrier(v.astype(jnp.bfloat16)).astype(jnp.float32)

@jax.custom_vjp
def low_back(v):
    return v

def low_keep(v):
    return (low(v), None)

def low_pass(kept, grad):
    return (grad,)

def back_keep(v):
    return (v, None)

def back_low(kept, grad):
    return (low(grad),)
low.defvjp(low_keep, low_pass)
low_back.defvjp(back_keep, back_low)

def precise_dot(left_side, right_side):
    return jnp.dot(left_side, right_side, precision=EXACT_PRECISION, preferred_element_type=jnp.float32)

def scale_norm(values, gain_vec):
    return values * lax.rsqrt(lax.optimization_barrier(jnp.mean(values * values, axis=-1, keepdims=True)) + EPSILON) * gain_vec

def unit_rows(values):
    return values * lax.rsqrt(lax.optimization_barrier(jnp.sum(values * values, axis=-1, keepdims=True)) + EPSILON)

def token_step(recurrent_state, element):
    single_query_row, single_key_row, value_row, beta_row, rate_row = element
    retrieved_values = jnp.einsum('cz,czx->cx', single_key_row, recurrent_state, precision=EXACT_PRECISION)
    recurrent_state = rate_row[:, None, None] * (recurrent_state - beta_row[:, None, None] * single_key_row[:, :, None] * retrieved_values[:, None, :]) + beta_row[:, None, None] * single_key_row[:, :, None] * value_row[:, None, :]
    produced_output = jnp.einsum('cz,czx->cx', single_query_row, recurrent_state, precision=EXACT_PRECISION) * KEY_SIZE ** (-0.5)
    return (recurrent_state, produced_output)

def recur_block(recurrent_state, pieces):
    return lax.scan(token_step, recurrent_state, pieces)

def reference(inputs, doc_starts, decay_rate, mixer_gain, w_query, w_key, w_value, w_beta, w_gating, conv_query, conv_key, conv_value, head_gain, w_output, feed_gain, w_gate, w_up, w_down, cotangent):
    block_count = max(1, STREAM_TOKENS // 4096)
    block_rows = STREAM_TOKENS // block_count
    document = jnp.cumsum(doc_starts).astype(jnp.int32)
    decay_values = decay_rate * (1 - doc_starts).astype(jnp.float32)[:, None]
    params = tuple((piece.astype(jnp.float32) for piece in (inputs, mixer_gain, w_query, w_key, w_value, w_beta, w_gating, conv_query, conv_key, conv_value, head_gain, w_output, feed_gain, w_gate, w_up, w_down)))

    def forward_pass(inputs_f, gain_one, full_query, full_key, full_value, full_beta, full_gating, taps_query, taps_key, taps_value, gain_head, full_output, gain_two, full_gate, full_up, full_down):
        conv_weights = jnp.concatenate([taps_query, taps_key, taps_value], axis=1)
        width_all = conv_weights.shape[1]

        def block_step(carried, element):
            recurrent_state, tail_rows, tail_doc = carried
            inputs_block, doc_block, rate_block = element
            normed_one = low(scale_norm(inputs_block, gain_one))
            query_pre = low_back(low(precise_dot(normed_one, full_query)))
            key_pre = low_back(low(precise_dot(normed_one, full_key)))
            value_pre = low_back(low(precise_dot(normed_one, full_value)))
            joined = jnp.concatenate([query_pre, key_pre, value_pre], axis=1)
            extended = jnp.concatenate([tail_rows, joined], axis=0)
            extended_doc = jnp.concatenate([tail_doc, doc_block])
            mixed = jnp.zeros((block_rows, width_all), jnp.float32)
            for shift_lag in range(CONV):
                keep_mask = (extended_doc[CONV - 1 - shift_lag:CONV - 1 - shift_lag + block_rows] == doc_block).astype(jnp.float32)[:, None]
                mixed = mixed + conv_weights[shift_lag] * extended[CONV - 1 - shift_lag:CONV - 1 - shift_lag + block_rows] * keep_mask
            activated = jax.nn.silu(mixed)
            query_unit = low_back(low(unit_rows(activated[:, :KDIM].reshape(block_rows, MIXER_HEADS, KEY_SIZE))))
            key_unit = low_back(low(unit_rows(activated[:, KDIM:2 * KDIM].reshape(block_rows, MIXER_HEADS, KEY_SIZE))))
            value_act = low_back(low(activated[:, 2 * KDIM:])).reshape(block_rows, MIXER_HEADS, DV)
            beta_gate = jax.nn.sigmoid(low_back(precise_dot(normed_one, full_beta)))
            pieces = tuple((piece.reshape((block_rows // BLOCK, BLOCK) + piece.shape[1:]) for piece in (query_unit, key_unit, value_act, beta_gate, rate_block)))
            recurrent_state, produced_output = lax.scan(jax.checkpoint(recur_block), recurrent_state, pieces)
            mixer_out = produced_output.reshape(block_rows, MIXER_HEADS, DV)
            gating_pre = low_back(low(precise_dot(normed_one, full_gating))).reshape(block_rows, MIXER_HEADS, DV)
            normed_out = mixer_out * lax.rsqrt(lax.optimization_barrier(jnp.mean(mixer_out * mixer_out, axis=-1, keepdims=True)) + EPSILON)
            gated_out = low_back(low((normed_out * gain_head * jax.nn.silu(gating_pre)).reshape(block_rows, VDIM)))
            middle = inputs_block + low_back(precise_dot(gated_out, full_output))
            normed_two = low(scale_norm(middle, gain_two))
            gate_lin = low_back(precise_dot(normed_two, full_gate))
            up_lin = low_back(precise_dot(normed_two, full_up))
            hidden = low_back(low(jax.nn.silu(gate_lin) * up_lin))
            result = middle + low_back(precise_dot(hidden, full_down))
            return ((recurrent_state, joined[block_rows - (CONV - 1):], doc_block[block_rows - (CONV - 1):]), result)
        start = (jnp.zeros((MIXER_HEADS, KEY_SIZE, DV), jnp.float32), jnp.zeros((CONV - 1, width_all), jnp.float32), jnp.full((CONV - 1,), -1, jnp.int32))
        elements = (inputs_f.reshape(block_count, block_rows, D), document.reshape(block_count, block_rows), decay_values.reshape(block_count, block_rows, MIXER_HEADS))
        _, results = lax.scan(jax.checkpoint(block_step), start, elements)
        return results.reshape(STREAM_TOKENS, D)
    output, pullback = jax.vjp(forward_pass, *params)
    grads = pullback(cotangent.astype(jnp.float32))
    return (output.astype(jnp.bfloat16), grads[0], grads[1], grads[2], grads[3], grads[4], grads[5], grads[6], grads[7], grads[8], grads[9], grads[10], grads[11], grads[12], grads[13], grads[14], grads[15])
```

```python
import jax
import jax.numpy as jnp
from jax import lax
from jax.sharding import PartitionSpec as P
from jax.experimental import pallas as pl
from jax.experimental.pallas import tpu as pltpu

KEY_SIZE = 128
DV = 256
CONV = 4
BLOCK = 64
EPSILON = 1e-06
F32 = jnp.float32
BF16 = jnp.bfloat16
LOGIT = 2 * KEY_SIZE + 2 * DV
PACK = LOGIT + 128
MIXED = 2 * KEY_SIZE + DV
SCALE = KEY_SIZE**-0.5
UNROLL = 4


def mm(a, b, dims=((1,), (0,))):
    return lax.dot_general(a, b, (dims, ((), ())), preferred_element_type=F32)


NT = ((1,), (1,))
TN = ((0,), (0,))


def halves(a):
    high = a.astype(BF16)
    return high, (a - high.astype(F32)).astype(BF16)


def mm_left(a, b, dims=((1,), (0,))):
    high, low = halves(a)
    return mm(high, b, dims) + mm(low, b, dims)


def mm_right(a, b, dims=((1,), (0,))):
    high, low = halves(b)
    return mm(a, high, dims) + mm(a, low, dims)


def mm_both(a, b, dims=((1,), (0,))):
    a_high, a_low = halves(a)
    b_high, b_low = halves(b)
    return mm(a_high, b_high, dims) + (mm(a_high, b_low, dims) + mm(a_low, b_high, dims))


def block_masks():
    row = lax.broadcasted_iota(jnp.int32, (BLOCK, BLOCK), 0)
    col = lax.broadcasted_iota(jnp.int32, (BLOCK, BLOCK), 1)
    strict = row > col
    levels = []
    size = 1
    while size < BLOCK:
        levels.append(
            (row // (2 * size) == col // (2 * size)) & (row // size % 2 == 1) & (col // size % 2 == 0)
        )
        size *= 2
    return strict, levels, (row == col).astype(F32)


def unit_lower_inverses(systems, levels, eye):
    inverses = [eye - jnp.where(levels[0], system, 0.0) for system in systems]
    for level in levels[1:]:
        inner = [
            mm_both(jnp.where(level, system, 0.0), inverse)
            for system, inverse in zip(systems, inverses)
        ]
        inverses = [
            inverse - mm_both(inverse, part) for inverse, part in zip(inverses, inner)
        ]
    return inverses


def rows_of(index):
    return pl.ds(pl.multiple_of(index * BLOCK, BLOCK), BLOCK)


def row_sums(values):
    return jnp.sum(values.reshape(values.shape[0] // 8, 8, values.shape[1]), axis=0)


def beta_columns(packed):
    logit = packed[:, :1].astype(F32) + packed[:, 1:2].astype(F32)
    beta = jax.nn.sigmoid(logit)
    return beta, jnp.broadcast_to(beta, (BLOCK, 128)).T[:BLOCK]


def units_of(mixed):
    gate = jax.nn.sigmoid(mixed)
    act = mixed * gate
    query, key = act[:, :KEY_SIZE], act[:, KEY_SIZE : 2 * KEY_SIZE]
    query_scale = lax.rsqrt(jnp.sum(query * query, axis=-1, keepdims=True) + EPSILON)
    key_scale = lax.rsqrt(jnp.sum(key * key, axis=-1, keepdims=True) + EPSILON)
    return gate, act, query * query_scale, key * key_scale, query_scale, key_scale


def forward_kernel(
    place,
    pre,
    decay_grid,
    cols,
    rows,
    taps,
    head_gain,
    gated,
    mixer_out,
    mixed_out,
    inverse_out,
    state_out,
    fresh_out,
    carry_out,
    read_out,
    both_maps,
    value_part,
    out_part,
    add_part,
):
    blocks = decay_grid.shape[0]
    strict, levels, eye = block_masks()
    key_eye = (
        lax.broadcasted_iota(jnp.int32, (KEY_SIZE, KEY_SIZE), 0)
        == lax.broadcasted_iota(jnp.int32, (KEY_SIZE, KEY_SIZE), 1)
    ).astype(F32)

    def prepare(group, _):
        work = []
        for lane in range(UNROLL):
            b = group * UNROLL + lane
            here = rows_of(b)
            source = place[b]
            before = place[jnp.maximum(b - 1, 0)]
            current = pre[rows_of(source), :MIXED].astype(F32)
            edge = pre[
                pl.ds(pl.multiple_of(before * BLOCK + BLOCK - 16, 16), 16), :MIXED
            ].astype(F32)
            extended = jnp.concatenate([edge[8:], current], axis=0)
            mixed = taps[0:1] * current
            for lag in range(1, CONV):
                mixed = mixed + (taps[lag : lag + 1] * cols[here, 1 + lag : 2 + lag]) * pltpu.roll(
                    extended, lag, 0
                )[8:]
            mixed_out[here, :] = mixed
            _, act, query, key, _, _ = units_of(mixed)
            query, key, value = query.astype(BF16), key.astype(BF16), act[:, 2 * KEY_SIZE :].astype(BF16)
            beta, beta_row = beta_columns(pre[rows_of(source), LOGIT:])
            link = decay_grid[b] * beta_row
            system = jnp.where(strict, link * mm(key, key, NT), 0.0)
            mixing = (SCALE * mm(query, key, NT)) * link
            work.append((b, here, query, key, value, beta, system, mixing))
        inverses = unit_lower_inverses([item[6] for item in work], levels, eye)
        for (b, here, query, key, value, beta, system, mixing), inverse in zip(work, inverses):
            inverse_out[here, :] = inverse
            carry = cols[here, 0:1]
            tail = cols[here, 1:2] * beta
            fresh_values = mm_left(inverse, value)
            fresh_keys = mm_left(inverse * rows[b, 0:1, :], key)
            low_mixing = mixing.astype(BF16)
            read = (SCALE * carry) * query.astype(F32) - mm(low_mixing, fresh_keys.astype(BF16))
            value_part[here, :] = fresh_values
            out_part[here, :] = mm(low_mixing, fresh_values.astype(BF16))
            read_out[here, :] = read.astype(BF16)
            both_maps[b, :BLOCK] = read.astype(BF16)
            both_maps[b, BLOCK:] = fresh_keys.astype(BF16)
            carry_end = carry[BLOCK - 1 : BLOCK]
            carry_out[b] = carry_end * key_eye - mm_right(key, tail * fresh_keys, TN)
            add_part[b] = mm_right(key, tail * fresh_values, TN)
        return 0

    lax.fori_loop(0, blocks // UNROLL, prepare, 0)

    def chain(b, state):
        state_out[b] = state.astype(BF16)
        return mm_both(carry_out[b], state) + add_part[b]

    lax.fori_loop(0, blocks, chain, jnp.zeros((KEY_SIZE, DV), F32))

    def finish(group, _):
        for lane in range(UNROLL):
            b = group * UNROLL + lane
            here = rows_of(b)
            source = place[b]
            both = mm(both_maps[b], state_out[b])
            produced = both[:BLOCK] + out_part[here, :]
            fresh_out[here, :] = (value_part[here, :] - both[BLOCK:]).astype(BF16)
            mixer_out[here, :] = produced
            scale = lax.rsqrt(jnp.mean(produced * produced, axis=-1, keepdims=True) + EPSILON)
            gate = pre[rows_of(source), MIXED:LOGIT].astype(F32)
            gated[rows_of(source), :] = (
                produced * scale * head_gain[0:1] * (gate * jax.nn.sigmoid(gate))
            ).astype(BF16)
        return 0

    lax.fori_loop(0, blocks // UNROLL, finish, 0)


def backward_kernel(
    place,
    d_gated,
    pre,
    decay_grid,
    cols,
    taps,
    head_gain,
    mixer_out,
    mixed_in,
    inverse_in,
    state_in,
    fresh_in,
    carry_in,
    read_in,
    d_pre,
    grad_taps,
    grad_gain,
    d_out,
    pull_part,
    end_state,
    d_mixed,
):
    blocks = decay_grid.shape[0]
    strict, _, _ = block_masks()
    lane_index = lax.broadcasted_iota(jnp.int32, (BLOCK, PACK - LOGIT), 1)
    grad_taps[...] = jnp.zeros_like(grad_taps)
    grad_gain[...] = jnp.zeros_like(grad_gain)
    d_mixed[blocks * BLOCK :, :] = jnp.zeros((8, MIXED), F32)

    def prepare(group, _):
        for lane in range(UNROLL):
            b = group * UNROLL + lane
            here = rows_of(b)
            there = rows_of(place[b])
            grad = d_gated[there, :].astype(F32)
            gate = pre[there, MIXED:LOGIT].astype(F32)
            produced = mixer_out[here, :]
            scale = lax.rsqrt(jnp.mean(produced * produced, axis=-1, keepdims=True) + EPSILON)
            normed = produced * scale
            sig = jax.nn.sigmoid(gate)
            act = gate * sig
            weighted = grad * head_gain[0:1]
            pulled = weighted * act
            along = jnp.mean(pulled * normed, axis=-1, keepdims=True)
            low = (scale * (pulled - normed * along)).astype(BF16)
            grad_gain[...] += row_sums(grad * normed * act)
            d_pre[there, MIXED:LOGIT] = (
                weighted * normed * (sig * (1.0 + gate * (1.0 - sig)))
            ).astype(BF16)
            d_out[here, :] = low
            pull_part[b] = mm(read_in[here, :], low, TN)
        return 0

    lax.fori_loop(0, blocks // UNROLL, prepare, 0)

    def chain(step, state):
        b = blocks - 1 - step
        end_state[b] = state.astype(BF16)
        return mm_both(carry_in[b], state, TN) + pull_part[b]

    lax.fori_loop(0, blocks, chain, jnp.zeros((KEY_SIZE, DV), F32))

    def finish(group, _):
        for lane in range(UNROLL):
            b = group * UNROLL + lane
            here = rows_of(b)
            there = rows_of(place[b])
            mixed = mixed_in[here, :]
            gate, act, query_unit, key_unit, query_scale, key_scale = units_of(mixed)
            query, key = query_unit.astype(BF16), key_unit.astype(BF16)
            beta, beta_row = beta_columns(pre[there, LOGIT:])
            link = decay_grid[b] * beta_row
            mixing = (SCALE * mm(query, key, NT)) * link
            carry = cols[here, 0:1]
            tail = cols[here, 1:2] * beta
            low = d_out[here, :]
            end = end_state[b]
            start = state_in[b]
            fresh = fresh_in[here, :]
            d_fresh = mm(mixing.astype(BF16), low, TN) + tail * mm(key, end)
            d_right = mm_left(inverse_in[here, :], d_fresh.astype(BF16), TN)
            d_right_low = d_right.astype(BF16)
            d_logit = (1.0 - beta) * jnp.sum(fresh.astype(F32) * d_right, axis=-1, keepdims=True)
            pair = jnp.concatenate([low, d_right_low], axis=0)
            on_state = mm(pair, start, NT)
            on_fresh = mm(pair, fresh, NT)
            read_grad = (SCALE * on_fresh[:BLOCK]) * link
            system_grad = jnp.where(strict, -on_fresh[BLOCK:] * link, 0.0)
            d_query = (SCALE * carry) * on_state[:BLOCK] + mm(read_grad.astype(BF16), key)
            d_key = (
                mm((system_grad + system_grad.T).astype(BF16), key)
                + mm(read_grad.astype(BF16), query, TN)
                + tail * mm(fresh, end, NT)
                - carry * on_state[BLOCK:]
            )
            d_query = d_query.astype(BF16).astype(F32)
            d_key = d_key.astype(BF16).astype(F32)
            slope = gate * (1.0 + mixed * (1.0 - gate))
            d_mixed[here, :KEY_SIZE] = (
                d_query - query_unit * jnp.sum(query_unit * d_query, axis=-1, keepdims=True)
            ) * (query_scale * slope[:, :KEY_SIZE])
            d_mixed[here, KEY_SIZE : 2 * KEY_SIZE] = (
                d_key - key_unit * jnp.sum(key_unit * d_key, axis=-1, keepdims=True)
            ) * (key_scale * slope[:, KEY_SIZE : 2 * KEY_SIZE])
            d_mixed[here, 2 * KEY_SIZE :] = d_right_low.astype(F32) * slope[:, 2 * KEY_SIZE :]
            d_pre[there, LOGIT:] = jnp.where(lane_index == 0, d_logit, 0.0).astype(BF16)
        return 0

    lax.fori_loop(0, blocks // UNROLL, finish, 0)

    def unmix(group, _):
        for lane in range(UNROLL):
            b = group * UNROLL + lane
            there = rows_of(place[b])
            longer = pl.ds(pl.multiple_of(b * BLOCK, BLOCK), BLOCK + 8)
            extended = d_mixed[longer, :]
            current = pre[there, :MIXED].astype(F32)
            total = taps[0:1] * extended[:BLOCK]
            grad_taps[0] += row_sums(current * extended[:BLOCK])
            for lag in range(1, CONV):
                kept = cols[longer, 1 + lag : 2 + lag] * extended
                moved = pltpu.roll(kept, BLOCK + 8 - lag, 0)[:BLOCK]
                total = total + taps[lag : lag + 1] * moved
                grad_taps[lag] += row_sums(current * moved)
            d_pre[there, :MIXED] = total.astype(BF16)
        return 0

    lax.fori_loop(0, blocks // UNROLL, unmix, 0)


VMEM_SPEC = pl.BlockSpec(memory_space=pltpu.VMEM)
SMEM_SPEC = pl.BlockSpec(memory_space=pltpu.SMEM)


def mixer_forward(place, pre, decay_grid, cols, rows, taps, head_gain):
    tokens, blocks = pre.shape[0], decay_grid.shape[0]
    shape = jax.ShapeDtypeStruct
    return pl.pallas_call(
        forward_kernel,
        out_shape=(
            shape((tokens, DV), BF16),
            shape((tokens, DV), F32),
            shape((tokens, MIXED), F32),
            shape((tokens, BLOCK), F32),
            shape((blocks, KEY_SIZE, DV), BF16),
            shape((tokens, DV), BF16),
            shape((blocks, KEY_SIZE, KEY_SIZE), F32),
            shape((tokens, KEY_SIZE), BF16),
        ),
        in_specs=[SMEM_SPEC] + [VMEM_SPEC] * 6,
        out_specs=[VMEM_SPEC] * 8,
        scratch_shapes=[
            pltpu.VMEM((blocks, 2 * BLOCK, KEY_SIZE), BF16),
            pltpu.VMEM((tokens, DV), F32),
            pltpu.VMEM((tokens, DV), F32),
            pltpu.VMEM((blocks, KEY_SIZE, DV), F32),
        ],
        compiler_params=pltpu.CompilerParams(vmem_limit_bytes=52 * 1024 * 1024),
        name="mixer_forward",
    )(place, pre, decay_grid, cols, rows, taps, head_gain)


def mixer_backward(place, d_gated, pre, decay_grid, cols, taps, head_gain, kept):
    tokens, blocks = pre.shape[0], decay_grid.shape[0]
    shape = jax.ShapeDtypeStruct
    return pl.pallas_call(
        backward_kernel,
        out_shape=(
            shape((tokens, PACK), BF16),
            shape((CONV, 8, MIXED), F32),
            shape((8, DV), F32),
        ),
        in_specs=[SMEM_SPEC] + [VMEM_SPEC] * 13,
        out_specs=[VMEM_SPEC] * 3,
        scratch_shapes=[
            pltpu.VMEM((tokens, DV), BF16),
            pltpu.VMEM((blocks, KEY_SIZE, DV), F32),
            pltpu.VMEM((blocks, KEY_SIZE, DV), BF16),
            pltpu.VMEM((tokens + 8, MIXED), F32),
        ],
        compiler_params=pltpu.CompilerParams(vmem_limit_bytes=52 * 1024 * 1024),
        name="mixer_backward",
    )(place, d_gated, pre, decay_grid, cols, taps, head_gain, *kept)


def stream_tables(rate, starts):
    blocks = rate.shape[0] // BLOCK
    level = jnp.cumsum(jnp.log(rate).reshape(blocks, BLOCK), axis=-1)
    segment = jnp.cumsum(starts.reshape(blocks, BLOCK), axis=-1)
    positions = jnp.arange(BLOCK)
    causal = positions[:, None] >= positions[None, :]
    linked = (segment[:, :, None] == segment[:, None, :]) & causal
    spread = jnp.where(causal, level[:, :, None] - level[:, None, :], 0.0)
    decay_grid = jnp.where(linked, jnp.exp(spread), 0.0)
    carry = jnp.where(segment == 0, jnp.exp(level), 0.0)
    tail = decay_grid[:, BLOCK - 1, :]
    keep = 1.0 - starts
    padded = jnp.concatenate([jnp.zeros((2,), F32), keep])
    keep_two = keep * padded[1:-1]
    keep_three = keep_two * padded[:-2]
    zero = jnp.zeros_like(keep)
    cols = jnp.stack([carry.reshape(-1), tail.reshape(-1), keep, keep_two, keep_three, zero, zero, zero], axis=1)
    cols = jnp.concatenate([cols, jnp.zeros((8, 8), F32)], axis=0)
    rows = jnp.broadcast_to(carry[:, None, :], (blocks, 8, BLOCK))
    return decay_grid, cols, rows


CHIPS = 16
CORES = 2
MIXER_HEADS = 16
BOTH = ("seq", "head")


def along_x(index):
    return index ^ 1


def along_y(index):
    return index ^ 2


def along_z(steps):
    return lambda index: (index + 4 * steps) % CHIPS


def send(value, target):
    return lax.ppermute(value, "seq", [(index, target(index)) for index in range(CHIPS)])


def swap_cores(value):
    return lax.ppermute(value, "head", [(0, 1), (1, 0)])


def stacked(values):
    return jnp.concatenate(values, axis=0)


def total_of(*values):
    total = values[0].astype(F32)
    for value in values[1:]:
        total = total + value.astype(F32)
    return total


def plane_gather(block):
    half = block.shape[0] // 2
    from_x, from_y = send(block, along_x), send(block, along_y)
    far_low, far_high = send(from_y[:half], along_x), send(from_x[half:], along_y)
    return [block, from_x, from_y, stacked([far_low, far_high])]


def gather_rows(block):
    levels = [block] + [send(block, along_z(steps)) for steps in (1, 2, 3)]
    planes = [plane_gather(level) for level in levels]
    return stacked([planes[j][p] for p in range(4) for j in range(4)])


def plane_scatter(own, for_x, for_y, far):
    half = own.shape[0] // 2
    low, high = send(far[:half], along_x), send(far[half:], along_y)
    for_y = stacked([total_of(for_y[:half], low).astype(BF16), for_y[half:]])
    for_x = stacked([for_x[:half], total_of(for_x[half:], high).astype(BF16)])
    return total_of(own, send(for_x, along_x), send(for_y, along_y))


def scatter_rows(parts):
    rows = parts.shape[0] // CHIPS
    pieces = [[parts[(4 * p + j) * rows : (4 * p + j + 1) * rows] for p in range(4)] for j in range(4)]
    arrived = []
    for j in (1, 2, 3):
        arrived.append(send(plane_scatter(*pieces[j]).astype(BF16), along_z(-j)))
    return total_of(plane_scatter(*pieces[0]), *arrived)


def head_routes(step):
    return [
        (
            chip * CORES + core,
            ((CHIPS // CORES) * core + (chip + step) % (CHIPS // CORES)) * CORES + chip // (CHIPS // CORES),
        )
        for chip in range(CHIPS)
        for core in range(CORES)
    ]


def to_heads(pieces):
    steps = CHIPS // CORES
    chip = lax.axis_index("seq")
    moved = [
        lax.ppermute(
            lax.dynamic_index_in_dim(pieces, (chip + step) % steps, 0, False), BOTH, head_routes(step)
        )
        for step in range(steps)
    ]
    order = jnp.stack(moved)
    return jnp.take(order, (chip % steps - jnp.arange(steps)) % steps, axis=0)


def from_heads(pieces):
    steps = CHIPS // CORES
    chip = lax.axis_index("seq")
    moved = []
    for step in range(steps):
        back = [(target, source) for source, target in head_routes(step)]
        moved.append(
            lax.ppermute(
                lax.dynamic_index_in_dim(pieces, (chip - step) % steps, 0, False), BOTH, back
            )
        )
    order = jnp.stack(moved)
    return jnp.take(order, (jnp.arange(steps) - chip) % steps, axis=0)


def nn(a, b):
    return mm(a, b)


def nt(a, b):
    return mm(a, b, NT)


def tn(a, b):
    return mm(a, b, TN)


def head_plan(
    inputs,
    doc_starts,
    decay_rate,
    mixer_gain,
    w_query,
    w_key,
    w_value,
    w_beta,
    w_gating,
    conv_query,
    conv_key,
    conv_value,
    head_gain,
    w_output,
    feed_gain,
    w_gate,
    w_up,
    w_down,
    cotangent,
):
    chip, core = lax.axis_index("seq"), lax.axis_index("head")
    first = core == 0
    tok_rows, width = inputs.shape
    half_rows, half_width = tok_rows // CORES, width // CORES
    row_count = w_query.shape[0]
    head_count = w_query.shape[1] // KEY_SIZE
    units = w_gate.shape[1] // CHIPS

    def own_rows(values):
        return lax.dynamic_slice_in_dim(values, core * half_rows, half_rows, 0)

    def turned(values):
        return jnp.where(
            first,
            values,
            jnp.concatenate([values[:, half_width:], values[:, :half_width]], axis=1),
        )

    def both_rows(own):
        other = swap_cores(own)
        return stacked([jnp.where(first, own, other), jnp.where(first, other, own)])

    gain_one = mixer_gain.astype(F32)[:, None]
    gain_two = feed_gain.astype(F32)[:, None]

    def by_head(weights, size):
        return weights.reshape(row_count, head_count, size).transpose(1, 0, 2)

    beta_pair = jnp.broadcast_to(w_beta.T[:, :, None], (head_count, row_count, 2))
    packed_in = jnp.concatenate(
        [
            by_head(w_query, KEY_SIZE),
            by_head(w_key, KEY_SIZE),
            by_head(w_value, DV),
            by_head(w_gating, DV),
            beta_pair,
            jnp.zeros((head_count, row_count, PACK - LOGIT - 2), BF16),
        ],
        axis=2,
    )
    packed_in = (packed_in.astype(F32) * gain_one).astype(BF16)
    out_pieces = w_output.reshape(head_count, DV, row_count).transpose(0, 2, 1)

    inputs_own = own_rows(inputs).astype(F32)
    scale_one = lax.rsqrt(jnp.mean(inputs_own * inputs_own, axis=-1, keepdims=True) + EPSILON)
    normed_own = (inputs_own * scale_one).astype(BF16)
    normed_all = gather_rows(turned(normed_own))
    mine_in = to_heads(packed_in).reshape(half_width, PACK)
    weights_in = stacked([mine_in, swap_cores(mine_in)])

    notes = stacked(
        [decay_rate.T, doc_starts.astype(F32)[None], jnp.zeros((7, tok_rows), F32)]
    )
    notes = lax.all_gather(notes, BOTH, axis=0).reshape(CHIPS, CORES, 16, tok_rows)
    rate = lax.dynamic_index_in_dim(
        lax.dynamic_index_in_dim(notes, chip // head_count, 1, False), chip % head_count, 1, False
    ).reshape(-1)
    starts = notes[:, 0, 8].reshape(-1)
    decay_grid, cols, rows = stream_tables(rate, starts)
    taps_here = jnp.concatenate(
        [
            conv_query.reshape(CONV, head_count, KEY_SIZE),
            conv_key.reshape(CONV, head_count, KEY_SIZE),
            conv_value.reshape(CONV, head_count, DV),
        ],
        axis=2,
    ).transpose(1, 0, 2)
    taps_there = swap_cores(taps_here)
    taps = lax.dynamic_index_in_dim(
        jnp.where(chip // head_count == core, taps_here, taps_there), chip % head_count, 0, False
    ).astype(F32)
    taps = stacked([taps, jnp.zeros_like(taps)])
    gain_head = jnp.broadcast_to(head_gain.astype(F32)[None], (8, DV))

    blocks = jnp.arange(CHIPS * CORES)
    far = blocks // CORES
    place = (
        4 * ((far ^ chip) % 4) + (chip // 4 - far // 4) % 4 + CHIPS * (blocks % CORES != core)
    ).astype(jnp.int32)

    feed = jnp.concatenate(
        [
            (w_gate.astype(F32) * gain_two).astype(BF16).T.reshape(CHIPS, units, row_count),
            (w_up.astype(F32) * gain_two).astype(BF16).T.reshape(CHIPS, units, row_count),
            w_down.reshape(CHIPS, units, row_count),
        ],
        axis=1,
    )

    raw = nn(normed_all, weights_in)
    column = lax.broadcasted_iota(jnp.int32, raw.shape, 1)
    pre_own = jnp.where(
        column == LOGIT + 1,
        raw - lax.reduce_precision(raw, exponent_bits=8, mantissa_bits=7),
        raw,
    ).astype(BF16)
    pre = stacked([pre_own, swap_cores(pre_own)])
    mine_out = to_heads(out_pieces).reshape(half_width, DV)
    weights_out = stacked([mine_out, swap_cores(mine_out)])
    feed_mine = lax.all_to_all(feed, "seq", split_axis=0, concat_axis=0, tiled=True)
    feed_other = swap_cores(feed_mine)

    def unit_rows(position):
        return stacked(
            [
                part[:, position * units : (position + 1) * units].transpose(1, 0, 2).reshape(units, width)
                for part in (feed_mine, feed_other)
            ]
        )

    gate_rows, up_rows, down_rows = unit_rows(0), unit_rows(1), unit_rows(2)
    cot_own = own_rows(cotangent)
    cot_all = lax.all_gather(cot_own, "seq", axis=0, tiled=False)
    relative = jnp.arange(CHIPS)
    order = 4 * ((chip // 4 - relative % 4) % 4) + ((chip % 4) ^ (relative // 4))
    cot_all = jnp.take(cot_all, order, axis=0).reshape(CHIPS * half_rows, width)
    gated, *kept = mixer_forward(place, pre, decay_grid, cols, rows, taps, gain_head)
    own_count = CHIPS * half_rows
    mixed_sum = scatter_rows(nt(gated[:own_count], weights_out).astype(BF16))
    middle = inputs_own + turned(mixed_sum)
    scale_two = lax.rsqrt(jnp.mean(middle * middle, axis=-1, keepdims=True) + EPSILON)
    normed_mid = middle * scale_two
    mid_all = gather_rows(normed_mid.astype(BF16))

    gate_lin = nt(mid_all, gate_rows)
    up_lin = nt(mid_all, up_rows)
    d_hidden = nt(cot_all, down_rows).astype(BF16).astype(F32)
    sig = jax.nn.sigmoid(gate_lin)
    act = gate_lin * sig
    hidden = (act * up_lin).astype(BF16)
    d_gate = (d_hidden * up_lin * (sig * (1.0 + gate_lin * (1.0 - sig)))).astype(BF16)
    d_up = (d_hidden * act).astype(BF16)
    e_two = scatter_rows((nn(d_gate, gate_rows) + nn(d_up, up_rows)).astype(BF16))
    d_middle = cot_own.astype(F32) + scale_two * (
        e_two - normed_mid * jnp.mean(e_two * normed_mid, axis=-1, keepdims=True)
    )
    d_mid_all = gather_rows(turned(d_middle.astype(BF16)))

    d_gated_own = nn(d_mid_all, weights_out).astype(BF16)
    d_gated = stacked([d_gated_own, swap_cores(d_gated_own)])
    d_pre, grad_taps, grad_gain = mixer_backward(
        place, d_gated, pre, decay_grid, cols, taps, gain_head, kept
    )

    feed_out = scatter_rows(nn(hidden, down_rows).astype(BF16))
    block_out = both_rows((middle + feed_out).astype(BF16))
    parts = [tn(d_gate, mid_all), tn(d_up, mid_all), tn(hidden, cot_all)]
    keep_part = jnp.concatenate([part[:units] for part in parts], axis=0)
    give_part = jnp.concatenate([part[units:] for part in parts], axis=0).astype(BF16)
    feed_grad = (keep_part + swap_cores(give_part).astype(F32)).astype(BF16)
    feed_grad = feed_grad.reshape(3 * units, CHIPS, row_count).transpose(1, 0, 2)
    feed_back = lax.all_to_all(feed_grad, "seq", split_axis=0, concat_axis=0, tiled=True).astype(F32)
    raw_gate = feed_back[:, :units].reshape(CHIPS * units, row_count).T
    raw_up = feed_back[:, units : 2 * units].reshape(CHIPS * units, row_count).T
    grad_down = feed_back[:, 2 * units :].reshape(CHIPS * units, row_count)
    grad_gate, grad_up = raw_gate * gain_two, raw_up * gain_two
    feed_gain_part = jnp.sum(
        raw_gate * w_gate.astype(F32) + raw_up * w_up.astype(F32), axis=1
    )

    e_one = scatter_rows(nt(d_pre[:own_count], weights_in).astype(BF16))
    e_one = turned(e_one)
    normed_one = inputs_own * scale_one
    grad_own = d_middle + scale_one * (
        e_one - normed_one * jnp.mean(e_one * normed_one, axis=-1, keepdims=True)
    )
    grad_inputs = both_rows(grad_own)
    normed_other = swap_cores(normed_all[:, half_width:])
    grad_in = tn(normed_all[:, :half_width], d_pre[:own_count]) + tn(normed_other, d_pre[own_count:])
    grad_in = from_heads(grad_in.astype(BF16).reshape(CHIPS // CORES, row_count, PACK))
    d_mid_other = swap_cores(d_mid_all[:, half_width:])
    grad_out = tn(d_mid_all[:, :half_width], gated[:own_count]) + tn(d_mid_other, gated[own_count:])
    grad_out = from_heads(grad_out.astype(BF16).reshape(CHIPS // CORES, row_count, DV))
    grad_output = grad_out.astype(F32).transpose(0, 2, 1).reshape(head_count * DV, row_count)

    def by_rows(start, size):
        part = grad_in[:, :, start : start + size].astype(F32)
        return part.transpose(1, 0, 2).reshape(row_count, head_count * size)

    raw_query = by_rows(0, KEY_SIZE)
    raw_key = by_rows(KEY_SIZE, KEY_SIZE)
    raw_value = by_rows(2 * KEY_SIZE, DV)
    raw_gating = by_rows(MIXED, DV)
    raw_beta = by_rows(LOGIT, 1)
    mixer_gain_part = (
        jnp.sum(raw_query * w_query.astype(F32), axis=1)
        + jnp.sum(raw_key * w_key.astype(F32), axis=1)
        + jnp.sum(raw_value * w_value.astype(F32), axis=1)
        + jnp.sum(raw_gating * w_gating.astype(F32), axis=1)
        + jnp.sum(raw_beta * w_beta.astype(F32), axis=1)
    )
    gain_parts = jnp.stack([mixer_gain_part, feed_gain_part])
    gain_totals = gain_parts + swap_cores(gain_parts)

    small = jnp.concatenate([jnp.sum(grad_taps, axis=1).reshape(-1), jnp.sum(grad_gain, axis=0)])
    small = lax.all_gather(small.reshape(-1, 128), "seq", axis=0).reshape(CHIPS, -1)
    taps_all = lax.dynamic_slice_in_dim(small[:, : CONV * MIXED], core * head_count, head_count, 0)
    taps_all = taps_all.reshape(head_count, CONV, MIXED).transpose(1, 0, 2)
    return (
        block_out,
        grad_inputs,
        gain_totals[0],
        raw_query * gain_one,
        raw_key * gain_one,
        raw_value * gain_one,
        raw_beta * gain_one,
        raw_gating * gain_one,
        taps_all[:, :, :KEY_SIZE].reshape(CONV, head_count * KEY_SIZE),
        taps_all[:, :, KEY_SIZE : 2 * KEY_SIZE].reshape(CONV, head_count * KEY_SIZE),
        taps_all[:, :, 2 * KEY_SIZE :].reshape(CONV, head_count * DV),
        jnp.sum(small[:, CONV * MIXED :], axis=0),
        grad_output,
        gain_totals[1],
        grad_gate,
        grad_up,
        grad_down,
    )


EXACT_PRECISION = lax.Precision.HIGHEST


def passed_along(value, axis, steps):
    count = lax.axis_size(axis)
    first, last = (max(0, -steps), min(count, count - steps))
    return lax.ppermute(value, axis, [(source, source + steps) for source in range(first, last)])


def entering(value, axis, join, neutral):
    count, mine = (lax.axis_size(axis), lax.axis_index(axis))
    pieces = jax.tree.map(lambda part: lax.all_gather(part, axis), value)
    subtotal = jax.tree.map(
        lambda part, zero: jnp.full_like(part, 0) + jnp.asarray(zero, part.dtype), value, neutral
    )

    def lap(position, subtotal):
        longer = join(subtotal, jax.tree.map(lambda part: part[position], pieces))
        return jax.tree.map(lambda new, old: jnp.where(position < mine, new, old), longer, subtotal)

    return lax.fori_loop(0, count - 1, lap, subtotal)


def carried_in(shard, axis, join, neutral):
    count = lax.axis_size(axis)
    place = lax.axis_index(axis)
    ahead = count - 1 - place
    gathered = jax.tree.map(
        lambda a, kind: lax.all_gather(a.astype(kind), axis),
        shard,
        jax.tree.map(lambda a: jnp.bfloat16 if a.dtype == jnp.float32 else a.dtype, shard),
    )
    state = jax.tree.map(lambda a, e: jnp.zeros_like(a) + jnp.asarray(e, a.dtype), shard, neutral)

    def one(lap, state):
        source = count - 1 - lap
        return join(
            state,
            jax.tree.map(
                lambda a, own: lax.dynamic_index_in_dim(a, source, 0, False).astype(own.dtype),
                gathered,
                shard,
            ),
        )

    return lax.fori_loop(0, ahead, one, state)


def high_einsum(einsum_form, *arrays):
    return jnp.einsum(
        einsum_form, *arrays, precision=EXACT_PRECISION, preferred_element_type=jnp.float32
    )


def low_dot(left_side, right_side):
    return jnp.dot(left_side, right_side, preferred_element_type=jnp.float32)


def inner_dot(left_side, right_side):
    return lax.dot_general(
        left_side, right_side, (((0,), (0,)), ((), ())), preferred_element_type=jnp.float32
    )


def outer_dot(left_side, right_side):
    return lax.dot_general(
        left_side, right_side, (((1,), (1,)), ((), ())), preferred_element_type=jnp.float32
    )


def rounded(values):
    return lax.optimization_barrier(values.astype(jnp.bfloat16)).astype(jnp.float32)


def scale_norm(values, gain_vec):
    return (
        values * lax.rsqrt(jnp.mean(values * values, axis=-1, keepdims=True) + EPSILON) * gain_vec
    )


def unit_rows(values):
    return values * lax.rsqrt(jnp.sum(values * values, axis=-1, keepdims=True) + EPSILON)


def swiglu(gate_lin, up_lin):
    return jax.nn.silu(gate_lin) * up_lin


def compose_maps(earlier_map, later_map):
    return (
        high_einsum("hde,hef->hdf", later_map[0], earlier_map[0]),
        high_einsum("hde,hef->hdf", later_map[0], earlier_map[1]) + later_map[1],
    )


def gather_plan(
    inputs,
    doc_starts,
    decay_rate,
    mixer_gain,
    w_query,
    w_key,
    w_value,
    w_beta,
    w_gating,
    conv_query,
    conv_key,
    conv_value,
    head_gain,
    w_output,
    feed_gain,
    w_gate,
    w_up,
    w_down,
    cotangent,
):
    tok_rows = inputs.shape[0]
    head_count = decay_rate.shape[1]
    key_width = w_query.shape[1]
    value_width = w_value.shape[1]
    edge_count = CONV - 1
    block_count = tok_rows // BLOCK
    gathered = (
        lax.all_gather(mixer_gain, "seq", axis=0, tiled=True),
        lax.all_gather(w_query, "seq", axis=0, tiled=True),
        lax.all_gather(w_key, "seq", axis=0, tiled=True),
        lax.all_gather(w_value, "seq", axis=0, tiled=True),
        lax.all_gather(w_beta, "seq", axis=0, tiled=True),
        lax.all_gather(w_gating, "seq", axis=0, tiled=True),
        lax.all_gather(w_output, "seq", axis=1, tiled=True),
        lax.all_gather(feed_gain, "seq", axis=0, tiled=True),
        lax.all_gather(w_gate, "seq", axis=0, tiled=True),
        lax.all_gather(w_up, "seq", axis=0, tiled=True),
        lax.all_gather(w_down, "seq", axis=1, tiled=True),
    )
    (
        gain_one,
        full_query,
        full_key,
        full_value,
        full_beta,
        full_gating,
        full_output,
        gain_two,
        full_gate,
        full_up,
        full_down,
    ) = gathered
    inputs_float = inputs.astype(jnp.float32)
    normed_float, norm_one_back = jax.vjp(scale_norm, inputs_float, gain_one.astype(jnp.float32))
    normed_one = normed_float.astype(jnp.bfloat16)
    query_pre = low_dot(normed_one, full_query).astype(jnp.bfloat16)
    key_pre = low_dot(normed_one, full_key).astype(jnp.bfloat16)
    value_pre = low_dot(normed_one, full_value).astype(jnp.bfloat16)
    gating_pre = low_dot(normed_one, full_gating).astype(jnp.bfloat16)
    beta_logit = low_dot(normed_one, full_beta)
    joined = jnp.concatenate([query_pre, key_pre, value_pre], axis=1)
    tail_starts = doc_starts[tok_rows - edge_count :]
    later_starts = jnp.cumsum(tail_starts[::-1])[::-1] - tail_starts
    sender_keep = (later_starts == 0).astype(jnp.bfloat16)[:, None]
    edge_in = passed_along(joined[tok_rows - edge_count :] * sender_keep, "seq", 1)
    local_doc = jnp.cumsum(doc_starts)
    padded_doc = jnp.concatenate([jnp.zeros((edge_count,), local_doc.dtype), local_doc])
    keep_masks = [
        (
            padded_doc[edge_count - shift_lag : edge_count - shift_lag + tok_rows] == local_doc
        ).astype(jnp.float32)[:, None]
        for shift_lag in range(CONV)
    ]

    def conv_piece(extended, conv_weights):
        mixed = keep_masks[0] * conv_weights[0] * extended[edge_count:]
        for shift_lag in range(1, CONV):
            mixed = (
                mixed
                + keep_masks[shift_lag]
                * conv_weights[shift_lag]
                * extended[edge_count - shift_lag : edge_count - shift_lag + tok_rows]
            )
        activated = jax.nn.silu(mixed)
        query_unit = unit_rows(activated[:, :key_width].reshape(tok_rows, head_count, KEY_SIZE))
        key_unit = unit_rows(
            activated[:, key_width : 2 * key_width].reshape(tok_rows, head_count, KEY_SIZE)
        )
        value_act = activated[:, 2 * key_width :].reshape(tok_rows, head_count, DV)
        return (query_unit, key_unit, value_act)

    extended = jnp.concatenate([edge_in, joined], axis=0).astype(jnp.float32)
    conv_weights = jnp.concatenate([conv_query, conv_key, conv_value], axis=1).astype(jnp.float32)
    (query_unit, key_unit, value_act), conv_back = jax.vjp(conv_piece, extended, conv_weights)

    def to_blocks(values):
        return values.reshape(block_count, BLOCK, head_count, values.shape[-1]).transpose(
            0, 2, 1, 3
        )

    def from_blocks(values):
        return values.transpose(0, 2, 1, 3).reshape(tok_rows, head_count, values.shape[-1])

    log_rate = jnp.log(decay_rate).reshape(block_count, BLOCK, head_count).transpose(0, 2, 1)
    log_level = jnp.cumsum(log_rate, axis=-1)
    segment = jnp.cumsum(doc_starts.reshape(block_count, BLOCK), axis=-1)
    positions = jnp.arange(BLOCK)
    causal = positions[:, None] >= positions[None, :]
    strict = positions[:, None] > positions[None, :]
    linked = (segment[:, None, :, None] == segment[:, None, None, :]) & causal
    spread = jnp.where(causal, log_level[..., :, None] - log_level[..., None, :], 0.0)
    decay_grid = jnp.where(linked, jnp.exp(spread), 0.0)
    carry_in = jnp.where(segment[:, None, :] == 0, jnp.exp(log_level), 0.0)
    tail_decay = decay_grid[..., BLOCK - 1, :]
    key_eye = jnp.eye(KEY_SIZE, dtype=jnp.float32)
    block_eye = jnp.eye(BLOCK, dtype=jnp.float32)

    def block_terms(query_blocks, key_blocks, value_blocks, logit_blocks):
        beta_gate = jax.nn.sigmoid(logit_blocks)
        key_gram = high_einsum("nhcd,nhmd->nhcm", key_blocks, key_blocks)
        system = block_eye + jnp.where(strict, decay_grid * key_gram * beta_gate[..., None, :], 0.0)
        right_side = jnp.concatenate([value_blocks, carry_in[..., None] * key_blocks], axis=-1)
        solved = jax.scipy.linalg.solve_triangular(
            system, right_side, lower=True, unit_diagonal=True
        )
        fresh_values = solved[..., :DV]
        fresh_keys = solved[..., DV:]
        mixing = (
            high_einsum("nhcd,nhmd->nhcm", query_blocks, key_blocks)
            * decay_grid
            * beta_gate[..., None, :]
        )
        weighted = key_blocks * (tail_decay * beta_gate)[..., None]
        block_maps = carry_in[..., BLOCK - 1, None, None] * key_eye - high_einsum(
            "nhcd,nhce->nhde", weighted, fresh_keys
        )
        block_adds = high_einsum("nhcd,nhce->nhde", weighted, fresh_values)

        def chain_step(current, element):
            return (compose_maps(current, element), None)

        start_map = (
            jnp.broadcast_to(key_eye, (head_count, KEY_SIZE, KEY_SIZE)),
            jnp.zeros((head_count, KEY_SIZE, DV), jnp.float32),
        )
        device_pair, _ = lax.scan(chain_step, start_map, (block_maps, block_adds))
        return (
            (fresh_values, fresh_keys, mixing, block_maps, block_adds),
            device_pair[0],
            device_pair[1],
        )

    def block_outputs(block_parts, query_blocks, start_state):

        def step_block(current, element):
            fresh_values, fresh_keys, mixing, block_map, block_add, query_part, carry_part = element
            updated = fresh_values - high_einsum("hcd,hde->hce", fresh_keys, current)
            produced_output = (
                carry_part[..., None] * high_einsum("hcd,hde->hce", query_part, current)
                + high_einsum("hcm,hme->hce", mixing, updated)
            ) * KEY_SIZE ** (-0.5)
            return (high_einsum("hde,hef->hdf", block_map, current) + block_add, produced_output)

        _, emitted_all = lax.scan(step_block, start_state, block_parts + (query_blocks, carry_in))
        return emitted_all

    query_blocks = to_blocks(rounded(query_unit))
    key_blocks = to_blocks(rounded(key_unit))
    value_blocks = to_blocks(rounded(value_act))
    logit_blocks = beta_logit.reshape(block_count, BLOCK, head_count).transpose(0, 2, 1)
    (block_parts, device_map, device_add), terms_back = jax.vjp(
        block_terms, query_blocks, key_blocks, value_blocks, logit_blocks
    )
    identity = (jnp.broadcast_to(key_eye, device_map.shape), jnp.zeros_like(device_add))
    prefix = entering((device_map, device_add), "seq", compose_maps, identity)
    start_state = prefix[1]
    produced_output, emitted_back = jax.vjp(block_outputs, block_parts, query_blocks, start_state)

    def gated_norm(values, gating_values, gain_vec):
        normed_out = values * lax.rsqrt(jnp.mean(values * values, axis=-1, keepdims=True) + EPSILON)
        return (normed_out * gain_vec * jax.nn.silu(gating_values)).reshape(tok_rows, value_width)

    mixer_out = from_blocks(produced_output)
    gated_float, gated_back = jax.vjp(
        gated_norm,
        mixer_out,
        gating_pre.astype(jnp.float32).reshape(tok_rows, head_count, DV),
        head_gain.astype(jnp.float32),
    )
    gated_out = gated_float.astype(jnp.bfloat16)
    middle = inputs_float + lax.psum(
        low_dot(gated_out, full_output).astype(jnp.bfloat16), "head"
    ).astype(jnp.float32)
    normed_middle, norm_two_back = jax.vjp(scale_norm, middle, gain_two.astype(jnp.float32))
    normed_two = normed_middle.astype(jnp.bfloat16)
    gate_lin = low_dot(normed_two, full_gate)
    up_lin = low_dot(normed_two, full_up)
    hidden_float, swiglu_back = jax.vjp(swiglu, gate_lin, up_lin)
    hidden = hidden_float.astype(jnp.bfloat16)
    feed_out = lax.psum(low_dot(hidden, full_down).astype(jnp.bfloat16), "head").astype(jnp.float32)
    block_out = (middle + feed_out).astype(jnp.bfloat16)
    regathered = (
        lax.all_gather(w_query, "seq", axis=0, tiled=True),
        lax.all_gather(w_key, "seq", axis=0, tiled=True),
        lax.all_gather(w_value, "seq", axis=0, tiled=True),
        lax.all_gather(w_beta, "seq", axis=0, tiled=True),
        lax.all_gather(w_gating, "seq", axis=0, tiled=True),
        lax.all_gather(w_output, "seq", axis=1, tiled=True),
        lax.all_gather(w_gate, "seq", axis=0, tiled=True),
        lax.all_gather(w_up, "seq", axis=0, tiled=True),
        lax.all_gather(w_down, "seq", axis=1, tiled=True),
    )
    (
        full_query,
        full_key,
        full_value,
        full_beta,
        full_gating,
        full_output,
        full_gate,
        full_up,
        full_down,
    ) = regathered
    cotangent_float = cotangent.astype(jnp.float32)
    grad_down = inner_dot(hidden, cotangent)
    d_hidden = rounded(outer_dot(cotangent, full_down))
    d_gate_float, d_up_float = swiglu_back(d_hidden)
    d_gate = d_gate_float.astype(jnp.bfloat16)
    d_up = d_up_float.astype(jnp.bfloat16)
    grad_gate = inner_dot(normed_two, d_gate)
    grad_up = inner_dot(normed_two, d_up)
    d_normed_two = lax.psum(
        (outer_dot(d_gate, full_gate) + outer_dot(d_up, full_up)).astype(jnp.bfloat16), "head"
    ).astype(jnp.float32)
    d_middle_norm, grad_gain_two = norm_two_back(d_normed_two)
    d_middle = cotangent_float + d_middle_norm
    d_middle_low = d_middle.astype(jnp.bfloat16)
    grad_output = inner_dot(gated_out, d_middle_low)
    d_gated = rounded(outer_dot(d_middle_low, full_output))
    d_mixer_out, d_gating_float, grad_head_part = gated_back(d_gated)
    d_gating = d_gating_float.reshape(tok_rows, value_width).astype(jnp.bfloat16)
    d_parts, d_query_late, d_start = emitted_back(to_blocks(d_mixer_out))
    chained = carried_in((jnp.swapaxes(device_map, 1, 2), d_start), "seq", compose_maps, identity)
    d_end = chained[1]
    d_map = high_einsum("hde,hfe->hdf", d_end, start_state)
    d_query_early, d_key_blocks, d_value_blocks, d_logit_blocks = terms_back(
        (d_parts, d_map, d_end)
    )
    d_query_unit = rounded(from_blocks(d_query_early + d_query_late))
    d_key_unit = rounded(from_blocks(d_key_blocks))
    d_value_act = rounded(from_blocks(d_value_blocks))
    d_beta_logit = (
        d_logit_blocks.transpose(0, 2, 1).reshape(tok_rows, head_count).astype(jnp.bfloat16)
    )
    d_extended, grad_conv_all = conv_back((d_query_unit, d_key_unit, d_value_act))
    returned = passed_along(d_extended[:edge_count].astype(jnp.bfloat16), "seq", -1).astype(
        jnp.float32
    )
    d_rows = d_extended[edge_count:]
    d_rows = jnp.concatenate(
        [
            d_rows[: tok_rows - edge_count],
            d_rows[tok_rows - edge_count :] + returned * sender_keep.astype(jnp.float32),
        ],
        axis=0,
    )
    d_joined = d_rows.astype(jnp.bfloat16)
    d_query_pre = d_joined[:, :key_width]
    d_key_pre = d_joined[:, key_width : 2 * key_width]
    d_value_pre = d_joined[:, 2 * key_width :]
    grad_query = inner_dot(normed_one, d_query_pre)
    grad_key = inner_dot(normed_one, d_key_pre)
    grad_value = inner_dot(normed_one, d_value_pre)
    grad_gating = inner_dot(normed_one, d_gating)
    grad_beta = inner_dot(normed_one, d_beta_logit)
    d_normed_part = (
        outer_dot(d_query_pre, full_query)
        + outer_dot(d_key_pre, full_key)
        + outer_dot(d_value_pre, full_value)
        + outer_dot(d_gating, full_gating)
        + outer_dot(d_beta_logit, full_beta)
    )
    d_normed_one, head_total = (
        lax.psum(d_normed_part.astype(jnp.bfloat16), "head").astype(jnp.float32),
        lax.psum(grad_head_part.astype(jnp.bfloat16), "head").astype(jnp.float32),
    )
    d_inputs_norm, grad_gain_one = norm_one_back(d_normed_one)
    grad_inputs = d_middle + d_inputs_norm
    small_totals = lax.psum((grad_conv_all, head_total), "seq")
    conv_total = small_totals[0]
    totals = (
        lax.psum_scatter(grad_gain_one, "seq", scatter_dimension=0, tiled=True),
        lax.psum_scatter(grad_query, "seq", scatter_dimension=0, tiled=True),
        lax.psum_scatter(grad_key, "seq", scatter_dimension=0, tiled=True),
        lax.psum_scatter(grad_value, "seq", scatter_dimension=0, tiled=True),
        lax.psum_scatter(grad_beta, "seq", scatter_dimension=0, tiled=True),
        lax.psum_scatter(grad_gating, "seq", scatter_dimension=0, tiled=True),
        lax.psum_scatter(grad_output, "seq", scatter_dimension=1, tiled=True),
        lax.psum_scatter(grad_gain_two, "seq", scatter_dimension=0, tiled=True),
        lax.psum_scatter(grad_gate, "seq", scatter_dimension=0, tiled=True),
        lax.psum_scatter(grad_up, "seq", scatter_dimension=0, tiled=True),
        lax.psum_scatter(grad_down, "seq", scatter_dimension=1, tiled=True),
    )
    return (
        block_out,
        grad_inputs,
        totals[0],
        totals[1],
        totals[2],
        totals[3],
        totals[4],
        totals[5],
        conv_total[:, :key_width],
        conv_total[:, key_width : 2 * key_width],
        conv_total[:, 2 * key_width :],
        small_totals[1],
        totals[6],
        totals[7],
        totals[8],
        totals[9],
        totals[10],
    )


def solution(mesh):
    in_specs = (
        P("seq", None),
        P("seq"),
        P("seq", "head"),
        P("seq"),
        P("seq", "head"),
        P("seq", "head"),
        P("seq", "head"),
        P("seq", "head"),
        P("seq", "head"),
        P(None, "head"),
        P(None, "head"),
        P(None, "head"),
        P(),
        P("head", "seq"),
        P("seq"),
        P("seq", "head"),
        P("seq", "head"),
        P("head", "seq"),
        P("seq", None),
    )
    out_specs = (
        P("seq", None),
        P("seq", None),
        P("seq"),
        P("seq", "head"),
        P("seq", "head"),
        P("seq", "head"),
        P("seq", "head"),
        P("seq", "head"),
        P(None, "head"),
        P(None, "head"),
        P(None, "head"),
        P(),
        P("head", "seq"),
        P("seq"),
        P("seq", "head"),
        P("seq", "head"),
        P("head", "seq"),
    )
    whole_heads = mesh.shape["seq"] == CHIPS and mesh.shape["head"] == CORES
    per_device = head_plan if whole_heads else gather_plan
    return jax.shard_map(
        per_device, mesh=mesh, in_specs=in_specs, out_specs=out_specs, check_vma=False
    )
```

```python
import jax
import jax.numpy as jnp
from jax import lax
from jax.sharding import PartitionSpec as P
from jax.experimental import pallas as pl
from jax.experimental.pallas import tpu as pltpu

KEY_SIZE = 128
DV = 256
CONV = 4
BLOCK = 64
EPSILON = 1e-06
F32 = jnp.float32
BF16 = jnp.bfloat16
LOGIT = 2 * KEY_SIZE + 2 * DV
PACK = LOGIT + 128
MIXED = 2 * KEY_SIZE + DV
SCALE = KEY_SIZE**-0.5
UNROLL = 4


def mm(a, b, dims=((1,), (0,))):
    return lax.dot_general(a, b, (dims, ((), ())), preferred_element_type=F32)


NT = ((1,), (1,))
TN = ((0,), (0,))


def halves(a):
    high = a.astype(BF16)
    return high, (a - high.astype(F32)).astype(BF16)


def mm_left(a, b, dims=((1,), (0,))):
    high, low = halves(a)
    return mm(high, b, dims) + mm(low, b, dims)


def mm_right(a, b, dims=((1,), (0,))):
    high, low = halves(b)
    return mm(a, high, dims) + mm(a, low, dims)


def mm_both(a, b, dims=((1,), (0,))):
    a_high, a_low = halves(a)
    b_high, b_low = halves(b)
    return mm(a_high, b_high, dims) + (mm(a_high, b_low, dims) + mm(a_low, b_high, dims))


def block_masks():
    row = lax.broadcasted_iota(jnp.int32, (BLOCK, BLOCK), 0)
    col = lax.broadcasted_iota(jnp.int32, (BLOCK, BLOCK), 1)
    strict = row > col
    levels = []
    size = 1
    while size < BLOCK:
        levels.append(
            (row // (2 * size) == col // (2 * size)) & (row // size % 2 == 1) & (col // size % 2 == 0)
        )
        size *= 2
    return strict, levels, (row == col).astype(F32)


def unit_lower_inverses(systems, levels, eye):
    inverses = [eye - jnp.where(levels[0], system, 0.0) for system in systems]
    for level in levels[1:]:
        inner = [
            mm_both(jnp.where(level, system, 0.0), inverse)
            for system, inverse in zip(systems, inverses)
        ]
        inverses = [
            inverse - mm_both(inverse, part) for inverse, part in zip(inverses, inner)
        ]
    return inverses


def rows_of(index):
    return pl.ds(pl.multiple_of(index * BLOCK, BLOCK), BLOCK)


def row_sums(values):
    return jnp.sum(values.reshape(values.shape[0] // 8, 8, values.shape[1]), axis=0)


def beta_columns(packed):
    logit = packed[:, :1].astype(F32) + packed[:, 1:2].astype(F32)
    beta = jax.nn.sigmoid(logit)
    return beta, jnp.broadcast_to(beta, (BLOCK, 128)).T[:BLOCK]


def units_of(mixed):
    gate = jax.nn.sigmoid(mixed)
    act = mixed * gate
    query, key = act[:, :KEY_SIZE], act[:, KEY_SIZE : 2 * KEY_SIZE]
    query_scale = lax.rsqrt(jnp.sum(query * query, axis=-1, keepdims=True) + EPSILON)
    key_scale = lax.rsqrt(jnp.sum(key * key, axis=-1, keepdims=True) + EPSILON)
    return gate, act, query * query_scale, key * key_scale, query_scale, key_scale


def forward_kernel(
    place,
    pre_own,
    pre_other,
    decay_grid,
    cols,
    rows,
    taps,
    head_gain,
    gated_own,
    gated_other,
    mixer_out,
    mixed_out,
    inverse_out,
    state_out,
    fresh_out,
    carry_out,
    read_out,
    both_maps,
    value_part,
    out_part,
    add_part,
    pre,
    gated,
):
    blocks = decay_grid.shape[0]
    half = pre_own.shape[0]
    pre[:half] = pre_own[...]
    pre[half:] = pre_other[...]
    strict, levels, eye = block_masks()
    key_eye = (
        lax.broadcasted_iota(jnp.int32, (KEY_SIZE, KEY_SIZE), 0)
        == lax.broadcasted_iota(jnp.int32, (KEY_SIZE, KEY_SIZE), 1)
    ).astype(F32)

    def prepare(group, _):
        work = []
        for lane in range(UNROLL):
            b = group * UNROLL + lane
            here = rows_of(b)
            source = place[b]
            before = place[jnp.maximum(b - 1, 0)]
            current = pre[rows_of(source), :MIXED].astype(F32)
            edge = pre[
                pl.ds(pl.multiple_of(before * BLOCK + BLOCK - 16, 16), 16), :MIXED
            ].astype(F32)
            extended = jnp.concatenate([edge[8:], current], axis=0)
            mixed = taps[0:1] * current
            for lag in range(1, CONV):
                mixed = mixed + (taps[lag : lag + 1] * cols[here, 1 + lag : 2 + lag]) * pltpu.roll(
                    extended, lag, 0
                )[8:]
            mixed_out[here, :] = mixed
            _, act, query, key, _, _ = units_of(mixed)
            query, key, value = query.astype(BF16), key.astype(BF16), act[:, 2 * KEY_SIZE :].astype(BF16)
            beta, beta_row = beta_columns(pre[rows_of(source), LOGIT:])
            link = decay_grid[b] * beta_row
            system = jnp.where(strict, link * mm(key, key, NT), 0.0)
            mixing = (SCALE * mm(query, key, NT)) * link
            work.append((b, here, query, key, value, beta, system, mixing))
        inverses = unit_lower_inverses([item[6] for item in work], levels, eye)
        for (b, here, query, key, value, beta, system, mixing), inverse in zip(work, inverses):
            inverse_out[here, :] = inverse
            carry = cols[here, 0:1]
            tail = cols[here, 1:2] * beta
            fresh_values = mm_left(inverse, value)
            fresh_keys = mm_left(inverse * rows[b, 0:1, :], key)
            low_mixing = mixing.astype(BF16)
            read = (SCALE * carry) * query.astype(F32) - mm(low_mixing, fresh_keys.astype(BF16))
            value_part[here, :] = fresh_values
            out_part[here, :] = mm(low_mixing, fresh_values.astype(BF16))
            read_out[here, :] = read.astype(BF16)
            both_maps[b, :BLOCK] = read.astype(BF16)
            both_maps[b, BLOCK:] = fresh_keys.astype(BF16)
            carry_end = carry[BLOCK - 1 : BLOCK]
            carry_out[b] = carry_end * key_eye - mm_right(key, tail * fresh_keys, TN)
            add_part[b] = mm_right(key, tail * fresh_values, TN)
        return 0

    lax.fori_loop(0, blocks // UNROLL, prepare, 0)

    def chain(b, state):
        state_out[b] = state.astype(BF16)
        return mm_both(carry_out[b], state) + add_part[b]

    lax.fori_loop(0, blocks, chain, jnp.zeros((KEY_SIZE, DV), F32))

    def finish(group, _):
        for lane in range(UNROLL):
            b = group * UNROLL + lane
            here = rows_of(b)
            source = place[b]
            both = mm(both_maps[b], state_out[b])
            produced = both[:BLOCK] + out_part[here, :]
            fresh_out[here, :] = (value_part[here, :] - both[BLOCK:]).astype(BF16)
            mixer_out[here, :] = produced
            scale = lax.rsqrt(jnp.mean(produced * produced, axis=-1, keepdims=True) + EPSILON)
            gate = pre[rows_of(source), MIXED:LOGIT].astype(F32)
            gated[rows_of(source), :] = (
                produced * scale * head_gain[0:1] * (gate * jax.nn.sigmoid(gate))
            ).astype(BF16)
        return 0

    lax.fori_loop(0, blocks // UNROLL, finish, 0)
    gated_own[...] = gated[:half]
    gated_other[...] = gated[half:]


def backward_kernel(
    place,
    d_gated_own,
    d_gated_other,
    pre_own,
    pre_other,
    decay_grid,
    cols,
    taps,
    head_gain,
    mixer_out,
    mixed_in,
    inverse_in,
    state_in,
    fresh_in,
    carry_in,
    read_in,
    d_pre_own,
    d_pre_other,
    grad_taps,
    grad_gain,
    d_out,
    pull_part,
    end_state,
    d_mixed,
    d_gated,
    pre,
    d_pre,
):
    blocks = decay_grid.shape[0]
    half = pre_own.shape[0]
    pre[:half] = pre_own[...]
    pre[half:] = pre_other[...]
    d_gated[:half] = d_gated_own[...]
    d_gated[half:] = d_gated_other[...]
    strict, _, _ = block_masks()
    lane_index = lax.broadcasted_iota(jnp.int32, (BLOCK, PACK - LOGIT), 1)
    grad_taps[...] = jnp.zeros_like(grad_taps)
    grad_gain[...] = jnp.zeros_like(grad_gain)
    d_mixed[blocks * BLOCK :, :] = jnp.zeros((8, MIXED), F32)

    def prepare(group, _):
        for lane in range(UNROLL):
            b = group * UNROLL + lane
            here = rows_of(b)
            there = rows_of(place[b])
            grad = d_gated[there, :].astype(F32)
            gate = pre[there, MIXED:LOGIT].astype(F32)
            produced = mixer_out[here, :]
            scale = lax.rsqrt(jnp.mean(produced * produced, axis=-1, keepdims=True) + EPSILON)
            normed = produced * scale
            sig = jax.nn.sigmoid(gate)
            act = gate * sig
            weighted = grad * head_gain[0:1]
            pulled = weighted * act
            along = jnp.mean(pulled * normed, axis=-1, keepdims=True)
            low = (scale * (pulled - normed * along)).astype(BF16)
            grad_gain[...] += row_sums(grad * normed * act)
            d_pre[there, MIXED:LOGIT] = (
                weighted * normed * (sig * (1.0 + gate * (1.0 - sig)))
            ).astype(BF16)
            d_out[here, :] = low
            pull_part[b] = mm(read_in[here, :], low, TN)
        return 0

    lax.fori_loop(0, blocks // UNROLL, prepare, 0)

    def chain(step, state):
        b = blocks - 1 - step
        end_state[b] = state.astype(BF16)
        return mm_both(carry_in[b], state, TN) + pull_part[b]

    lax.fori_loop(0, blocks, chain, jnp.zeros((KEY_SIZE, DV), F32))

    def finish(group, _):
        for lane in range(UNROLL):
            b = group * UNROLL + lane
            here = rows_of(b)
            there = rows_of(place[b])
            mixed = mixed_in[here, :]
            gate, act, query_unit, key_unit, query_scale, key_scale = units_of(mixed)
            query, key = query_unit.astype(BF16), key_unit.astype(BF16)
            beta, beta_row = beta_columns(pre[there, LOGIT:])
            link = decay_grid[b] * beta_row
            mixing = (SCALE * mm(query, key, NT)) * link
            carry = cols[here, 0:1]
            tail = cols[here, 1:2] * beta
            low = d_out[here, :]
            end = end_state[b]
            start = state_in[b]
            fresh = fresh_in[here, :]
            d_fresh = mm(mixing.astype(BF16), low, TN) + tail * mm(key, end)
            d_right = mm_left(inverse_in[here, :], d_fresh.astype(BF16), TN)
            d_right_low = d_right.astype(BF16)
            d_logit = (1.0 - beta) * jnp.sum(fresh.astype(F32) * d_right, axis=-1, keepdims=True)
            pair = jnp.concatenate([low, d_right_low], axis=0)
            on_state = mm(pair, start, NT)
            on_fresh = mm(pair, fresh, NT)
            read_grad = (SCALE * on_fresh[:BLOCK]) * link
            system_grad = jnp.where(strict, -on_fresh[BLOCK:] * link, 0.0)
            d_query = (SCALE * carry) * on_state[:BLOCK] + mm(read_grad.astype(BF16), key)
            d_key = (
                mm((system_grad + system_grad.T).astype(BF16), key)
                + mm(read_grad.astype(BF16), query, TN)
                + tail * mm(fresh, end, NT)
                - carry * on_state[BLOCK:]
            )
            d_query = d_query.astype(BF16).astype(F32)
            d_key = d_key.astype(BF16).astype(F32)
            slope = gate * (1.0 + mixed * (1.0 - gate))
            d_mixed[here, :KEY_SIZE] = (
                d_query - query_unit * jnp.sum(query_unit * d_query, axis=-1, keepdims=True)
            ) * (query_scale * slope[:, :KEY_SIZE])
            d_mixed[here, KEY_SIZE : 2 * KEY_SIZE] = (
                d_key - key_unit * jnp.sum(key_unit * d_key, axis=-1, keepdims=True)
            ) * (key_scale * slope[:, KEY_SIZE : 2 * KEY_SIZE])
            d_mixed[here, 2 * KEY_SIZE :] = d_right_low.astype(F32) * slope[:, 2 * KEY_SIZE :]
            d_pre[there, LOGIT:] = jnp.where(lane_index == 0, d_logit, 0.0).astype(BF16)
        return 0

    lax.fori_loop(0, blocks // UNROLL, finish, 0)

    def unmix(group, _):
        for lane in range(UNROLL):
            b = group * UNROLL + lane
            there = rows_of(place[b])
            longer = pl.ds(pl.multiple_of(b * BLOCK, BLOCK), BLOCK + 8)
            extended = d_mixed[longer, :]
            current = pre[there, :MIXED].astype(F32)
            total = taps[0:1] * extended[:BLOCK]
            grad_taps[0] += row_sums(current * extended[:BLOCK])
            for lag in range(1, CONV):
                kept = cols[longer, 1 + lag : 2 + lag] * extended
                moved = pltpu.roll(kept, BLOCK + 8 - lag, 0)[:BLOCK]
                total = total + taps[lag : lag + 1] * moved
                grad_taps[lag] += row_sums(current * moved)
            d_pre[there, :MIXED] = total.astype(BF16)
        return 0

    lax.fori_loop(0, blocks // UNROLL, unmix, 0)
    d_pre_own[...] = d_pre[:half]
    d_pre_other[...] = d_pre[half:]


VMEM_SPEC = pl.BlockSpec(memory_space=pltpu.VMEM)
SMEM_SPEC = pl.BlockSpec(memory_space=pltpu.SMEM)
KERNEL_COST = pl.CostEstimate(flops=30_000_000_000, bytes_accessed=100_000_000, transcendentals=0)


def mixer_forward(place, pre_own, pre_other, decay_grid, cols, rows, taps, head_gain):
    blocks = decay_grid.shape[0]
    half, tokens = pre_own.shape[0], blocks * BLOCK
    shape = jax.ShapeDtypeStruct
    return pl.pallas_call(
        forward_kernel,
        out_shape=(
            shape((half, DV), BF16),
            shape((half, DV), BF16),
            shape((tokens, DV), F32),
            shape((tokens, MIXED), F32),
            shape((tokens, BLOCK), F32),
            shape((blocks, KEY_SIZE, DV), BF16),
            shape((tokens, DV), BF16),
            shape((blocks, KEY_SIZE, KEY_SIZE), F32),
            shape((tokens, KEY_SIZE), BF16),
        ),
        in_specs=[SMEM_SPEC] + [VMEM_SPEC] * 7,
        out_specs=[VMEM_SPEC] * 9,
        scratch_shapes=[
            pltpu.VMEM((blocks, 2 * BLOCK, KEY_SIZE), BF16),
            pltpu.VMEM((tokens, DV), F32),
            pltpu.VMEM((tokens, DV), F32),
            pltpu.VMEM((blocks, KEY_SIZE, DV), F32),
            pltpu.VMEM((tokens, PACK), BF16),
            pltpu.VMEM((tokens, DV), BF16),
        ],
        compiler_params=pltpu.CompilerParams(vmem_limit_bytes=52 * 1024 * 1024),
        cost_estimate=KERNEL_COST,
        name="mixer_forward",
    )(place, pre_own, pre_other, decay_grid, cols, rows, taps, head_gain)


def mixer_backward(place, d_gated, pre, decay_grid, cols, taps, head_gain, kept):
    blocks = decay_grid.shape[0]
    half, tokens = pre[0].shape[0], blocks * BLOCK
    shape = jax.ShapeDtypeStruct
    return pl.pallas_call(
        backward_kernel,
        out_shape=(
            shape((half, PACK), BF16),
            shape((half, PACK), BF16),
            shape((CONV, 8, MIXED), F32),
            shape((8, DV), F32),
        ),
        in_specs=[SMEM_SPEC] + [VMEM_SPEC] * 15,
        out_specs=[VMEM_SPEC] * 4,
        scratch_shapes=[
            pltpu.VMEM((tokens, DV), BF16),
            pltpu.VMEM((blocks, KEY_SIZE, DV), F32),
            pltpu.VMEM((blocks, KEY_SIZE, DV), BF16),
            pltpu.VMEM((tokens + 8, MIXED), F32),
            pltpu.VMEM((tokens, DV), BF16),
            pltpu.VMEM((tokens, PACK), BF16),
            pltpu.VMEM((tokens, PACK), BF16),
        ],
        compiler_params=pltpu.CompilerParams(vmem_limit_bytes=52 * 1024 * 1024),
        cost_estimate=KERNEL_COST,
        name="mixer_backward",
    )(place, *d_gated, *pre, decay_grid, cols, taps, head_gain, *kept)


def stream_tables(rate, starts):
    blocks = rate.shape[0] // BLOCK
    level = jnp.cumsum(jnp.log(rate).reshape(blocks, BLOCK), axis=-1)
    segment = jnp.cumsum(starts.reshape(blocks, BLOCK), axis=-1)
    positions = jnp.arange(BLOCK)
    causal = positions[:, None] >= positions[None, :]
    linked = (segment[:, :, None] == segment[:, None, :]) & causal
    spread = jnp.where(causal, level[:, :, None] - level[:, None, :], 0.0)
    decay_grid = jnp.where(linked, jnp.exp(spread), 0.0)
    carry = jnp.where(segment == 0, jnp.exp(level), 0.0)
    tail = decay_grid[:, BLOCK - 1, :]
    keep = 1.0 - starts
    padded = jnp.concatenate([jnp.zeros((2,), F32), keep])
    keep_two = keep * padded[1:-1]
    keep_three = keep_two * padded[:-2]
    zero = jnp.zeros_like(keep)
    cols = jnp.stack([carry.reshape(-1), tail.reshape(-1), keep, keep_two, keep_three, zero, zero, zero], axis=1)
    cols = jnp.concatenate([cols, jnp.zeros((8, 8), F32)], axis=0)
    rows = jnp.broadcast_to(carry[:, None, :], (blocks, 8, BLOCK))
    return decay_grid, cols, rows


def unpack_kernel(
    grads, gain, w_query, w_key, w_value, w_gating, w_beta, query, key, value, gating, beta, gain_part
):
    heads = grads.shape[0]
    scale = gain[...]
    total = jnp.zeros((grads.shape[1], 128), F32)

    def lane_sums(values):
        part = values[:, :128]
        for start in range(128, values.shape[1], 128):
            part = part + values[:, start : start + 128]
        return part

    columns = []
    for head in range(heads):
        start = 0
        for out, weights, size in (
            (query, w_query, KEY_SIZE),
            (key, w_key, KEY_SIZE),
            (value, w_value, DV),
            (gating, w_gating, DV),
        ):
            place = slice(head * size, (head + 1) * size)
            part = grads[head, :, start : start + size].astype(F32)
            out[:, place] = part * scale
            total = total + lane_sums(part * weights[:, place].astype(F32))
            start += size
        columns.append(grads[head, :, LOGIT : LOGIT + 1].astype(F32))
    columns = jnp.concatenate(columns, axis=1)
    beta[...] = columns * scale
    gain_part[...] = jnp.sum(total, axis=1, keepdims=True) + jnp.sum(
        columns * w_beta[...].astype(F32), axis=1, keepdims=True
    )


def unpack_heads(grads, gain, w_query, w_key, w_value, w_gating, w_beta):
    shape = jax.ShapeDtypeStruct
    weights = (w_query, w_key, w_value, w_gating, w_beta)
    query, key, value, gating, beta, gain_part = pl.pallas_call(
        unpack_kernel,
        out_shape=tuple(shape(w.shape, F32) for w in weights) + (shape((gain.shape[0], 1), F32),),
        in_specs=[VMEM_SPEC] * 7,
        out_specs=[VMEM_SPEC] * 6,
        compiler_params=pltpu.CompilerParams(vmem_limit_bytes=32 * 1024 * 1024),
        name="unpack_heads",
    )(grads, gain, *weights)
    return query, key, value, gating, beta, gain_part[:, 0]


def pack_kernel(
    core, gain, w_query, w_key, w_value, w_gating, w_beta, w_output, rates, starts, kept, given
):
    heads = kept.shape[0]
    half = kept.shape[1]
    first = core[0] == 0
    scale = gain[...]
    lanes = lax.broadcasted_iota(jnp.int32, (2 * half, 128), 1)
    blank = jnp.zeros((half - 8, 128), F32)

    def two_rows(values):
        right = lanes[: values.shape[0]] >= half
        return jnp.where(right, pltpu.roll(values, half, 1), 0.0), jnp.where(right, values, 0.0)

    rate = rates[...]
    high = rate.astype(BF16).astype(F32)
    middle = (rate - high).astype(BF16).astype(F32)
    notes = [*two_rows(high), *two_rows(middle), *two_rows(rate - high - middle)]
    start_rows = two_rows(jnp.broadcast_to(starts[...], (8, 2 * half)))

    def place(head, columns, values):
        low, high = values[:half], values[half:]
        kept[head, :, columns] = jnp.where(first, low, high).astype(BF16)
        given[head, :, columns] = jnp.where(first, high, low).astype(BF16)

    for head in range(heads):
        start = 0
        for weights, size in ((w_query, KEY_SIZE), (w_key, KEY_SIZE), (w_value, DV), (w_gating, DV)):
            part = weights[:, head * size : (head + 1) * size].astype(F32) * scale
            place(head, slice(start, start + size), part)
            start += size
        beta = w_beta[:, head : head + 1].astype(F32) * scale
        place(
            head, slice(PACK, PACK + DV), w_output[head * DV : (head + 1) * DV, :].astype(F32).T
        )
        note = [part[head : head + 1] for part in notes] + [part[:1] for part in start_rows]
        note = jnp.concatenate(note + [blank], axis=0)
        place(
            head, slice(LOGIT, PACK), jnp.where(lanes < 2, beta, 0.0) + jnp.concatenate([note, note], axis=0)
        )


def pack_heads(core, gain, w_query, w_key, w_value, w_gating, w_beta, w_output, rates, starts):
    rows = gain.shape[0]
    heads = w_query.shape[1] // KEY_SIZE
    shape = jax.ShapeDtypeStruct((heads, rows // 2, PACK + DV), BF16)
    return pl.pallas_call(
        pack_kernel,
        out_shape=(shape, shape),
        in_specs=[SMEM_SPEC] + [VMEM_SPEC] * 9,
        out_specs=[VMEM_SPEC] * 2,
        compiler_params=pltpu.CompilerParams(vmem_limit_bytes=32 * 1024 * 1024),
        name="pack_heads",
    )(core, gain, w_query, w_key, w_value, w_gating, w_beta, w_output, rates, starts)


CHIPS = 16
CORES = 2
BOTH = ("seq", "head")


def along_x(index):
    return index ^ 1


def along_y(index):
    return index ^ 2


def along_z(steps):
    return lambda index: (index + 4 * steps) % CHIPS


def send(value, target):
    return lax.ppermute(value, "seq", [(index, target(index)) for index in range(CHIPS)])


def swap_cores(value):
    return lax.ppermute(value, "head", [(0, 1), (1, 0)])


def exchange(pieces):
    return lax.all_to_all(pieces, "seq", split_axis=0, concat_axis=0, tiled=True)


def after(values, *earlier):
    return lax.optimization_barrier((values, earlier))[0]


def stacked(values):
    return jnp.concatenate(values, axis=0)


def total_of(*values):
    total = values[0].astype(F32)
    for value in values[1:]:
        total = total + value.astype(F32)
    return total


def gather_levels(block):
    return [block] + [send(block, along_z(steps)) for steps in (1, 2, 3)]


def gather_near(levels):
    blocks = [levels[0], stacked(levels[1:])]
    return [(block, send(block, along_x), send(block, along_y)) for block in blocks]


def gather_far(near):
    own, others = [
        (
            [block],
            [from_x],
            [from_y],
            [
                send(from_y[: block.shape[0] // 2], along_x),
                send(from_x[block.shape[0] // 2 :], along_y),
            ],
        )
        for block, from_x, from_y in near
    ]
    return stacked([piece for pair in zip(own, others) for part in pair for piece in part])


def scatter_begin(parts):
    rows = parts.shape[0] // CHIPS
    groups = []
    for first, last in ((0, 1), (1, 4)):
        own, for_x, for_y, far = [
            parts[(4 * plane + first) * rows : (4 * plane + last) * rows] for plane in range(4)
        ]
        half = far.shape[0] // 2
        groups.append(
            (own, for_x, for_y, send(far[:half], along_x), send(far[half:], along_y))
        )
    return groups


def scatter_near(groups):
    totals = []
    for own, for_x, for_y, low, high in groups:
        half = own.shape[0] // 2
        for_y = stacked([total_of(for_y[:half], low).astype(BF16), for_y[half:]])
        for_x = stacked([for_x[:half], total_of(for_x[half:], high).astype(BF16)])
        totals.append(total_of(own, send(for_x, along_x), send(for_y, along_y)))
    return totals[0], totals[1].astype(BF16)


def scatter_levels(own, away):
    rows = own.shape[0]
    return [own] + [send(away[(j - 1) * rows : j * rows], along_z(-j)) for j in (1, 2, 3)]


def nn(a, b):
    return mm(a, b)


def nt(a, b):
    return mm(a, b, NT)


def tn(a, b):
    return mm(a, b, TN)


def head_plan(
    inputs,
    doc_starts,
    decay_rate,
    mixer_gain,
    w_query,
    w_key,
    w_value,
    w_beta,
    w_gating,
    conv_query,
    conv_key,
    conv_value,
    head_gain,
    w_output,
    feed_gain,
    w_gate,
    w_up,
    w_down,
    cotangent,
):
    chip, core = lax.axis_index("seq"), lax.axis_index("head")
    first = core == 0
    tok_rows, width = inputs.shape
    half_rows = tok_rows // CORES
    row_count = w_query.shape[0]
    half_count = row_count // CORES
    head_count = w_query.shape[1] // KEY_SIZE
    units = w_gate.shape[1] // CHIPS
    own_count = CHIPS * half_rows

    def own_rows(values):
        return lax.dynamic_slice_in_dim(values, core * half_rows, half_rows, 0)

    def in_order(own, other, axis):
        return jnp.concatenate([jnp.where(first, own, other), jnp.where(first, other, own)], axis=axis)

    def split_by_core(pieces):
        kept = lax.dynamic_slice_in_dim(pieces, core * half_count, half_count, 1)
        given = lax.dynamic_slice_in_dim(pieces, (1 - core) * half_count, half_count, 1)
        return in_order(kept, swap_cores(given), 0)

    def joined_by_core(mine):
        both = in_order(mine[:, None], swap_cores(mine)[:, None], 1)
        return both.reshape(width, mine.shape[-1])

    inputs_own = own_rows(inputs).astype(F32)
    scale_one = lax.rsqrt(jnp.mean(inputs_own * inputs_own, axis=-1, keepdims=True) + EPSILON)
    normed_one = inputs_own * scale_one
    gain_one = mixer_gain.astype(F32)[:, None]
    gain_two = feed_gain.astype(F32)[:, None]

    in_kept, in_given = pack_heads(
        core.astype(jnp.int32)[None],
        gain_one,
        w_query,
        w_key,
        w_value,
        w_gating,
        w_beta,
        w_output,
        decay_rate.T,
        doc_starts.astype(F32)[None],
    )
    in_payload = in_order(in_kept, swap_cores(in_given), 0)
    one_levels = gather_levels(normed_one.astype(BF16))
    in_mine = exchange(after(in_payload, one_levels))
    normed_all = gather_far(gather_near(one_levels))
    in_mine = after(in_mine, normed_all)
    weights_all = joined_by_core(in_mine)
    weights_in, weights_out = weights_all[:, :PACK], weights_all[:, PACK:]

    taps_here = jnp.concatenate(
        [
            conv_query.reshape(CONV, head_count, KEY_SIZE),
            conv_key.reshape(CONV, head_count, KEY_SIZE),
            conv_value.reshape(CONV, head_count, DV),
        ],
        axis=2,
    ).transpose(1, 0, 2)
    taps_there = swap_cores(taps_here)
    taps = lax.dynamic_index_in_dim(
        jnp.where(chip // head_count == core, taps_here, taps_there), chip % head_count, 0, False
    ).astype(F32)
    taps = stacked([taps, jnp.zeros_like(taps)])
    gain_head = jnp.broadcast_to(head_gain.astype(F32)[None], (8, DV))
    seen = in_mine[:, :8, PACK - tok_rows // 2 : PACK].astype(F32).reshape(CHIPS, 4, tok_rows)
    rate = (seen[:, 0] + seen[:, 1] + seen[:, 2]).reshape(-1)
    starts = seen[:, 3].reshape(-1)
    decay_grid, cols, rows = stream_tables(rate, starts)

    blocks = jnp.arange(CHIPS * CORES)
    far = blocks // CORES
    place = (
        4 * ((far ^ chip) % 4) + (chip // 4 - far // 4) % 4 + CHIPS * (blocks % CORES != core)
    ).astype(jnp.int32)

    raw = nn(normed_all, weights_in)
    column = lax.broadcasted_iota(jnp.int32, raw.shape, 1)
    pre_own = jnp.where(
        column == LOGIT + 1,
        raw - lax.reduce_precision(raw, exponent_bits=8, mantissa_bits=7),
        raw,
    ).astype(BF16)
    pre = (pre_own, swap_cores(pre_own))

    feed = jnp.concatenate(
        [
            (w_gate.astype(F32) * gain_two).astype(BF16).T.reshape(CHIPS, units, row_count),
            (w_up.astype(F32) * gain_two).astype(BF16).T.reshape(CHIPS, units, row_count),
            w_down.reshape(CHIPS, units, row_count),
        ],
        axis=1,
    )
    feed = after(feed, normed_all, weights_in, cols)
    feed_mine = exchange(feed)
    cot_own = own_rows(cotangent)
    cot_gathered = lax.all_gather(cot_own, "seq", axis=0, tiled=False)
    gated_own, gated_other, *kept = mixer_forward(place, *pre, decay_grid, cols, rows, taps, gain_head)
    mixed_parts = nt(gated_own, weights_out).astype(BF16)
    mixed_sums = scatter_begin(mixed_parts)

    mixed_sums = scatter_near(mixed_sums)
    feed_mine, normed_late, cot_all = after((feed_mine, normed_all, cot_gathered), mixed_sums)
    relative = jnp.arange(CHIPS)
    order = 4 * ((chip // 4 - relative % 4) % 4) + ((chip % 4) ^ (relative // 4))
    cot_all = cot_all.at[order].get(mode="promise_in_bounds").reshape(own_count, width)
    feed_other = swap_cores(feed_mine)

    def unit_rows(position):
        return stacked(
            [
                part[:, position * units : (position + 1) * units].transpose(1, 0, 2).reshape(units, width)
                for part in (feed_mine, feed_other)
            ]
        )

    gate_rows, up_rows, down_rows = unit_rows(0), unit_rows(1), unit_rows(2)
    cut = normed_late.reshape(own_count, CHIPS, CORES, half_count)
    cut_mine = lax.dynamic_index_in_dim(cut, core, 2, False).reshape(own_count, width // CORES)
    cut_given = lax.dynamic_index_in_dim(cut, 1 - core, 2, False).reshape(own_count, width // CORES)
    cut_other = swap_cores(cut_given)

    d_hidden = nt(cot_all, down_rows).astype(BF16)
    middle = inputs_own + total_of(*scatter_levels(*mixed_sums))
    scale_two = lax.rsqrt(jnp.mean(middle * middle, axis=-1, keepdims=True) + EPSILON)
    normed_mid = middle * scale_two
    levels = gather_levels(normed_mid.astype(BF16))
    levels[1:] = after(levels[1:], gate_rows, up_rows, d_hidden, cut_mine, cut_other)
    mid_all = gather_far(gather_near(levels))

    gate_lin = nt(mid_all, gate_rows)
    up_lin = nt(mid_all, up_rows)
    d_hidden = d_hidden.astype(F32)
    sig = jax.nn.sigmoid(gate_lin)
    act = gate_lin * sig
    hidden = (act * up_lin).astype(BF16)
    d_gate = (d_hidden * up_lin * (sig * (1.0 + gate_lin * (1.0 - sig)))).astype(BF16)
    d_up = (d_hidden * act).astype(BF16)
    e_sums = scatter_near(scatter_begin((nn(d_gate, gate_rows) + nn(d_up, up_rows)).astype(BF16)))

    feed_parts = after(nn(hidden, down_rows).astype(BF16), e_sums)
    e_two = total_of(*scatter_levels(*e_sums))
    d_middle = cot_own.astype(F32) + scale_two * (
        e_two - normed_mid * jnp.mean(e_two * normed_mid, axis=-1, keepdims=True)
    )
    levels = gather_levels(d_middle.astype(BF16))

    parts = [tn(d_gate, mid_all), tn(d_up, mid_all), tn(hidden, cot_all)]
    keep_part = stacked([part[:units] for part in parts])
    give_part = stacked([part[units:] for part in parts]).astype(BF16)
    feed_grad = (keep_part + swap_cores(give_part).astype(F32)).astype(BF16)
    feed_grad = feed_grad.reshape(3 * units, CHIPS, row_count).transpose(1, 0, 2)
    feed_grad = jnp.pad(feed_grad, ((0, 0), (0, half_count * DV // row_count), (0, 0)))
    levels[1:] = after(levels[1:], feed_grad)
    seats = jnp.arange(CHIPS)
    seat = 4 * ((seats % 4) ^ (chip % 4)) + (chip // 4 - seats // 4) % 4
    feed_parts = feed_parts.reshape(CHIPS, half_rows, width)
    feed_parts = feed_parts.at[seat].get(mode="promise_in_bounds").reshape(own_count, width)
    near = after(gather_near(levels), feed_parts)
    d_mid_all = gather_far(near)
    feed_out = lax.psum_scatter(after(feed_parts, d_mid_all), "seq", scatter_dimension=0, tiled=True)

    d_gated_own = nn(d_mid_all, weights_out).astype(BF16)
    d_gated = (d_gated_own, swap_cores(d_gated_own))
    grad_out = tn(d_mid_all, gated_own).astype(BF16).reshape(CHIPS, CORES, half_count, DV)
    grad_out = total_of(
        lax.dynamic_index_in_dim(grad_out, core, 1, False),
        swap_cores(lax.dynamic_index_in_dim(grad_out, 1 - core, 1, False)),
    ).astype(BF16)
    feed_grad = lax.dynamic_update_slice(
        feed_grad, grad_out.reshape(CHIPS, half_count * DV // row_count, row_count), (0, 3 * units, 0)
    )
    feed_back = exchange(feed_grad)
    d_pre_own, d_pre_other, grad_taps, grad_gain = mixer_backward(
        place, d_gated, pre, decay_grid, cols, taps, gain_head, kept
    )

    d_pre_own, d_pre_other, feed_back = after((d_pre_own, d_pre_other, feed_back))


    small = jnp.concatenate([jnp.sum(grad_taps, axis=1).reshape(-1), jnp.sum(grad_gain, axis=0)])
    small = small.reshape(-1, 64)
    small_rows = small.shape[0]
    grad_in = tn(cut_mine, d_pre_own) + tn(cut_other, d_pre_other)
    small = jnp.pad(small, ((0, half_count - small_rows), (PACK - 64, 0)))
    grad_in = (grad_in.reshape(CHIPS, half_count, PACK) + small).astype(BF16)
    e_parts = nt(after(d_pre_own, grad_in), weights_in).astype(BF16)
    grad_in = exchange(grad_in)
    e_sums = scatter_near(scatter_begin(e_parts))
    e_sums, grad_in = after((e_sums, grad_in))
    small = grad_in[:, :small_rows, PACK - 64 :].astype(F32).reshape(CHIPS, -1)
    taps_all = lax.dynamic_slice_in_dim(small[:, : CONV * MIXED], core * head_count, head_count, 0)
    taps_all = taps_all.reshape(head_count, CONV, MIXED).transpose(1, 0, 2)

    def heads_here(back):
        mine = lax.dynamic_slice_in_dim(back, core * head_count, head_count, 0)
        given = lax.dynamic_slice_in_dim(back, (1 - core) * head_count, head_count, 0)
        return in_order(mine, swap_cores(given), 1)

    grad_in = heads_here(grad_in)
    block_out_own = (middle + feed_out.astype(F32)).astype(BF16)
    block_out = in_order(block_out_own, swap_cores(block_out_own), 0)
    e_one = total_of(*scatter_levels(*e_sums))
    grad_own = d_middle + scale_one * (
        e_one - normed_one * jnp.mean(e_one * normed_one, axis=-1, keepdims=True)
    )
    grad_inputs = in_order(grad_own, swap_cores(grad_own), 0)

    grad_out = heads_here(feed_back[:, 3 * units :].reshape(CHIPS, half_count, DV))
    grad_output = grad_out.astype(F32).transpose(0, 2, 1).reshape(head_count * DV, row_count)
    feed_back = feed_back[:, : 3 * units].astype(F32)
    raw_gate = feed_back[:, :units].reshape(CHIPS * units, row_count).T
    raw_up = feed_back[:, units : 2 * units].reshape(CHIPS * units, row_count).T
    grad_down = feed_back[:, 2 * units :].reshape(CHIPS * units, row_count)
    feed_gain_part = jnp.sum(raw_gate * w_gate.astype(F32) + raw_up * w_up.astype(F32), axis=1)

    raw_query, raw_key, raw_value, raw_gating, raw_beta, mixer_gain_part = unpack_heads(
        grad_in, gain_one, w_query, w_key, w_value, w_gating, w_beta
    )
    gain_parts = jnp.stack([mixer_gain_part, feed_gain_part])
    gain_totals = gain_parts + swap_cores(gain_parts)

    return (
        block_out,
        grad_inputs,
        gain_totals[0],
        raw_query,
        raw_key,
        raw_value,
        raw_beta,
        raw_gating,
        taps_all[:, :, :KEY_SIZE].reshape(CONV, head_count * KEY_SIZE),
        taps_all[:, :, KEY_SIZE : 2 * KEY_SIZE].reshape(CONV, head_count * KEY_SIZE),
        taps_all[:, :, 2 * KEY_SIZE :].reshape(CONV, head_count * DV),
        jnp.sum(small[:, CONV * MIXED :], axis=0),
        grad_output,
        gain_totals[1],
        raw_gate * gain_two,
        raw_up * gain_two,
        grad_down,
    )


EXACT_PRECISION = lax.Precision.HIGHEST


def passed_along(value, axis, steps):
    count = lax.axis_size(axis)
    first, last = (max(0, -steps), min(count, count - steps))
    return lax.ppermute(value, axis, [(source, source + steps) for source in range(first, last)])


def entering(value, axis, join, neutral):
    count, mine = (lax.axis_size(axis), lax.axis_index(axis))
    pieces = jax.tree.map(lambda part: lax.all_gather(part, axis), value)
    subtotal = jax.tree.map(
        lambda part, zero: jnp.full_like(part, 0) + jnp.asarray(zero, part.dtype), value, neutral
    )

    def lap(position, subtotal):
        longer = join(subtotal, jax.tree.map(lambda part: part[position], pieces))
        return jax.tree.map(lambda new, old: jnp.where(position < mine, new, old), longer, subtotal)

    return lax.fori_loop(0, count - 1, lap, subtotal)


def carried_in(shard, axis, join, neutral):
    count = lax.axis_size(axis)
    place = lax.axis_index(axis)
    ahead = count - 1 - place
    gathered = jax.tree.map(
        lambda a, kind: lax.all_gather(a.astype(kind), axis),
        shard,
        jax.tree.map(lambda a: jnp.bfloat16 if a.dtype == jnp.float32 else a.dtype, shard),
    )
    state = jax.tree.map(lambda a, e: jnp.zeros_like(a) + jnp.asarray(e, a.dtype), shard, neutral)

    def one(lap, state):
        source = count - 1 - lap
        return join(
            state,
            jax.tree.map(
                lambda a, own: lax.dynamic_index_in_dim(a, source, 0, False).astype(own.dtype),
                gathered,
                shard,
            ),
        )

    return lax.fori_loop(0, ahead, one, state)


def high_einsum(einsum_form, *arrays):
    return jnp.einsum(
        einsum_form, *arrays, precision=EXACT_PRECISION, preferred_element_type=jnp.float32
    )


def low_dot(left_side, right_side):
    return jnp.dot(left_side, right_side, preferred_element_type=jnp.float32)


def inner_dot(left_side, right_side):
    return lax.dot_general(
        left_side, right_side, (((0,), (0,)), ((), ())), preferred_element_type=jnp.float32
    )


def outer_dot(left_side, right_side):
    return lax.dot_general(
        left_side, right_side, (((1,), (1,)), ((), ())), preferred_element_type=jnp.float32
    )


def rounded(values):
    return lax.optimization_barrier(values.astype(jnp.bfloat16)).astype(jnp.float32)


def scale_norm(values, gain_vec):
    return (
        values * lax.rsqrt(jnp.mean(values * values, axis=-1, keepdims=True) + EPSILON) * gain_vec
    )


def unit_rows(values):
    return values * lax.rsqrt(jnp.sum(values * values, axis=-1, keepdims=True) + EPSILON)


def swiglu(gate_lin, up_lin):
    return jax.nn.silu(gate_lin) * up_lin


def compose_maps(earlier_map, later_map):
    return (
        high_einsum("hde,hef->hdf", later_map[0], earlier_map[0]),
        high_einsum("hde,hef->hdf", later_map[0], earlier_map[1]) + later_map[1],
    )


def gather_plan(
    inputs,
    doc_starts,
    decay_rate,
    mixer_gain,
    w_query,
    w_key,
    w_value,
    w_beta,
    w_gating,
    conv_query,
    conv_key,
    conv_value,
    head_gain,
    w_output,
    feed_gain,
    w_gate,
    w_up,
    w_down,
    cotangent,
):
    tok_rows = inputs.shape[0]
    head_count = decay_rate.shape[1]
    key_width = w_query.shape[1]
    value_width = w_value.shape[1]
    edge_count = CONV - 1
    block_count = tok_rows // BLOCK
    gathered = (
        lax.all_gather(mixer_gain, "seq", axis=0, tiled=True),
        lax.all_gather(w_query, "seq", axis=0, tiled=True),
        lax.all_gather(w_key, "seq", axis=0, tiled=True),
        lax.all_gather(w_value, "seq", axis=0, tiled=True),
        lax.all_gather(w_beta, "seq", axis=0, tiled=True),
        lax.all_gather(w_gating, "seq", axis=0, tiled=True),
        lax.all_gather(w_output, "seq", axis=1, tiled=True),
        lax.all_gather(feed_gain, "seq", axis=0, tiled=True),
        lax.all_gather(w_gate, "seq", axis=0, tiled=True),
        lax.all_gather(w_up, "seq", axis=0, tiled=True),
        lax.all_gather(w_down, "seq", axis=1, tiled=True),
    )
    (
        gain_one,
        full_query,
        full_key,
        full_value,
        full_beta,
        full_gating,
        full_output,
        gain_two,
        full_gate,
        full_up,
        full_down,
    ) = gathered
    inputs_float = inputs.astype(jnp.float32)
    normed_float, norm_one_back = jax.vjp(scale_norm, inputs_float, gain_one.astype(jnp.float32))
    normed_one = normed_float.astype(jnp.bfloat16)
    query_pre = low_dot(normed_one, full_query).astype(jnp.bfloat16)
    key_pre = low_dot(normed_one, full_key).astype(jnp.bfloat16)
    value_pre = low_dot(normed_one, full_value).astype(jnp.bfloat16)
    gating_pre = low_dot(normed_one, full_gating).astype(jnp.bfloat16)
    beta_logit = low_dot(normed_one, full_beta)
    joined = jnp.concatenate([query_pre, key_pre, value_pre], axis=1)
    tail_starts = doc_starts[tok_rows - edge_count :]
    later_starts = jnp.cumsum(tail_starts[::-1])[::-1] - tail_starts
    sender_keep = (later_starts == 0).astype(jnp.bfloat16)[:, None]
    edge_in = passed_along(joined[tok_rows - edge_count :] * sender_keep, "seq", 1)
    local_doc = jnp.cumsum(doc_starts)
    padded_doc = jnp.concatenate([jnp.zeros((edge_count,), local_doc.dtype), local_doc])
    keep_masks = [
        (
            padded_doc[edge_count - shift_lag : edge_count - shift_lag + tok_rows] == local_doc
        ).astype(jnp.float32)[:, None]
        for shift_lag in range(CONV)
    ]

    def conv_piece(extended, conv_weights):
        mixed = keep_masks[0] * conv_weights[0] * extended[edge_count:]
        for shift_lag in range(1, CONV):
            mixed = (
                mixed
                + keep_masks[shift_lag]
                * conv_weights[shift_lag]
                * extended[edge_count - shift_lag : edge_count - shift_lag + tok_rows]
            )
        activated = jax.nn.silu(mixed)
        query_unit = unit_rows(activated[:, :key_width].reshape(tok_rows, head_count, KEY_SIZE))
        key_unit = unit_rows(
            activated[:, key_width : 2 * key_width].reshape(tok_rows, head_count, KEY_SIZE)
        )
        value_act = activated[:, 2 * key_width :].reshape(tok_rows, head_count, DV)
        return (query_unit, key_unit, value_act)

    extended = jnp.concatenate([edge_in, joined], axis=0).astype(jnp.float32)
    conv_weights = jnp.concatenate([conv_query, conv_key, conv_value], axis=1).astype(jnp.float32)
    (query_unit, key_unit, value_act), conv_back = jax.vjp(conv_piece, extended, conv_weights)

    def to_blocks(values):
        return values.reshape(block_count, BLOCK, head_count, values.shape[-1]).transpose(
            0, 2, 1, 3
        )

    def from_blocks(values):
        return values.transpose(0, 2, 1, 3).reshape(tok_rows, head_count, values.shape[-1])

    log_rate = jnp.log(decay_rate).reshape(block_count, BLOCK, head_count).transpose(0, 2, 1)
    log_level = jnp.cumsum(log_rate, axis=-1)
    segment = jnp.cumsum(doc_starts.reshape(block_count, BLOCK), axis=-1)
    positions = jnp.arange(BLOCK)
    causal = positions[:, None] >= positions[None, :]
    strict = positions[:, None] > positions[None, :]
    linked = (segment[:, None, :, None] == segment[:, None, None, :]) & causal
    spread = jnp.where(causal, log_level[..., :, None] - log_level[..., None, :], 0.0)
    decay_grid = jnp.where(linked, jnp.exp(spread), 0.0)
    carry_in = jnp.where(segment[:, None, :] == 0, jnp.exp(log_level), 0.0)
    tail_decay = decay_grid[..., BLOCK - 1, :]
    key_eye = jnp.eye(KEY_SIZE, dtype=jnp.float32)
    block_eye = jnp.eye(BLOCK, dtype=jnp.float32)

    def block_terms(query_blocks, key_blocks, value_blocks, logit_blocks):
        beta_gate = jax.nn.sigmoid(logit_blocks)
        key_gram = high_einsum("nhcd,nhmd->nhcm", key_blocks, key_blocks)
        system = block_eye + jnp.where(strict, decay_grid * key_gram * beta_gate[..., None, :], 0.0)
        right_side = jnp.concatenate([value_blocks, carry_in[..., None] * key_blocks], axis=-1)
        solved = jax.scipy.linalg.solve_triangular(
            system, right_side, lower=True, unit_diagonal=True
        )
        fresh_values = solved[..., :DV]
        fresh_keys = solved[..., DV:]
        mixing = (
            high_einsum("nhcd,nhmd->nhcm", query_blocks, key_blocks)
            * decay_grid
            * beta_gate[..., None, :]
        )
        weighted = key_blocks * (tail_decay * beta_gate)[..., None]
        block_maps = carry_in[..., BLOCK - 1, None, None] * key_eye - high_einsum(
            "nhcd,nhce->nhde", weighted, fresh_keys
        )
        block_adds = high_einsum("nhcd,nhce->nhde", weighted, fresh_values)

        def chain_step(current, element):
            return (compose_maps(current, element), None)

        start_map = (
            jnp.broadcast_to(key_eye, (head_count, KEY_SIZE, KEY_SIZE)),
            jnp.zeros((head_count, KEY_SIZE, DV), jnp.float32),
        )
        device_pair, _ = lax.scan(chain_step, start_map, (block_maps, block_adds))
        return (
            (fresh_values, fresh_keys, mixing, block_maps, block_adds),
            device_pair[0],
            device_pair[1],
        )

    def block_outputs(block_parts, query_blocks, start_state):

        def step_block(current, element):
            fresh_values, fresh_keys, mixing, block_map, block_add, query_part, carry_part = element
            updated = fresh_values - high_einsum("hcd,hde->hce", fresh_keys, current)
            produced_output = (
                carry_part[..., None] * high_einsum("hcd,hde->hce", query_part, current)
                + high_einsum("hcm,hme->hce", mixing, updated)
            ) * KEY_SIZE ** (-0.5)
            return (high_einsum("hde,hef->hdf", block_map, current) + block_add, produced_output)

        _, emitted_all = lax.scan(step_block, start_state, block_parts + (query_blocks, carry_in))
        return emitted_all

    query_blocks = to_blocks(rounded(query_unit))
    key_blocks = to_blocks(rounded(key_unit))
    value_blocks = to_blocks(rounded(value_act))
    logit_blocks = beta_logit.reshape(block_count, BLOCK, head_count).transpose(0, 2, 1)
    (block_parts, device_map, device_add), terms_back = jax.vjp(
        block_terms, query_blocks, key_blocks, value_blocks, logit_blocks
    )
    identity = (jnp.broadcast_to(key_eye, device_map.shape), jnp.zeros_like(device_add))
    prefix = entering((device_map, device_add), "seq", compose_maps, identity)
    start_state = prefix[1]
    produced_output, emitted_back = jax.vjp(block_outputs, block_parts, query_blocks, start_state)

    def gated_norm(values, gating_values, gain_vec):
        normed_out = values * lax.rsqrt(jnp.mean(values * values, axis=-1, keepdims=True) + EPSILON)
        return (normed_out * gain_vec * jax.nn.silu(gating_values)).reshape(tok_rows, value_width)

    mixer_out = from_blocks(produced_output)
    gated_float, gated_back = jax.vjp(
        gated_norm,
        mixer_out,
        gating_pre.astype(jnp.float32).reshape(tok_rows, head_count, DV),
        head_gain.astype(jnp.float32),
    )
    gated_out = gated_float.astype(jnp.bfloat16)
    middle = inputs_float + lax.psum(
        low_dot(gated_out, full_output).astype(jnp.bfloat16), "head"
    ).astype(jnp.float32)
    normed_middle, norm_two_back = jax.vjp(scale_norm, middle, gain_two.astype(jnp.float32))
    normed_two = normed_middle.astype(jnp.bfloat16)
    gate_lin = low_dot(normed_two, full_gate)
    up_lin = low_dot(normed_two, full_up)
    hidden_float, swiglu_back = jax.vjp(swiglu, gate_lin, up_lin)
    hidden = hidden_float.astype(jnp.bfloat16)
    feed_out = lax.psum(low_dot(hidden, full_down).astype(jnp.bfloat16), "head").astype(jnp.float32)
    block_out = (middle + feed_out).astype(jnp.bfloat16)
    regathered = (
        lax.all_gather(w_query, "seq", axis=0, tiled=True),
        lax.all_gather(w_key, "seq", axis=0, tiled=True),
        lax.all_gather(w_value, "seq", axis=0, tiled=True),
        lax.all_gather(w_beta, "seq", axis=0, tiled=True),
        lax.all_gather(w_gating, "seq", axis=0, tiled=True),
        lax.all_gather(w_output, "seq", axis=1, tiled=True),
        lax.all_gather(w_gate, "seq", axis=0, tiled=True),
        lax.all_gather(w_up, "seq", axis=0, tiled=True),
        lax.all_gather(w_down, "seq", axis=1, tiled=True),
    )
    (
        full_query,
        full_key,
        full_value,
        full_beta,
        full_gating,
        full_output,
        full_gate,
        full_up,
        full_down,
    ) = regathered
    cotangent_float = cotangent.astype(jnp.float32)
    grad_down = inner_dot(hidden, cotangent)
    d_hidden = rounded(outer_dot(cotangent, full_down))
    d_gate_float, d_up_float = swiglu_back(d_hidden)
    d_gate = d_gate_float.astype(jnp.bfloat16)
    d_up = d_up_float.astype(jnp.bfloat16)
    grad_gate = inner_dot(normed_two, d_gate)
    grad_up = inner_dot(normed_two, d_up)
    d_normed_two = lax.psum(
        (outer_dot(d_gate, full_gate) + outer_dot(d_up, full_up)).astype(jnp.bfloat16), "head"
    ).astype(jnp.float32)
    d_middle_norm, grad_gain_two = norm_two_back(d_normed_two)
    d_middle = cotangent_float + d_middle_norm
    d_middle_low = d_middle.astype(jnp.bfloat16)
    grad_output = inner_dot(gated_out, d_middle_low)
    d_gated = rounded(outer_dot(d_middle_low, full_output))
    d_mixer_out, d_gating_float, grad_head_part = gated_back(d_gated)
    d_gating = d_gating_float.reshape(tok_rows, value_width).astype(jnp.bfloat16)
    d_parts, d_query_late, d_start = emitted_back(to_blocks(d_mixer_out))
    chained = carried_in((jnp.swapaxes(device_map, 1, 2), d_start), "seq", compose_maps, identity)
    d_end = chained[1]
    d_map = high_einsum("hde,hfe->hdf", d_end, start_state)
    d_query_early, d_key_blocks, d_value_blocks, d_logit_blocks = terms_back(
        (d_parts, d_map, d_end)
    )
    d_query_unit = rounded(from_blocks(d_query_early + d_query_late))
    d_key_unit = rounded(from_blocks(d_key_blocks))
    d_value_act = rounded(from_blocks(d_value_blocks))
    d_beta_logit = (
        d_logit_blocks.transpose(0, 2, 1).reshape(tok_rows, head_count).astype(jnp.bfloat16)
    )
    d_extended, grad_conv_all = conv_back((d_query_unit, d_key_unit, d_value_act))
    returned = passed_along(d_extended[:edge_count].astype(jnp.bfloat16), "seq", -1).astype(
        jnp.float32
    )
    d_rows = d_extended[edge_count:]
    d_rows = jnp.concatenate(
        [
            d_rows[: tok_rows - edge_count],
            d_rows[tok_rows - edge_count :] + returned * sender_keep.astype(jnp.float32),
        ],
        axis=0,
    )
    d_joined = d_rows.astype(jnp.bfloat16)
    d_query_pre = d_joined[:, :key_width]
    d_key_pre = d_joined[:, key_width : 2 * key_width]
    d_value_pre = d_joined[:, 2 * key_width :]
    grad_query = inner_dot(normed_one, d_query_pre)
    grad_key = inner_dot(normed_one, d_key_pre)
    grad_value = inner_dot(normed_one, d_value_pre)
    grad_gating = inner_dot(normed_one, d_gating)
    grad_beta = inner_dot(normed_one, d_beta_logit)
    d_normed_part = (
        outer_dot(d_query_pre, full_query)
        + outer_dot(d_key_pre, full_key)
        + outer_dot(d_value_pre, full_value)
        + outer_dot(d_gating, full_gating)
        + outer_dot(d_beta_logit, full_beta)
    )
    d_normed_one, head_total = (
        lax.psum(d_normed_part.astype(jnp.bfloat16), "head").astype(jnp.float32),
        lax.psum(grad_head_part.astype(jnp.bfloat16), "head").astype(jnp.float32),
    )
    d_inputs_norm, grad_gain_one = norm_one_back(d_normed_one)
    grad_inputs = d_middle + d_inputs_norm
    small_totals = lax.psum((grad_conv_all, head_total), "seq")
    conv_total = small_totals[0]
    totals = (
        lax.psum_scatter(grad_gain_one, "seq", scatter_dimension=0, tiled=True),
        lax.psum_scatter(grad_query, "seq", scatter_dimension=0, tiled=True),
        lax.psum_scatter(grad_key, "seq", scatter_dimension=0, tiled=True),
        lax.psum_scatter(grad_value, "seq", scatter_dimension=0, tiled=True),
        lax.psum_scatter(grad_beta, "seq", scatter_dimension=0, tiled=True),
        lax.psum_scatter(grad_gating, "seq", scatter_dimension=0, tiled=True),
        lax.psum_scatter(grad_output, "seq", scatter_dimension=1, tiled=True),
        lax.psum_scatter(grad_gain_two, "seq", scatter_dimension=0, tiled=True),
        lax.psum_scatter(grad_gate, "seq", scatter_dimension=0, tiled=True),
        lax.psum_scatter(grad_up, "seq", scatter_dimension=0, tiled=True),
        lax.psum_scatter(grad_down, "seq", scatter_dimension=1, tiled=True),
    )
    return (
        block_out,
        grad_inputs,
        totals[0],
        totals[1],
        totals[2],
        totals[3],
        totals[4],
        totals[5],
        conv_total[:, :key_width],
        conv_total[:, key_width : 2 * key_width],
        conv_total[:, 2 * key_width :],
        small_totals[1],
        totals[6],
        totals[7],
        totals[8],
        totals[9],
        totals[10],
    )


def solution(mesh):
    in_specs = (
        P("seq", None),
        P("seq"),
        P("seq", "head"),
        P("seq"),
        P("seq", "head"),
        P("seq", "head"),
        P("seq", "head"),
        P("seq", "head"),
        P("seq", "head"),
        P(None, "head"),
        P(None, "head"),
        P(None, "head"),
        P(),
        P("head", "seq"),
        P("seq"),
        P("seq", "head"),
        P("seq", "head"),
        P("head", "seq"),
        P("seq", None),
    )
    out_specs = (
        P("seq", None),
        P("seq", None),
        P("seq"),
        P("seq", "head"),
        P("seq", "head"),
        P("seq", "head"),
        P("seq", "head"),
        P("seq", "head"),
        P(None, "head"),
        P(None, "head"),
        P(None, "head"),
        P(),
        P("head", "seq"),
        P("seq"),
        P("seq", "head"),
        P("seq", "head"),
        P("head", "seq"),
    )
    whole_heads = mesh.shape["seq"] == CHIPS and mesh.shape["head"] == CORES
    per_device = head_plan if whole_heads else gather_plan
    return jax.shard_map(
        per_device, mesh=mesh, in_specs=in_specs, out_specs=out_specs, check_vma=False
    )
```

```python
import jax
import jax.numpy as jnp
from jax import lax
from jax.sharding import PartitionSpec as P
from jax.experimental import pallas as pl
from jax.experimental.pallas import tpu as pltpu

KEY_SIZE = 128
DV = 256
CONV = 4
BLOCK = 64
EPSILON = 1e-06
F32 = jnp.float32
BF16 = jnp.bfloat16
LOGIT = 2 * KEY_SIZE + 2 * DV
PACK = LOGIT + 128
MIXED = 2 * KEY_SIZE + DV
SCALE = KEY_SIZE**-0.5
UNROLL = 16


def mm(a, b, dims=((1,), (0,))):
    return lax.dot_general(a, b, (dims, ((), ())), preferred_element_type=F32)


NT = ((1,), (1,))
TN = ((0,), (0,))


def halves(a):
    high = a.astype(BF16)
    return high, (a - high.astype(F32)).astype(BF16)


def mm_left(a, b, dims=((1,), (0,))):
    high, low = halves(a)
    return mm(high, b, dims) + mm(low, b, dims)


def mm_right(a, b, dims=((1,), (0,))):
    high, low = halves(b)
    return mm(a, high, dims) + mm(a, low, dims)


def mm_both(a, b, dims=((1,), (0,))):
    a_high, a_low = halves(a)
    b_high, b_low = halves(b)
    return mm(a_high, b_high, dims) + (mm(a_high, b_low, dims) + mm(a_low, b_high, dims))


def block_masks():
    row = lax.broadcasted_iota(jnp.int32, (BLOCK, BLOCK), 0)
    col = lax.broadcasted_iota(jnp.int32, (BLOCK, BLOCK), 1)
    strict = row > col
    levels = []
    size = 1
    while size < BLOCK:
        levels.append(
            (row // (2 * size) == col // (2 * size)) & (row // size % 2 == 1) & (col // size % 2 == 0)
        )
        size *= 2
    return strict, levels, (row == col).astype(F32)


def unit_lower_inverses(systems, levels, eye):
    inverses = [eye - jnp.where(levels[0], system, 0.0) for system in systems]
    for level in levels[1:]:
        inner = [
            mm_both(jnp.where(level, system, 0.0), inverse)
            for system, inverse in zip(systems, inverses)
        ]
        inverses = [
            inverse - mm_both(inverse, part) for inverse, part in zip(inverses, inner)
        ]
    return inverses


def rows_of(index):
    return pl.ds(pl.multiple_of(index * BLOCK, BLOCK), BLOCK)


def row_sums(values):
    return jnp.sum(values.reshape(values.shape[0] // 8, 8, values.shape[1]), axis=0)


def beta_columns(packed):
    logit = packed[:, :1].astype(F32) + packed[:, 1:2].astype(F32)
    beta = jax.nn.sigmoid(logit)
    return beta, jnp.broadcast_to(beta, (BLOCK, 128)).T[:BLOCK]


def units_of(mixed):
    gate = jax.nn.sigmoid(mixed)
    act = mixed * gate
    query, key = act[:, :KEY_SIZE], act[:, KEY_SIZE : 2 * KEY_SIZE]
    query_scale = lax.rsqrt(jnp.sum(query * query, axis=-1, keepdims=True) + EPSILON)
    key_scale = lax.rsqrt(jnp.sum(key * key, axis=-1, keepdims=True) + EPSILON)
    return gate, act, query * query_scale, key * key_scale, query_scale, key_scale


def forward_kernel(
    place,
    pre_own,
    pre_other,
    decay_grid,
    cols,
    rows,
    taps,
    head_gain,
    gated_own,
    gated_other,
    mixer_to,
    mixed_to,
    inverse_to,
    state_to,
    fresh_to,
    carry_to,
    read_to,
    mixer_out,
    mixed_out,
    inverse_out,
    state_out,
    fresh_out,
    carry_out,
    read_out,
    both_maps,
    value_part,
    out_part,
    add_part,
    pre,
    gated,
    marks,
):
    blocks = decay_grid.shape[0]
    half = pre_own.shape[0]
    loads = [
        pltpu.make_async_copy(pre_own, pre.at[:half], marks.at[0]),
        pltpu.make_async_copy(pre_other, pre.at[half:], marks.at[1]),
    ]
    prepared = [
        pltpu.make_async_copy(mixed_out, mixed_to, marks.at[2]),
        pltpu.make_async_copy(inverse_out, inverse_to, marks.at[3]),
        pltpu.make_async_copy(carry_out, carry_to, marks.at[4]),
        pltpu.make_async_copy(read_out, read_to, marks.at[5]),
    ]
    chained = [pltpu.make_async_copy(state_out, state_to, marks.at[6])]
    finished = [
        pltpu.make_async_copy(gated.at[:half], gated_own, marks.at[7]),
        pltpu.make_async_copy(gated.at[half:], gated_other, marks.at[8]),
        pltpu.make_async_copy(mixer_out, mixer_to, marks.at[9]),
        pltpu.make_async_copy(fresh_out, fresh_to, marks.at[10]),
    ]
    for copy in loads:
        copy.start()
    for copy in loads:
        copy.wait()
    strict, levels, eye = block_masks()
    key_eye = (
        lax.broadcasted_iota(jnp.int32, (KEY_SIZE, KEY_SIZE), 0)
        == lax.broadcasted_iota(jnp.int32, (KEY_SIZE, KEY_SIZE), 1)
    ).astype(F32)

    def prepare(group, _):
        work = []
        for lane in range(UNROLL):
            b = group * UNROLL + lane
            here = rows_of(b)
            source = place[b]
            before = place[jnp.maximum(b - 1, 0)]
            current = pre[rows_of(source), :MIXED].astype(F32)
            edge = pre[
                pl.ds(pl.multiple_of(before * BLOCK + BLOCK - 16, 16), 16), :MIXED
            ].astype(F32)
            extended = jnp.concatenate([edge[8:], current], axis=0)
            mixed = taps[0:1] * current
            for lag in range(1, CONV):
                mixed = mixed + (taps[lag : lag + 1] * cols[here, 1 + lag : 2 + lag]) * pltpu.roll(
                    extended, lag, 0
                )[8:]
            mixed_out[here, :] = mixed
            _, act, query, key, _, _ = units_of(mixed)
            query, key, value = query.astype(BF16), key.astype(BF16), act[:, 2 * KEY_SIZE :].astype(BF16)
            beta, beta_row = beta_columns(pre[rows_of(source), LOGIT:])
            link = decay_grid[b] * beta_row
            system = jnp.where(strict, link * mm(key, key, NT), 0.0)
            mixing = (SCALE * mm(query, key, NT)) * link
            work.append((b, here, query, key, value, beta, system, mixing))
        inverses = unit_lower_inverses([item[6] for item in work], levels, eye)
        for (b, here, query, key, value, beta, system, mixing), inverse in zip(work, inverses):
            inverse_out[here, :] = inverse
            carry = cols[here, 0:1]
            tail = cols[here, 1:2] * beta
            fresh_values = mm_left(inverse, value)
            fresh_keys = mm_left(inverse * rows[b, 0:1, :], key)
            low_mixing = mixing.astype(BF16)
            read = (SCALE * carry) * query.astype(F32) - mm(low_mixing, fresh_keys.astype(BF16))
            value_part[here, :] = fresh_values
            out_part[here, :] = mm(low_mixing, fresh_values.astype(BF16))
            read_out[here, :] = read.astype(BF16)
            both_maps[b, :BLOCK] = read.astype(BF16)
            both_maps[b, BLOCK:] = fresh_keys.astype(BF16)
            carry_end = carry[BLOCK - 1 : BLOCK]
            carry_out[b] = carry_end * key_eye - mm_right(key, tail * fresh_keys, TN)
            add_part[b] = mm_right(key, tail * fresh_values, TN)
        return 0

    lax.fori_loop(0, blocks // UNROLL, prepare, 0)
    for copy in prepared:
        copy.start()

    def chain(b, state):
        state_out[b] = state.astype(BF16)
        return mm_both(carry_out[b], state) + add_part[b]

    lax.fori_loop(0, blocks, chain, jnp.zeros((KEY_SIZE, DV), F32))
    for copy in chained:
        copy.start()

    def finish(group, _):
        for lane in range(UNROLL):
            b = group * UNROLL + lane
            here = rows_of(b)
            source = place[b]
            both = mm(both_maps[b], state_out[b])
            produced = both[:BLOCK] + out_part[here, :]
            fresh_out[here, :] = (value_part[here, :] - both[BLOCK:]).astype(BF16)
            mixer_out[here, :] = produced
            scale = lax.rsqrt(jnp.mean(produced * produced, axis=-1, keepdims=True) + EPSILON)
            gate = pre[rows_of(source), MIXED:LOGIT].astype(F32)
            gated[rows_of(source), :] = (
                produced * scale * head_gain[0:1] * (gate * jax.nn.sigmoid(gate))
            ).astype(BF16)
        return 0

    lax.fori_loop(0, blocks // UNROLL, finish, 0)
    for copy in finished:
        copy.start()
    for copy in prepared + chained + finished:
        copy.wait()


def backward_kernel(
    place,
    d_gated_own,
    d_gated_other,
    pre_own,
    pre_other,
    decay_grid,
    cols,
    taps,
    head_gain,
    mixer_from,
    mixed_from,
    inverse_from,
    state_from,
    fresh_from,
    carry_from,
    read_from,
    d_pre_own,
    d_pre_other,
    grad_taps,
    grad_gain,
    mixer_out,
    mixed_in,
    inverse_in,
    state_in,
    fresh_in,
    carry_in,
    read_in,
    d_out,
    pull_part,
    end_state,
    d_mixed,
    d_gated,
    pre,
    d_main,
    d_gating,
    d_logits,
    marks,
):
    blocks = decay_grid.shape[0]
    half = pre_own.shape[0]
    first_loads = [
        pltpu.make_async_copy(pre_own, pre.at[:half], marks.at[0]),
        pltpu.make_async_copy(pre_other, pre.at[half:], marks.at[1]),
        pltpu.make_async_copy(d_gated_own, d_gated.at[:half], marks.at[2]),
        pltpu.make_async_copy(d_gated_other, d_gated.at[half:], marks.at[3]),
        pltpu.make_async_copy(mixer_from, mixer_out, marks.at[4]),
        pltpu.make_async_copy(read_from, read_in, marks.at[5]),
    ]
    chain_loads = [pltpu.make_async_copy(carry_from, carry_in, marks.at[6])]
    late_loads = [
        pltpu.make_async_copy(mixed_from, mixed_in, marks.at[7]),
        pltpu.make_async_copy(inverse_from, inverse_in, marks.at[8]),
        pltpu.make_async_copy(state_from, state_in, marks.at[9]),
        pltpu.make_async_copy(fresh_from, fresh_in, marks.at[10]),
    ]

    def stores(source, columns, mark):
        return [
            pltpu.make_async_copy(source.at[:half], d_pre_own.at[:, columns], marks.at[mark]),
            pltpu.make_async_copy(source.at[half:], d_pre_other.at[:, columns], marks.at[mark + 1]),
        ]

    gating_stores = stores(d_gating, slice(MIXED, LOGIT), 11)
    logit_stores = stores(d_logits, slice(LOGIT, PACK), 13)
    main_stores = stores(d_main, slice(0, MIXED), 15)
    for copy in first_loads + chain_loads + late_loads:
        copy.start()
    for copy in first_loads:
        copy.wait()
    strict, _, _ = block_masks()
    lane_index = lax.broadcasted_iota(jnp.int32, (BLOCK, PACK - LOGIT), 1)
    grad_taps[...] = jnp.zeros_like(grad_taps)
    grad_gain[...] = jnp.zeros_like(grad_gain)
    d_mixed[blocks * BLOCK :, :] = jnp.zeros((8, MIXED), F32)

    def prepare(group, _):
        for lane in range(UNROLL):
            b = group * UNROLL + lane
            here = rows_of(b)
            there = rows_of(place[b])
            grad = d_gated[there, :].astype(F32)
            gate = pre[there, MIXED:LOGIT].astype(F32)
            produced = mixer_out[here, :]
            scale = lax.rsqrt(jnp.mean(produced * produced, axis=-1, keepdims=True) + EPSILON)
            normed = produced * scale
            sig = jax.nn.sigmoid(gate)
            act = gate * sig
            weighted = grad * head_gain[0:1]
            pulled = weighted * act
            along = jnp.mean(pulled * normed, axis=-1, keepdims=True)
            low = (scale * (pulled - normed * along)).astype(BF16)
            grad_gain[...] += row_sums(grad * normed * act)
            d_gating[there, :] = (
                weighted * normed * (sig * (1.0 + gate * (1.0 - sig)))
            ).astype(BF16)
            d_out[here, :] = low
            pull_part[b] = mm(read_in[here, :], low, TN)
        return 0

    lax.fori_loop(0, blocks // UNROLL, prepare, 0)
    for copy in gating_stores:
        copy.start()
    for copy in chain_loads:
        copy.wait()

    def chain(step, state):
        b = blocks - 1 - step
        end_state[b] = state.astype(BF16)
        return mm_both(carry_in[b], state, TN) + pull_part[b]

    lax.fori_loop(0, blocks, chain, jnp.zeros((KEY_SIZE, DV), F32))
    for copy in late_loads:
        copy.wait()

    def finish(group, _):
        for lane in range(UNROLL):
            b = group * UNROLL + lane
            here = rows_of(b)
            there = rows_of(place[b])
            mixed = mixed_in[here, :]
            gate, act, query_unit, key_unit, query_scale, key_scale = units_of(mixed)
            query, key = query_unit.astype(BF16), key_unit.astype(BF16)
            beta, beta_row = beta_columns(pre[there, LOGIT:])
            link = decay_grid[b] * beta_row
            mixing = (SCALE * mm(query, key, NT)) * link
            carry = cols[here, 0:1]
            tail = cols[here, 1:2] * beta
            low = d_out[here, :]
            end = end_state[b]
            start = state_in[b]
            fresh = fresh_in[here, :]
            d_fresh = mm(mixing.astype(BF16), low, TN) + tail * mm(key, end)
            d_right = mm_left(inverse_in[here, :], d_fresh.astype(BF16), TN)
            d_right_low = d_right.astype(BF16)
            d_logit = (1.0 - beta) * jnp.sum(fresh.astype(F32) * d_right, axis=-1, keepdims=True)
            pair = jnp.concatenate([low, d_right_low], axis=0)
            on_state = mm(pair, start, NT)
            on_fresh = mm(pair, fresh, NT)
            read_grad = (SCALE * on_fresh[:BLOCK]) * link
            system_grad = jnp.where(strict, -on_fresh[BLOCK:] * link, 0.0)
            d_query = (SCALE * carry) * on_state[:BLOCK] + mm(read_grad.astype(BF16), key)
            d_key = (
                mm((system_grad + system_grad.T).astype(BF16), key)
                + mm(read_grad.astype(BF16), query, TN)
                + tail * mm(fresh, end, NT)
                - carry * on_state[BLOCK:]
            )
            d_query = d_query.astype(BF16).astype(F32)
            d_key = d_key.astype(BF16).astype(F32)
            slope = gate * (1.0 + mixed * (1.0 - gate))
            d_mixed[here, :KEY_SIZE] = (
                d_query - query_unit * jnp.sum(query_unit * d_query, axis=-1, keepdims=True)
            ) * (query_scale * slope[:, :KEY_SIZE])
            d_mixed[here, KEY_SIZE : 2 * KEY_SIZE] = (
                d_key - key_unit * jnp.sum(key_unit * d_key, axis=-1, keepdims=True)
            ) * (key_scale * slope[:, KEY_SIZE : 2 * KEY_SIZE])
            d_mixed[here, 2 * KEY_SIZE :] = d_right_low.astype(F32) * slope[:, 2 * KEY_SIZE :]
            d_logits[there, :] = jnp.where(lane_index == 0, d_logit, 0.0).astype(BF16)
        return 0

    lax.fori_loop(0, blocks // UNROLL, finish, 0)
    for copy in logit_stores:
        copy.start()

    def unmix(group, _):
        for lane in range(UNROLL):
            b = group * UNROLL + lane
            there = rows_of(place[b])
            longer = pl.ds(pl.multiple_of(b * BLOCK, BLOCK), BLOCK + 8)
            extended = d_mixed[longer, :]
            current = pre[there, :MIXED].astype(F32)
            total = taps[0:1] * extended[:BLOCK]
            grad_taps[0] += row_sums(current * extended[:BLOCK])
            for lag in range(1, CONV):
                kept = cols[longer, 1 + lag : 2 + lag] * extended
                moved = pltpu.roll(kept, BLOCK + 8 - lag, 0)[:BLOCK]
                total = total + taps[lag : lag + 1] * moved
                grad_taps[lag] += row_sums(current * moved)
            d_main[there, :] = total.astype(BF16)
        return 0

    lax.fori_loop(0, blocks // UNROLL, unmix, 0)
    for copy in main_stores:
        copy.start()
    for copy in gating_stores + logit_stores + main_stores:
        copy.wait()


VMEM_SPEC = pl.BlockSpec(memory_space=pltpu.VMEM)
SMEM_SPEC = pl.BlockSpec(memory_space=pltpu.SMEM)
ANY_SPEC = pl.BlockSpec(memory_space=pl.ANY)
FORWARD_COST = pl.CostEstimate(flops=30_000_000_000, bytes_accessed=100_000_000, transcendentals=0)
BACKWARD_COST = pl.CostEstimate(flops=1_000_000, bytes_accessed=1_000, transcendentals=0)


def mixer_forward(place, pre_own, pre_other, decay_grid, cols, rows, taps, head_gain):
    blocks = decay_grid.shape[0]
    half, tokens = pre_own.shape[0], blocks * BLOCK
    shape = jax.ShapeDtypeStruct
    return pl.pallas_call(
        forward_kernel,
        out_shape=(
            shape((half, DV), BF16),
            shape((half, DV), BF16),
            shape((tokens, DV), F32),
            shape((tokens, MIXED), F32),
            shape((tokens, BLOCK), F32),
            shape((blocks, KEY_SIZE, DV), BF16),
            shape((tokens, DV), BF16),
            shape((blocks, KEY_SIZE, KEY_SIZE), F32),
            shape((tokens, KEY_SIZE), BF16),
        ),
        in_specs=[SMEM_SPEC] + [ANY_SPEC] * 2 + [VMEM_SPEC] * 5,
        out_specs=[ANY_SPEC] * 9,
        scratch_shapes=[
            pltpu.VMEM((tokens, DV), F32),
            pltpu.VMEM((tokens, MIXED), F32),
            pltpu.VMEM((tokens, BLOCK), F32),
            pltpu.VMEM((blocks, KEY_SIZE, DV), BF16),
            pltpu.VMEM((tokens, DV), BF16),
            pltpu.VMEM((blocks, KEY_SIZE, KEY_SIZE), F32),
            pltpu.VMEM((tokens, KEY_SIZE), BF16),
            pltpu.VMEM((blocks, 2 * BLOCK, KEY_SIZE), BF16),
            pltpu.VMEM((tokens, DV), F32),
            pltpu.VMEM((tokens, DV), F32),
            pltpu.VMEM((blocks, KEY_SIZE, DV), F32),
            pltpu.VMEM((tokens, PACK), BF16),
            pltpu.VMEM((tokens, DV), BF16),
            pltpu.SemaphoreType.DMA((11,)),
        ],
        compiler_params=pltpu.CompilerParams(vmem_limit_bytes=52 * 1024 * 1024),
        cost_estimate=FORWARD_COST,
        name="mixer_forward",
    )(place, pre_own, pre_other, decay_grid, cols, rows, taps, head_gain)


def mixer_backward(place, d_gated, pre, decay_grid, cols, taps, head_gain, kept):
    blocks = decay_grid.shape[0]
    half, tokens = pre[0].shape[0], blocks * BLOCK
    shape = jax.ShapeDtypeStruct
    return pl.pallas_call(
        backward_kernel,
        out_shape=(
            shape((half, PACK), BF16),
            shape((half, PACK), BF16),
            shape((CONV, 8, MIXED), F32),
            shape((8, DV), F32),
        ),
        in_specs=[SMEM_SPEC] + [ANY_SPEC] * 4 + [VMEM_SPEC] * 4 + [ANY_SPEC] * 7,
        out_specs=[ANY_SPEC] * 2 + [VMEM_SPEC] * 2,
        scratch_shapes=[
            pltpu.VMEM((tokens, DV), F32),
            pltpu.VMEM((tokens, MIXED), F32),
            pltpu.VMEM((tokens, BLOCK), F32),
            pltpu.VMEM((blocks, KEY_SIZE, DV), BF16),
            pltpu.VMEM((tokens, DV), BF16),
            pltpu.VMEM((blocks, KEY_SIZE, KEY_SIZE), F32),
            pltpu.VMEM((tokens, KEY_SIZE), BF16),
            pltpu.VMEM((tokens, DV), BF16),
            pltpu.VMEM((blocks, KEY_SIZE, DV), F32),
            pltpu.VMEM((blocks, KEY_SIZE, DV), BF16),
            pltpu.VMEM((tokens + 8, MIXED), F32),
            pltpu.VMEM((tokens, DV), BF16),
            pltpu.VMEM((tokens, PACK), BF16),
            pltpu.VMEM((tokens, MIXED), BF16),
            pltpu.VMEM((tokens, DV), BF16),
            pltpu.VMEM((tokens, PACK - LOGIT), BF16),
            pltpu.SemaphoreType.DMA((17,)),
        ],
        compiler_params=pltpu.CompilerParams(vmem_limit_bytes=52 * 1024 * 1024),
        cost_estimate=BACKWARD_COST,
        name="mixer_backward",
    )(place, *d_gated, *pre, decay_grid, cols, taps, head_gain, *kept)


def stream_tables(rate, starts):
    blocks = rate.shape[0] // BLOCK
    level = jnp.cumsum(jnp.log(rate).reshape(blocks, BLOCK), axis=-1)
    segment = jnp.cumsum(starts.reshape(blocks, BLOCK), axis=-1)
    positions = jnp.arange(BLOCK)
    causal = positions[:, None] >= positions[None, :]
    linked = (segment[:, :, None] == segment[:, None, :]) & causal
    spread = jnp.where(causal, level[:, :, None] - level[:, None, :], 0.0)
    decay_grid = jnp.where(linked, jnp.exp(spread), 0.0)
    carry = jnp.where(segment == 0, jnp.exp(level), 0.0)
    tail = decay_grid[:, BLOCK - 1, :]
    keep = 1.0 - starts
    padded = jnp.concatenate([jnp.zeros((2,), F32), keep])
    keep_two = keep * padded[1:-1]
    keep_three = keep_two * padded[:-2]
    zero = jnp.zeros_like(keep)
    cols = jnp.stack([carry.reshape(-1), tail.reshape(-1), keep, keep_two, keep_three, zero, zero, zero], axis=1)
    cols = jnp.concatenate([cols, jnp.zeros((8, 8), F32)], axis=0)
    rows = jnp.broadcast_to(carry[:, None, :], (blocks, 8, BLOCK))
    return decay_grid, cols, rows


def unpack_kernel(
    grads, gain, w_query, w_key, w_value, w_gating, w_beta, query, key, value, gating, beta, gain_part
):
    heads = grads.shape[0]
    scale = gain[...]
    total = jnp.zeros((grads.shape[1], 128), F32)

    def lane_sums(values):
        part = values[:, :128]
        for start in range(128, values.shape[1], 128):
            part = part + values[:, start : start + 128]
        return part

    columns = []
    for head in range(heads):
        start = 0
        for out, weights, size in (
            (query, w_query, KEY_SIZE),
            (key, w_key, KEY_SIZE),
            (value, w_value, DV),
            (gating, w_gating, DV),
        ):
            place = slice(head * size, (head + 1) * size)
            part = grads[head, :, start : start + size].astype(F32)
            out[:, place] = part * scale
            total = total + lane_sums(part * weights[:, place].astype(F32))
            start += size
        columns.append(grads[head, :, LOGIT : LOGIT + 1].astype(F32))
    columns = jnp.concatenate(columns, axis=1)
    beta[...] = columns * scale
    gain_part[...] = jnp.sum(total, axis=1, keepdims=True) + jnp.sum(
        columns * w_beta[...].astype(F32), axis=1, keepdims=True
    )


def unpack_heads(grads, gain, w_query, w_key, w_value, w_gating, w_beta):
    shape = jax.ShapeDtypeStruct
    weights = (w_query, w_key, w_value, w_gating, w_beta)
    query, key, value, gating, beta, gain_part = pl.pallas_call(
        unpack_kernel,
        out_shape=tuple(shape(w.shape, F32) for w in weights) + (shape((gain.shape[0], 1), F32),),
        in_specs=[VMEM_SPEC] * 7,
        out_specs=[VMEM_SPEC] * 6,
        compiler_params=pltpu.CompilerParams(vmem_limit_bytes=32 * 1024 * 1024),
        name="unpack_heads",
    )(grads, gain, *weights)
    return query, key, value, gating, beta, gain_part[:, 0]


def pack_kernel(
    core, gain, w_query, w_key, w_value, w_gating, w_beta, w_output, rates, starts, kept, given
):
    heads = kept.shape[0]
    half = kept.shape[1]
    first = core[0] == 0
    scale = gain[...]
    lanes = lax.broadcasted_iota(jnp.int32, (2 * half, 128), 1)
    blank = jnp.zeros((half - 8, 128), F32)

    def two_rows(values):
        right = lanes[: values.shape[0]] >= half
        return jnp.where(right, pltpu.roll(values, half, 1), 0.0), jnp.where(right, values, 0.0)

    rate = rates[...]
    high = rate.astype(BF16).astype(F32)
    middle = (rate - high).astype(BF16).astype(F32)
    notes = [*two_rows(high), *two_rows(middle), *two_rows(rate - high - middle)]
    start_rows = two_rows(jnp.broadcast_to(starts[...], (8, 2 * half)))

    def place(head, columns, values):
        low, high = values[:half], values[half:]
        kept[head, :, columns] = jnp.where(first, low, high).astype(BF16)
        given[head, :, columns] = jnp.where(first, high, low).astype(BF16)

    for head in range(heads):
        start = 0
        for weights, size in ((w_query, KEY_SIZE), (w_key, KEY_SIZE), (w_value, DV), (w_gating, DV)):
            part = weights[:, head * size : (head + 1) * size].astype(F32) * scale
            place(head, slice(start, start + size), part)
            start += size
        beta = w_beta[:, head : head + 1].astype(F32) * scale
        place(
            head, slice(PACK, PACK + DV), w_output[head * DV : (head + 1) * DV, :].astype(F32).T
        )
        note = [part[head : head + 1] for part in notes] + [part[:1] for part in start_rows]
        note = jnp.concatenate(note + [blank], axis=0)
        place(
            head, slice(LOGIT, PACK), jnp.where(lanes < 2, beta, 0.0) + jnp.concatenate([note, note], axis=0)
        )


def pack_heads(core, gain, w_query, w_key, w_value, w_gating, w_beta, w_output, rates, starts):
    rows = gain.shape[0]
    heads = w_query.shape[1] // KEY_SIZE
    shape = jax.ShapeDtypeStruct((heads, rows // 2, PACK + DV), BF16)
    return pl.pallas_call(
        pack_kernel,
        out_shape=(shape, shape),
        in_specs=[SMEM_SPEC] + [VMEM_SPEC] * 9,
        out_specs=[VMEM_SPEC] * 2,
        compiler_params=pltpu.CompilerParams(vmem_limit_bytes=32 * 1024 * 1024),
        name="pack_heads",
    )(core, gain, w_query, w_key, w_value, w_gating, w_beta, w_output, rates, starts)


def join_kernel(*refs):
    *pieces, out = refs
    start = 0
    for piece in pieces:
        out[start : start + piece.shape[0]] = piece[...]
        start += piece.shape[0]


def joined_rows(pieces):
    rows, width = sum(piece.shape[0] for piece in pieces), pieces[0].shape[1]
    steps = 2

    def block(size):
        return pl.BlockSpec((size, width // steps), lambda step: (0, step))

    return pl.pallas_call(
        join_kernel,
        out_shape=jax.ShapeDtypeStruct((rows, width), pieces[0].dtype),
        grid=(steps,),
        in_specs=[block(piece.shape[0]) for piece in pieces],
        out_specs=block(rows),
        name="joined_rows",
    )(*pieces)


CHIPS = 16
CORES = 2
BOTH = ("seq", "head")


def along_x(index):
    return index ^ 1


def along_y(index):
    return index ^ 2


def along_z(steps):
    return lambda index: (index + 4 * steps) % CHIPS


def send(value, target):
    return lax.ppermute(value, "seq", [(index, target(index)) for index in range(CHIPS)])


def swap_cores(value):
    return lax.ppermute(value, "head", [(0, 1), (1, 0)])


def exchange(pieces):
    return lax.all_to_all(pieces, "seq", split_axis=0, concat_axis=0, tiled=True)


def after(values, *earlier):
    return lax.optimization_barrier((values, earlier))[0]


def stacked(values):
    return jnp.concatenate(values, axis=0)


def total_of(*values):
    total = values[0].astype(F32)
    for value in values[1:]:
        total = total + value.astype(F32)
    return total


def gather_levels(block):
    return [block] + [send(block, along_z(steps)) for steps in (1, 2, 3)]


def gather_near(levels):
    block = stacked(levels)
    return block, send(block, along_x), send(block, along_y)


def gather_far(near):
    _, from_x, from_y = near
    half = from_x.shape[0] // 2
    return near + (send(from_y[:half], along_x), send(from_x[half:], along_y))


def gather_rows(block):
    return stacked(gather_far(gather_near(gather_levels(block))))


def scatter_far(parts):
    rows = parts.shape[0] // 8
    return parts, send(parts[6 * rows : 7 * rows], along_x), send(parts[7 * rows :], along_y)


def scatter_near(begun):
    parts, low, high = begun
    rows = parts.shape[0] // 8
    for_x = stacked([parts[2 * rows : 3 * rows], total_of(parts[3 * rows : 4 * rows], high).astype(BF16)])
    for_y = stacked([total_of(parts[4 * rows : 5 * rows], low).astype(BF16), parts[5 * rows : 6 * rows]])
    return parts[: 2 * rows], send(for_x, along_x), send(for_y, along_y)


def scatter_levels(near):
    own, from_x, from_y = near
    total = total_of(own, from_x, from_y)
    rows = total.shape[0] // 4
    return [total[:rows]] + [
        send(total[j * rows : (j + 1) * rows].astype(BF16), along_z(-j)) for j in (1, 2, 3)
    ]


def nn(a, b):
    return mm(a, b)


def nt(a, b):
    return mm(a, b, NT)


def tn(a, b):
    return mm(a, b, TN)


def head_plan(
    inputs,
    doc_starts,
    decay_rate,
    mixer_gain,
    w_query,
    w_key,
    w_value,
    w_beta,
    w_gating,
    conv_query,
    conv_key,
    conv_value,
    head_gain,
    w_output,
    feed_gain,
    w_gate,
    w_up,
    w_down,
    cotangent,
):
    chip, core = lax.axis_index("seq"), lax.axis_index("head")
    first = core == 0
    tok_rows, width = inputs.shape
    half_rows = tok_rows // CORES
    row_count = w_query.shape[0]
    half_count = row_count // CORES
    head_count = w_query.shape[1] // KEY_SIZE
    units = w_gate.shape[1] // CHIPS
    own_count = CHIPS * half_rows

    def own_rows(values):
        return lax.dynamic_slice_in_dim(values, core * half_rows, half_rows, 0)

    def in_order(own, other, axis):
        return jnp.concatenate([jnp.where(first, own, other), jnp.where(first, other, own)], axis=axis)

    def split_by_core(pieces):
        kept = lax.dynamic_slice_in_dim(pieces, core * half_count, half_count, 1)
        given = lax.dynamic_slice_in_dim(pieces, (1 - core) * half_count, half_count, 1)
        return in_order(kept, swap_cores(given), 0)

    def joined_by_core(mine):
        both = in_order(mine[:, None], swap_cores(mine)[:, None], 1)
        return both.reshape(width, mine.shape[-1])

    inputs_own = own_rows(inputs).astype(F32)
    scale_one = lax.rsqrt(jnp.mean(inputs_own * inputs_own, axis=-1, keepdims=True) + EPSILON)
    normed_one = inputs_own * scale_one
    gain_one = mixer_gain.astype(F32)[:, None]
    gain_two = feed_gain.astype(F32)[:, None]

    in_kept, in_given = pack_heads(
        core.astype(jnp.int32)[None],
        gain_one,
        w_query,
        w_key,
        w_value,
        w_gating,
        w_beta,
        w_output,
        decay_rate.T,
        doc_starts.astype(F32)[None],
    )
    in_payload = in_order(in_kept, swap_cores(in_given), 0)
    one_levels = gather_levels(normed_one.astype(BF16))
    in_mine = exchange(after(in_payload, one_levels))
    one_near = gather_near(one_levels)
    in_mine = after(in_mine, one_near)
    normed_all = stacked(gather_far(one_near))
    weights_all = joined_by_core(in_mine)
    weights_in, weights_out = weights_all[:, :PACK], weights_all[:, PACK:]

    taps_here = jnp.concatenate(
        [
            conv_query.reshape(CONV, head_count, KEY_SIZE),
            conv_key.reshape(CONV, head_count, KEY_SIZE),
            conv_value.reshape(CONV, head_count, DV),
        ],
        axis=2,
    ).transpose(1, 0, 2)
    taps_there = swap_cores(taps_here)
    taps = lax.dynamic_index_in_dim(
        jnp.where(chip // head_count == core, taps_here, taps_there), chip % head_count, 0, False
    ).astype(F32)
    taps = stacked([taps, jnp.zeros_like(taps)])
    gain_head = jnp.broadcast_to(head_gain.astype(F32)[None], (8, DV))
    seen = in_mine[:, :8, PACK - tok_rows // 2 : PACK].astype(F32).reshape(CHIPS, 4, tok_rows)
    rate = (seen[:, 0] + seen[:, 1] + seen[:, 2]).reshape(-1)
    starts = seen[:, 3].reshape(-1)
    decay_grid, cols, rows = stream_tables(rate, starts)

    blocks = jnp.arange(CHIPS * CORES)
    far = blocks // CORES
    place = (
        4 * ((far ^ chip) % 4) + (chip // 4 - far // 4) % 4 + CHIPS * (blocks % CORES != core)
    ).astype(jnp.int32)

    raw = nn(normed_all, weights_in)
    column = lax.broadcasted_iota(jnp.int32, raw.shape, 1)
    pre_own = jnp.where(
        column == LOGIT + 1,
        raw - lax.reduce_precision(raw, exponent_bits=8, mantissa_bits=7),
        raw,
    ).astype(BF16)
    pre = (pre_own, swap_cores(pre_own))

    feed = jnp.concatenate(
        [
            (w_gate.astype(F32) * gain_two).astype(BF16).T.reshape(CHIPS, units, row_count),
            (w_up.astype(F32) * gain_two).astype(BF16).T.reshape(CHIPS, units, row_count),
            w_down.reshape(CHIPS, units, row_count),
        ],
        axis=1,
    )
    feed = after(feed, in_mine)
    feed_mine = exchange(feed)
    gated_own, gated_other, *kept = mixer_forward(place, *pre, decay_grid, cols, rows, taps, gain_head)
    mixed_parts = nt(gated_own, weights_out).astype(BF16)
    mixed = scatter_far(mixed_parts)

    cot_own = own_rows(cotangent)
    mixed, cot, feed_mine = after((mixed, cot_own, feed_mine))
    mixed, cot = scatter_near(mixed), gather_levels(cot)
    feed_other = swap_cores(feed_mine)
    mixed, cot, normed_late = after((mixed, cot, normed_all))
    mixed, cot = scatter_levels(mixed), gather_near(cot)

    def unit_rows(position):
        return stacked(
            [
                part[:, position * units : (position + 1) * units].transpose(1, 0, 2).reshape(units, width)
                for part in (feed_mine, feed_other)
            ]
        )

    gate_rows, up_rows, down_rows = unit_rows(0), unit_rows(1), unit_rows(2)
    cut = normed_late.reshape(own_count, CHIPS, CORES, half_count)
    cut_mine = lax.dynamic_index_in_dim(cut, core, 2, False).reshape(own_count, width // CORES)
    cut_given = lax.dynamic_index_in_dim(cut, 1 - core, 2, False).reshape(own_count, width // CORES)
    cut_other = swap_cores(cut_given)

    mixed, cot = after((mixed, cot))
    middle = inputs_own + total_of(*mixed)
    scale_two = lax.rsqrt(jnp.mean(middle * middle, axis=-1, keepdims=True) + EPSILON)
    normed_mid = middle * scale_two
    mid, cot = gather_levels(normed_mid.astype(BF16)), gather_far(cot)
    mid, cot, gate_rows, up_rows, down_rows, cut_mine, cut_other = after(
        (mid, cot, gate_rows, up_rows, down_rows, cut_mine, cut_other)
    )
    mid = gather_near(mid)
    cot_all = stacked(cot)
    d_hidden = nt(cot_all, down_rows).astype(BF16)
    mid, d_hidden = after((mid, d_hidden))
    mid_all = stacked(gather_far(mid))

    gate_lin = nt(mid_all, gate_rows)
    up_lin = nt(mid_all, up_rows)
    d_hidden = d_hidden.astype(F32)
    sig = jax.nn.sigmoid(gate_lin)
    act = gate_lin * sig
    hidden = (act * up_lin).astype(BF16)
    d_gate = (d_hidden * up_lin * (sig * (1.0 + gate_lin * (1.0 - sig)))).astype(BF16)
    d_up = (d_hidden * act).astype(BF16)
    e_mid = scatter_far((nn(d_gate, gate_rows) + nn(d_up, up_rows)).astype(BF16))
    feed_parts = nn(after(hidden, e_mid[0]), down_rows).astype(BF16)
    e_mid, feed_parts = after((e_mid, feed_parts))
    e_mid = scatter_near(e_mid)

    parts = [tn(d_gate, mid_all), tn(d_up, mid_all), tn(hidden, cot_all)]
    keep_part = stacked([part[:units] for part in parts])
    give_part = stacked([part[units:] for part in parts]).astype(BF16)
    e_mid, feed_out, keep_part, give_part = after((e_mid, feed_parts, keep_part, give_part))
    e_mid, feed_out = scatter_levels(e_mid), scatter_far(feed_out)
    e_mid, feed_out = after((e_mid, feed_out))
    e_two = total_of(*e_mid)
    d_middle = cot_own.astype(F32) + scale_two * (
        e_two - normed_mid * jnp.mean(e_two * normed_mid, axis=-1, keepdims=True)
    )
    d_mid, feed_out = gather_levels(d_middle.astype(BF16)), scatter_near(feed_out)
    feed_grad = (keep_part + swap_cores(give_part).astype(F32)).astype(BF16)
    feed_grad = feed_grad.reshape(3 * units, CHIPS, row_count).transpose(1, 0, 2)
    feed_grad = jnp.pad(feed_grad, ((0, 0), (0, half_count * DV // row_count), (0, 0)))
    d_mid, feed_out, feed_grad = after((d_mid, feed_out, feed_grad))
    d_mid, feed_out = gather_near(d_mid), scatter_levels(feed_out)
    d_mid, feed_out = after((d_mid, feed_out))
    d_mid_all = stacked(gather_far(d_mid))

    d_gated_own = nn(d_mid_all, weights_out).astype(BF16)
    d_gated = (d_gated_own, swap_cores(d_gated_own))
    grad_out = tn(d_mid_all, gated_own).astype(BF16).reshape(CHIPS, CORES, half_count, DV)
    grad_out = total_of(
        lax.dynamic_index_in_dim(grad_out, core, 1, False),
        swap_cores(lax.dynamic_index_in_dim(grad_out, 1 - core, 1, False)),
    ).astype(BF16)
    feed_grad = lax.dynamic_update_slice(
        feed_grad, grad_out.reshape(CHIPS, half_count * DV // row_count, row_count), (0, 3 * units, 0)
    )
    feed_back = exchange(feed_grad)
    d_pre_own, d_pre_other, grad_taps, grad_gain = mixer_backward(
        place, d_gated, pre, decay_grid, cols, taps, gain_head, kept
    )


    small = jnp.concatenate([jnp.sum(grad_taps, axis=1).reshape(-1), jnp.sum(grad_gain, axis=0)])
    small = small.reshape(-1, 64)
    small_rows = small.shape[0]
    grad_in = tn(cut_mine, d_pre_own) + tn(cut_other, d_pre_other)
    small = jnp.pad(small, ((0, half_count - small_rows), (PACK - 64, 0)))
    grad_in = (grad_in.reshape(CHIPS, half_count, PACK) + small).astype(BF16)
    grad_in, feed_back = after((grad_in, feed_back))
    e_parts = nt(after(d_pre_own, grad_in), weights_in).astype(BF16)
    grad_in = exchange(grad_in)
    e_sums = scatter_near(scatter_far(e_parts))
    e_sums, grad_in, feed_back = after((e_sums, grad_in, feed_back))
    small = grad_in[:, :small_rows, PACK - 64 :].astype(F32).reshape(CHIPS, -1)
    taps_all = lax.dynamic_slice_in_dim(small[:, : CONV * MIXED], core * head_count, head_count, 0)
    taps_all = taps_all.reshape(head_count, CONV, MIXED).transpose(1, 0, 2)

    def heads_here(back):
        mine = lax.dynamic_slice_in_dim(back, core * head_count, head_count, 0)
        given = lax.dynamic_slice_in_dim(back, (1 - core) * head_count, head_count, 0)
        return in_order(mine, swap_cores(given), 1)

    grad_in = heads_here(grad_in)
    block_out_own = (middle + total_of(*feed_out)).astype(BF16)
    block_out = in_order(block_out_own, swap_cores(block_out_own), 0)
    e_levels = scatter_levels(e_sums)

    grad_out = heads_here(feed_back[:, 3 * units :].reshape(CHIPS, half_count, DV))
    grad_output = grad_out.astype(F32).transpose(0, 2, 1).reshape(head_count * DV, row_count)
    feed_back = feed_back[:, : 3 * units].astype(F32)
    raw_gate = feed_back[:, :units].reshape(CHIPS * units, row_count).T
    raw_up = feed_back[:, units : 2 * units].reshape(CHIPS * units, row_count).T
    grad_down = feed_back[:, 2 * units :].reshape(CHIPS * units, row_count)
    feed_gain_part = jnp.sum(raw_gate * w_gate.astype(F32) + raw_up * w_up.astype(F32), axis=1)

    raw_query, raw_key, raw_value, raw_gating, raw_beta, mixer_gain_part = unpack_heads(
        grad_in, gain_one, w_query, w_key, w_value, w_gating, w_beta
    )
    gain_parts = jnp.stack([mixer_gain_part, feed_gain_part])
    gain_totals = gain_parts + swap_cores(gain_parts)

    others = (
        gain_totals[0],
        raw_query,
        raw_key,
        raw_value,
        raw_beta,
        raw_gating,
        taps_all[:, :, :KEY_SIZE].reshape(CONV, head_count * KEY_SIZE),
        taps_all[:, :, KEY_SIZE : 2 * KEY_SIZE].reshape(CONV, head_count * KEY_SIZE),
        taps_all[:, :, 2 * KEY_SIZE :].reshape(CONV, head_count * DV),
        jnp.sum(small[:, CONV * MIXED :], axis=0),
        grad_output,
        gain_totals[1],
        raw_gate * gain_two,
        raw_up * gain_two,
        grad_down,
    )
    e_levels, block_out, others = after((e_levels, block_out, others))
    e_one = total_of(*e_levels)
    grad_own = d_middle + scale_one * (
        e_one - normed_one * jnp.mean(e_one * normed_one, axis=-1, keepdims=True)
    )
    grad_inputs = in_order(grad_own, swap_cores(grad_own), 0)
    return (block_out, grad_inputs) + others


EXACT_PRECISION = lax.Precision.HIGHEST


def passed_along(value, axis, steps):
    count = lax.axis_size(axis)
    first, last = (max(0, -steps), min(count, count - steps))
    return lax.ppermute(value, axis, [(source, source + steps) for source in range(first, last)])


def entering(value, axis, join, neutral):
    count, mine = (lax.axis_size(axis), lax.axis_index(axis))
    pieces = jax.tree.map(lambda part: lax.all_gather(part, axis), value)
    subtotal = jax.tree.map(
        lambda part, zero: jnp.full_like(part, 0) + jnp.asarray(zero, part.dtype), value, neutral
    )

    def lap(position, subtotal):
        longer = join(subtotal, jax.tree.map(lambda part: part[position], pieces))
        return jax.tree.map(lambda new, old: jnp.where(position < mine, new, old), longer, subtotal)

    return lax.fori_loop(0, count - 1, lap, subtotal)


def carried_in(shard, axis, join, neutral):
    count = lax.axis_size(axis)
    place = lax.axis_index(axis)
    ahead = count - 1 - place
    gathered = jax.tree.map(
        lambda a, kind: lax.all_gather(a.astype(kind), axis),
        shard,
        jax.tree.map(lambda a: jnp.bfloat16 if a.dtype == jnp.float32 else a.dtype, shard),
    )
    state = jax.tree.map(lambda a, e: jnp.zeros_like(a) + jnp.asarray(e, a.dtype), shard, neutral)

    def one(lap, state):
        source = count - 1 - lap
        return join(
            state,
            jax.tree.map(
                lambda a, own: lax.dynamic_index_in_dim(a, source, 0, False).astype(own.dtype),
                gathered,
                shard,
            ),
        )

    return lax.fori_loop(0, ahead, one, state)


def high_einsum(einsum_form, *arrays):
    return jnp.einsum(
        einsum_form, *arrays, precision=EXACT_PRECISION, preferred_element_type=jnp.float32
    )


def low_dot(left_side, right_side):
    return jnp.dot(left_side, right_side, preferred_element_type=jnp.float32)


def inner_dot(left_side, right_side):
    return lax.dot_general(
        left_side, right_side, (((0,), (0,)), ((), ())), preferred_element_type=jnp.float32
    )


def outer_dot(left_side, right_side):
    return lax.dot_general(
        left_side, right_side, (((1,), (1,)), ((), ())), preferred_element_type=jnp.float32
    )


def rounded(values):
    return lax.optimization_barrier(values.astype(jnp.bfloat16)).astype(jnp.float32)


def scale_norm(values, gain_vec):
    return (
        values * lax.rsqrt(jnp.mean(values * values, axis=-1, keepdims=True) + EPSILON) * gain_vec
    )


def unit_rows(values):
    return values * lax.rsqrt(jnp.sum(values * values, axis=-1, keepdims=True) + EPSILON)


def swiglu(gate_lin, up_lin):
    return jax.nn.silu(gate_lin) * up_lin


def compose_maps(earlier_map, later_map):
    return (
        high_einsum("hde,hef->hdf", later_map[0], earlier_map[0]),
        high_einsum("hde,hef->hdf", later_map[0], earlier_map[1]) + later_map[1],
    )


def gather_plan(
    inputs,
    doc_starts,
    decay_rate,
    mixer_gain,
    w_query,
    w_key,
    w_value,
    w_beta,
    w_gating,
    conv_query,
    conv_key,
    conv_value,
    head_gain,
    w_output,
    feed_gain,
    w_gate,
    w_up,
    w_down,
    cotangent,
):
    tok_rows = inputs.shape[0]
    head_count = decay_rate.shape[1]
    key_width = w_query.shape[1]
    value_width = w_value.shape[1]
    edge_count = CONV - 1
    block_count = tok_rows // BLOCK
    gathered = (
        lax.all_gather(mixer_gain, "seq", axis=0, tiled=True),
        lax.all_gather(w_query, "seq", axis=0, tiled=True),
        lax.all_gather(w_key, "seq", axis=0, tiled=True),
        lax.all_gather(w_value, "seq", axis=0, tiled=True),
        lax.all_gather(w_beta, "seq", axis=0, tiled=True),
        lax.all_gather(w_gating, "seq", axis=0, tiled=True),
        lax.all_gather(w_output, "seq", axis=1, tiled=True),
        lax.all_gather(feed_gain, "seq", axis=0, tiled=True),
        lax.all_gather(w_gate, "seq", axis=0, tiled=True),
        lax.all_gather(w_up, "seq", axis=0, tiled=True),
        lax.all_gather(w_down, "seq", axis=1, tiled=True),
    )
    (
        gain_one,
        full_query,
        full_key,
        full_value,
        full_beta,
        full_gating,
        full_output,
        gain_two,
        full_gate,
        full_up,
        full_down,
    ) = gathered
    inputs_float = inputs.astype(jnp.float32)
    normed_float, norm_one_back = jax.vjp(scale_norm, inputs_float, gain_one.astype(jnp.float32))
    normed_one = normed_float.astype(jnp.bfloat16)
    query_pre = low_dot(normed_one, full_query).astype(jnp.bfloat16)
    key_pre = low_dot(normed_one, full_key).astype(jnp.bfloat16)
    value_pre = low_dot(normed_one, full_value).astype(jnp.bfloat16)
    gating_pre = low_dot(normed_one, full_gating).astype(jnp.bfloat16)
    beta_logit = low_dot(normed_one, full_beta)
    joined = jnp.concatenate([query_pre, key_pre, value_pre], axis=1)
    tail_starts = doc_starts[tok_rows - edge_count :]
    later_starts = jnp.cumsum(tail_starts[::-1])[::-1] - tail_starts
    sender_keep = (later_starts == 0).astype(jnp.bfloat16)[:, None]
    edge_in = passed_along(joined[tok_rows - edge_count :] * sender_keep, "seq", 1)
    local_doc = jnp.cumsum(doc_starts)
    padded_doc = jnp.concatenate([jnp.zeros((edge_count,), local_doc.dtype), local_doc])
    keep_masks = [
        (
            padded_doc[edge_count - shift_lag : edge_count - shift_lag + tok_rows] == local_doc
        ).astype(jnp.float32)[:, None]
        for shift_lag in range(CONV)
    ]

    def conv_piece(extended, conv_weights):
        mixed = keep_masks[0] * conv_weights[0] * extended[edge_count:]
        for shift_lag in range(1, CONV):
            mixed = (
                mixed
                + keep_masks[shift_lag]
                * conv_weights[shift_lag]
                * extended[edge_count - shift_lag : edge_count - shift_lag + tok_rows]
            )
        activated = jax.nn.silu(mixed)
        query_unit = unit_rows(activated[:, :key_width].reshape(tok_rows, head_count, KEY_SIZE))
        key_unit = unit_rows(
            activated[:, key_width : 2 * key_width].reshape(tok_rows, head_count, KEY_SIZE)
        )
        value_act = activated[:, 2 * key_width :].reshape(tok_rows, head_count, DV)
        return (query_unit, key_unit, value_act)

    extended = jnp.concatenate([edge_in, joined], axis=0).astype(jnp.float32)
    conv_weights = jnp.concatenate([conv_query, conv_key, conv_value], axis=1).astype(jnp.float32)
    (query_unit, key_unit, value_act), conv_back = jax.vjp(conv_piece, extended, conv_weights)

    def to_blocks(values):
        return values.reshape(block_count, BLOCK, head_count, values.shape[-1]).transpose(
            0, 2, 1, 3
        )

    def from_blocks(values):
        return values.transpose(0, 2, 1, 3).reshape(tok_rows, head_count, values.shape[-1])

    log_rate = jnp.log(decay_rate).reshape(block_count, BLOCK, head_count).transpose(0, 2, 1)
    log_level = jnp.cumsum(log_rate, axis=-1)
    segment = jnp.cumsum(doc_starts.reshape(block_count, BLOCK), axis=-1)
    positions = jnp.arange(BLOCK)
    causal = positions[:, None] >= positions[None, :]
    strict = positions[:, None] > positions[None, :]
    linked = (segment[:, None, :, None] == segment[:, None, None, :]) & causal
    spread = jnp.where(causal, log_level[..., :, None] - log_level[..., None, :], 0.0)
    decay_grid = jnp.where(linked, jnp.exp(spread), 0.0)
    carry_in = jnp.where(segment[:, None, :] == 0, jnp.exp(log_level), 0.0)
    tail_decay = decay_grid[..., BLOCK - 1, :]
    key_eye = jnp.eye(KEY_SIZE, dtype=jnp.float32)
    block_eye = jnp.eye(BLOCK, dtype=jnp.float32)

    def block_terms(query_blocks, key_blocks, value_blocks, logit_blocks):
        beta_gate = jax.nn.sigmoid(logit_blocks)
        key_gram = high_einsum("nhcd,nhmd->nhcm", key_blocks, key_blocks)
        system = block_eye + jnp.where(strict, decay_grid * key_gram * beta_gate[..., None, :], 0.0)
        right_side = jnp.concatenate([value_blocks, carry_in[..., None] * key_blocks], axis=-1)
        solved = jax.scipy.linalg.solve_triangular(
            system, right_side, lower=True, unit_diagonal=True
        )
        fresh_values = solved[..., :DV]
        fresh_keys = solved[..., DV:]
        mixing = (
            high_einsum("nhcd,nhmd->nhcm", query_blocks, key_blocks)
            * decay_grid
            * beta_gate[..., None, :]
        )
        weighted = key_blocks * (tail_decay * beta_gate)[..., None]
        block_maps = carry_in[..., BLOCK - 1, None, None] * key_eye - high_einsum(
            "nhcd,nhce->nhde", weighted, fresh_keys
        )
        block_adds = high_einsum("nhcd,nhce->nhde", weighted, fresh_values)

        def chain_step(current, element):
            return (compose_maps(current, element), None)

        start_map = (
            jnp.broadcast_to(key_eye, (head_count, KEY_SIZE, KEY_SIZE)),
            jnp.zeros((head_count, KEY_SIZE, DV), jnp.float32),
        )
        device_pair, _ = lax.scan(chain_step, start_map, (block_maps, block_adds))
        return (
            (fresh_values, fresh_keys, mixing, block_maps, block_adds),
            device_pair[0],
            device_pair[1],
        )

    def block_outputs(block_parts, query_blocks, start_state):

        def step_block(current, element):
            fresh_values, fresh_keys, mixing, block_map, block_add, query_part, carry_part = element
            updated = fresh_values - high_einsum("hcd,hde->hce", fresh_keys, current)
            produced_output = (
                carry_part[..., None] * high_einsum("hcd,hde->hce", query_part, current)
                + high_einsum("hcm,hme->hce", mixing, updated)
            ) * KEY_SIZE ** (-0.5)
            return (high_einsum("hde,hef->hdf", block_map, current) + block_add, produced_output)

        _, emitted_all = lax.scan(step_block, start_state, block_parts + (query_blocks, carry_in))
        return emitted_all

    query_blocks = to_blocks(rounded(query_unit))
    key_blocks = to_blocks(rounded(key_unit))
    value_blocks = to_blocks(rounded(value_act))
    logit_blocks = beta_logit.reshape(block_count, BLOCK, head_count).transpose(0, 2, 1)
    (block_parts, device_map, device_add), terms_back = jax.vjp(
        block_terms, query_blocks, key_blocks, value_blocks, logit_blocks
    )
    identity = (jnp.broadcast_to(key_eye, device_map.shape), jnp.zeros_like(device_add))
    prefix = entering((device_map, device_add), "seq", compose_maps, identity)
    start_state = prefix[1]
    produced_output, emitted_back = jax.vjp(block_outputs, block_parts, query_blocks, start_state)

    def gated_norm(values, gating_values, gain_vec):
        normed_out = values * lax.rsqrt(jnp.mean(values * values, axis=-1, keepdims=True) + EPSILON)
        return (normed_out * gain_vec * jax.nn.silu(gating_values)).reshape(tok_rows, value_width)

    mixer_out = from_blocks(produced_output)
    gated_float, gated_back = jax.vjp(
        gated_norm,
        mixer_out,
        gating_pre.astype(jnp.float32).reshape(tok_rows, head_count, DV),
        head_gain.astype(jnp.float32),
    )
    gated_out = gated_float.astype(jnp.bfloat16)
    middle = inputs_float + lax.psum(
        low_dot(gated_out, full_output).astype(jnp.bfloat16), "head"
    ).astype(jnp.float32)
    normed_middle, norm_two_back = jax.vjp(scale_norm, middle, gain_two.astype(jnp.float32))
    normed_two = normed_middle.astype(jnp.bfloat16)
    gate_lin = low_dot(normed_two, full_gate)
    up_lin = low_dot(normed_two, full_up)
    hidden_float, swiglu_back = jax.vjp(swiglu, gate_lin, up_lin)
    hidden = hidden_float.astype(jnp.bfloat16)
    feed_out = lax.psum(low_dot(hidden, full_down).astype(jnp.bfloat16), "head").astype(jnp.float32)
    block_out = (middle + feed_out).astype(jnp.bfloat16)
    regathered = (
        lax.all_gather(w_query, "seq", axis=0, tiled=True),
        lax.all_gather(w_key, "seq", axis=0, tiled=True),
        lax.all_gather(w_value, "seq", axis=0, tiled=True),
        lax.all_gather(w_beta, "seq", axis=0, tiled=True),
        lax.all_gather(w_gating, "seq", axis=0, tiled=True),
        lax.all_gather(w_output, "seq", axis=1, tiled=True),
        lax.all_gather(w_gate, "seq", axis=0, tiled=True),
        lax.all_gather(w_up, "seq", axis=0, tiled=True),
        lax.all_gather(w_down, "seq", axis=1, tiled=True),
    )
    (
        full_query,
        full_key,
        full_value,
        full_beta,
        full_gating,
        full_output,
        full_gate,
        full_up,
        full_down,
    ) = regathered
    cotangent_float = cotangent.astype(jnp.float32)
    grad_down = inner_dot(hidden, cotangent)
    d_hidden = rounded(outer_dot(cotangent, full_down))
    d_gate_float, d_up_float = swiglu_back(d_hidden)
    d_gate = d_gate_float.astype(jnp.bfloat16)
    d_up = d_up_float.astype(jnp.bfloat16)
    grad_gate = inner_dot(normed_two, d_gate)
    grad_up = inner_dot(normed_two, d_up)
    d_normed_two = lax.psum(
        (outer_dot(d_gate, full_gate) + outer_dot(d_up, full_up)).astype(jnp.bfloat16), "head"
    ).astype(jnp.float32)
    d_middle_norm, grad_gain_two = norm_two_back(d_normed_two)
    d_middle = cotangent_float + d_middle_norm
    d_middle_low = d_middle.astype(jnp.bfloat16)
    grad_output = inner_dot(gated_out, d_middle_low)
    d_gated = rounded(outer_dot(d_middle_low, full_output))
    d_mixer_out, d_gating_float, grad_head_part = gated_back(d_gated)
    d_gating = d_gating_float.reshape(tok_rows, value_width).astype(jnp.bfloat16)
    d_parts, d_query_late, d_start = emitted_back(to_blocks(d_mixer_out))
    chained = carried_in((jnp.swapaxes(device_map, 1, 2), d_start), "seq", compose_maps, identity)
    d_end = chained[1]
    d_map = high_einsum("hde,hfe->hdf", d_end, start_state)
    d_query_early, d_key_blocks, d_value_blocks, d_logit_blocks = terms_back(
        (d_parts, d_map, d_end)
    )
    d_query_unit = rounded(from_blocks(d_query_early + d_query_late))
    d_key_unit = rounded(from_blocks(d_key_blocks))
    d_value_act = rounded(from_blocks(d_value_blocks))
    d_beta_logit = (
        d_logit_blocks.transpose(0, 2, 1).reshape(tok_rows, head_count).astype(jnp.bfloat16)
    )
    d_extended, grad_conv_all = conv_back((d_query_unit, d_key_unit, d_value_act))
    returned = passed_along(d_extended[:edge_count].astype(jnp.bfloat16), "seq", -1).astype(
        jnp.float32
    )
    d_rows = d_extended[edge_count:]
    d_rows = jnp.concatenate(
        [
            d_rows[: tok_rows - edge_count],
            d_rows[tok_rows - edge_count :] + returned * sender_keep.astype(jnp.float32),
        ],
        axis=0,
    )
    d_joined = d_rows.astype(jnp.bfloat16)
    d_query_pre = d_joined[:, :key_width]
    d_key_pre = d_joined[:, key_width : 2 * key_width]
    d_value_pre = d_joined[:, 2 * key_width :]
    grad_query = inner_dot(normed_one, d_query_pre)
    grad_key = inner_dot(normed_one, d_key_pre)
    grad_value = inner_dot(normed_one, d_value_pre)
    grad_gating = inner_dot(normed_one, d_gating)
    grad_beta = inner_dot(normed_one, d_beta_logit)
    d_normed_part = (
        outer_dot(d_query_pre, full_query)
        + outer_dot(d_key_pre, full_key)
        + outer_dot(d_value_pre, full_value)
        + outer_dot(d_gating, full_gating)
        + outer_dot(d_beta_logit, full_beta)
    )
    d_normed_one, head_total = (
        lax.psum(d_normed_part.astype(jnp.bfloat16), "head").astype(jnp.float32),
        lax.psum(grad_head_part.astype(jnp.bfloat16), "head").astype(jnp.float32),
    )
    d_inputs_norm, grad_gain_one = norm_one_back(d_normed_one)
    grad_inputs = d_middle + d_inputs_norm
    small_totals = lax.psum((grad_conv_all, head_total), "seq")
    conv_total = small_totals[0]
    totals = (
        lax.psum_scatter(grad_gain_one, "seq", scatter_dimension=0, tiled=True),
        lax.psum_scatter(grad_query, "seq", scatter_dimension=0, tiled=True),
        lax.psum_scatter(grad_key, "seq", scatter_dimension=0, tiled=True),
        lax.psum_scatter(grad_value, "seq", scatter_dimension=0, tiled=True),
        lax.psum_scatter(grad_beta, "seq", scatter_dimension=0, tiled=True),
        lax.psum_scatter(grad_gating, "seq", scatter_dimension=0, tiled=True),
        lax.psum_scatter(grad_output, "seq", scatter_dimension=1, tiled=True),
        lax.psum_scatter(grad_gain_two, "seq", scatter_dimension=0, tiled=True),
        lax.psum_scatter(grad_gate, "seq", scatter_dimension=0, tiled=True),
        lax.psum_scatter(grad_up, "seq", scatter_dimension=0, tiled=True),
        lax.psum_scatter(grad_down, "seq", scatter_dimension=1, tiled=True),
    )
    return (
        block_out,
        grad_inputs,
        totals[0],
        totals[1],
        totals[2],
        totals[3],
        totals[4],
        totals[5],
        conv_total[:, :key_width],
        conv_total[:, key_width : 2 * key_width],
        conv_total[:, 2 * key_width :],
        small_totals[1],
        totals[6],
        totals[7],
        totals[8],
        totals[9],
        totals[10],
    )


def solution(mesh):
    in_specs = (
        P("seq", None),
        P("seq"),
        P("seq", "head"),
        P("seq"),
        P("seq", "head"),
        P("seq", "head"),
        P("seq", "head"),
        P("seq", "head"),
        P("seq", "head"),
        P(None, "head"),
        P(None, "head"),
        P(None, "head"),
        P(),
        P("head", "seq"),
        P("seq"),
        P("seq", "head"),
        P("seq", "head"),
        P("head", "seq"),
        P("seq", None),
    )
    out_specs = (
        P("seq", None),
        P("seq", None),
        P("seq"),
        P("seq", "head"),
        P("seq", "head"),
        P("seq", "head"),
        P("seq", "head"),
        P("seq", "head"),
        P(None, "head"),
        P(None, "head"),
        P(None, "head"),
        P(),
        P("head", "seq"),
        P("seq"),
        P("seq", "head"),
        P("seq", "head"),
        P("head", "seq"),
    )
    whole_heads = mesh.shape["seq"] == CHIPS and mesh.shape["head"] == CORES
    per_device = head_plan if whole_heads else gather_plan
    return jax.shard_map(
        per_device, mesh=mesh, in_specs=in_specs, out_specs=out_specs, check_vma=False
    )
```

```python
import jax
import jax.numpy as jnp
from jax import lax
from jax.sharding import PartitionSpec as P
from jax.experimental import pallas as pl
from jax.experimental.pallas import tpu as pltpu

KEY_SIZE = 128
DV = 256
CONV = 4
BLOCK = 64
EPSILON = 1e-06
F32 = jnp.float32
BF16 = jnp.bfloat16
LOGIT = 2 * KEY_SIZE + 2 * DV
PACK = LOGIT + 128
MIXED = 2 * KEY_SIZE + DV
SCALE = KEY_SIZE**-0.5
UNROLL = 16


def mm(a, b, dims=((1,), (0,))):
    return lax.dot_general(a, b, (dims, ((), ())), preferred_element_type=F32)


NT = ((1,), (1,))
TN = ((0,), (0,))


def halves(a):
    high = a.astype(BF16)
    return high, (a - high.astype(F32)).astype(BF16)


def mm_left(a, b, dims=((1,), (0,))):
    high, low = halves(a)
    return mm(high, b, dims) + mm(low, b, dims)


def mm_right(a, b, dims=((1,), (0,))):
    high, low = halves(b)
    return mm(a, high, dims) + mm(a, low, dims)


def mm_both(a, b, dims=((1,), (0,))):
    a_high, a_low = halves(a)
    b_high, b_low = halves(b)
    return mm(a_high, b_high, dims) + (mm(a_high, b_low, dims) + mm(a_low, b_high, dims))


def block_masks():
    row = lax.broadcasted_iota(jnp.int32, (BLOCK, BLOCK), 0)
    col = lax.broadcasted_iota(jnp.int32, (BLOCK, BLOCK), 1)
    strict = row > col
    levels = []
    size = 1
    while size < BLOCK:
        levels.append(
            (row // (2 * size) == col // (2 * size)) & (row // size % 2 == 1) & (col // size % 2 == 0)
        )
        size *= 2
    return strict, levels, (row == col).astype(F32)


def unit_lower_inverses(systems, levels, eye):
    inverses = [eye - jnp.where(levels[0], system, 0.0) for system in systems]
    for level in levels[1:]:
        inner = [
            mm_both(jnp.where(level, system, 0.0), inverse)
            for system, inverse in zip(systems, inverses)
        ]
        inverses = [
            inverse - mm_both(inverse, part) for inverse, part in zip(inverses, inner)
        ]
    return inverses


def rows_of(index):
    return pl.ds(pl.multiple_of(index * BLOCK, BLOCK), BLOCK)


def row_sums(values):
    return jnp.sum(values.reshape(values.shape[0] // 8, 8, values.shape[1]), axis=0)


def beta_columns(packed):
    logit = packed[:, :1].astype(F32) + packed[:, 1:2].astype(F32)
    beta = jax.nn.sigmoid(logit)
    return beta, jnp.broadcast_to(beta, (BLOCK, 128)).T[:BLOCK]


def units_of(mixed):
    gate = jax.nn.sigmoid(mixed)
    act = mixed * gate
    query, key = act[:, :KEY_SIZE], act[:, KEY_SIZE : 2 * KEY_SIZE]
    query_scale = lax.rsqrt(jnp.sum(query * query, axis=-1, keepdims=True) + EPSILON)
    key_scale = lax.rsqrt(jnp.sum(key * key, axis=-1, keepdims=True) + EPSILON)
    return gate, act, query * query_scale, key * key_scale, query_scale, key_scale


def forward_kernel(
    place,
    pre_own,
    pre_other,
    decay_grid,
    cols,
    rows,
    taps,
    head_gain,
    gated_own,
    gated_other,
    mixer_to,
    mixed_to,
    inverse_to,
    state_to,
    fresh_to,
    carry_to,
    read_to,
    mixer_out,
    mixed_out,
    inverse_out,
    state_out,
    fresh_out,
    carry_out,
    read_out,
    both_maps,
    value_part,
    out_part,
    add_part,
    pre,
    gated,
    marks,
):
    blocks = decay_grid.shape[0]
    half = pre_own.shape[0]
    loads = [
        pltpu.make_async_copy(pre_own, pre.at[:half], marks.at[0]),
        pltpu.make_async_copy(pre_other, pre.at[half:], marks.at[1]),
    ]
    prepared = [
        pltpu.make_async_copy(mixed_out, mixed_to, marks.at[2]),
        pltpu.make_async_copy(inverse_out, inverse_to, marks.at[3]),
        pltpu.make_async_copy(carry_out, carry_to, marks.at[4]),
        pltpu.make_async_copy(read_out, read_to, marks.at[5]),
    ]
    chained = [pltpu.make_async_copy(state_out, state_to, marks.at[6])]
    finished = [
        pltpu.make_async_copy(gated.at[:half], gated_own, marks.at[7]),
        pltpu.make_async_copy(gated.at[half:], gated_other, marks.at[8]),
        pltpu.make_async_copy(mixer_out, mixer_to, marks.at[9]),
        pltpu.make_async_copy(fresh_out, fresh_to, marks.at[10]),
    ]
    for copy in loads:
        copy.start()
    for copy in loads:
        copy.wait()
    strict, levels, eye = block_masks()
    key_eye = (
        lax.broadcasted_iota(jnp.int32, (KEY_SIZE, KEY_SIZE), 0)
        == lax.broadcasted_iota(jnp.int32, (KEY_SIZE, KEY_SIZE), 1)
    ).astype(F32)

    def prepare(group, _):
        work = []
        for lane in range(UNROLL):
            b = group * UNROLL + lane
            here = rows_of(b)
            source = place[b]
            before = place[jnp.maximum(b - 1, 0)]
            current = pre[rows_of(source), :MIXED].astype(F32)
            edge = pre[
                pl.ds(pl.multiple_of(before * BLOCK + BLOCK - 16, 16), 16), :MIXED
            ].astype(F32)
            extended = jnp.concatenate([edge[8:], current], axis=0)
            mixed = taps[0:1] * current
            for lag in range(1, CONV):
                mixed = mixed + (taps[lag : lag + 1] * cols[here, 1 + lag : 2 + lag]) * pltpu.roll(
                    extended, lag, 0
                )[8:]
            mixed_out[here, :] = mixed
            _, act, query, key, _, _ = units_of(mixed)
            query, key, value = query.astype(BF16), key.astype(BF16), act[:, 2 * KEY_SIZE :].astype(BF16)
            beta, beta_row = beta_columns(pre[rows_of(source), LOGIT:])
            link = decay_grid[b] * beta_row
            system = jnp.where(strict, link * mm(key, key, NT), 0.0)
            mixing = (SCALE * mm(query, key, NT)) * link
            work.append((b, here, query, key, value, beta, system, mixing))
        inverses = unit_lower_inverses([item[6] for item in work], levels, eye)
        for (b, here, query, key, value, beta, system, mixing), inverse in zip(work, inverses):
            inverse_out[here, :] = inverse
            carry = cols[here, 0:1]
            tail = cols[here, 1:2] * beta
            fresh_values = mm_left(inverse, value)
            fresh_keys = mm_left(inverse * rows[b, 0:1, :], key)
            low_mixing = mixing.astype(BF16)
            read = (SCALE * carry) * query.astype(F32) - mm(low_mixing, fresh_keys.astype(BF16))
            value_part[here, :] = fresh_values
            out_part[here, :] = mm(low_mixing, fresh_values.astype(BF16))
            read_out[here, :] = read.astype(BF16)
            both_maps[b, :BLOCK] = read.astype(BF16)
            both_maps[b, BLOCK:] = fresh_keys.astype(BF16)
            carry_end = carry[BLOCK - 1 : BLOCK]
            carry_out[b] = carry_end * key_eye - mm_right(key, tail * fresh_keys, TN)
            add_part[b] = mm_right(key, tail * fresh_values, TN)
        return 0

    lax.fori_loop(0, blocks // UNROLL, prepare, 0)
    for copy in prepared:
        copy.start()

    def chain(b, state):
        state_out[b] = state.astype(BF16)
        return mm_both(carry_out[b], state) + add_part[b]

    lax.fori_loop(0, blocks, chain, jnp.zeros((KEY_SIZE, DV), F32))
    for copy in chained:
        copy.start()

    def finish(group, _):
        for lane in range(UNROLL):
            b = group * UNROLL + lane
            here = rows_of(b)
            source = place[b]
            both = mm(both_maps[b], state_out[b])
            produced = both[:BLOCK] + out_part[here, :]
            fresh_out[here, :] = (value_part[here, :] - both[BLOCK:]).astype(BF16)
            mixer_out[here, :] = produced
            scale = lax.rsqrt(jnp.mean(produced * produced, axis=-1, keepdims=True) + EPSILON)
            gate = pre[rows_of(source), MIXED:LOGIT].astype(F32)
            gated[rows_of(source), :] = (
                produced * scale * head_gain[0:1] * (gate * jax.nn.sigmoid(gate))
            ).astype(BF16)
        return 0

    lax.fori_loop(0, blocks // UNROLL, finish, 0)
    for copy in finished:
        copy.start()
    for copy in prepared + chained + finished:
        copy.wait()


def backward_kernel(
    place,
    d_gated_own,
    d_gated_other,
    pre_own,
    pre_other,
    decay_grid,
    cols,
    taps,
    head_gain,
    mixer_from,
    mixed_from,
    inverse_from,
    state_from,
    fresh_from,
    carry_from,
    read_from,
    d_pre_own,
    d_pre_other,
    grad_taps,
    grad_gain,
    mixer_out,
    mixed_in,
    inverse_in,
    state_in,
    fresh_in,
    carry_in,
    read_in,
    d_out,
    pull_part,
    end_state,
    d_mixed,
    d_gated,
    pre,
    d_main,
    d_gating,
    d_logits,
    marks,
):
    blocks = decay_grid.shape[0]
    half = pre_own.shape[0]
    first_loads = [
        pltpu.make_async_copy(pre_own, pre.at[:half], marks.at[0]),
        pltpu.make_async_copy(pre_other, pre.at[half:], marks.at[1]),
        pltpu.make_async_copy(d_gated_own, d_gated.at[:half], marks.at[2]),
        pltpu.make_async_copy(d_gated_other, d_gated.at[half:], marks.at[3]),
        pltpu.make_async_copy(mixer_from, mixer_out, marks.at[4]),
        pltpu.make_async_copy(read_from, read_in, marks.at[5]),
    ]
    chain_loads = [pltpu.make_async_copy(carry_from, carry_in, marks.at[6])]
    late_loads = [
        pltpu.make_async_copy(mixed_from, mixed_in, marks.at[7]),
        pltpu.make_async_copy(inverse_from, inverse_in, marks.at[8]),
        pltpu.make_async_copy(state_from, state_in, marks.at[9]),
        pltpu.make_async_copy(fresh_from, fresh_in, marks.at[10]),
    ]

    def stores(source, columns, mark):
        return [
            pltpu.make_async_copy(source.at[:half], d_pre_own.at[:, columns], marks.at[mark]),
            pltpu.make_async_copy(source.at[half:], d_pre_other.at[:, columns], marks.at[mark + 1]),
        ]

    gating_stores = stores(d_gating, slice(MIXED, LOGIT), 11)
    logit_stores = stores(d_logits, slice(LOGIT, PACK), 13)
    main_stores = stores(d_main, slice(0, MIXED), 15)
    for copy in first_loads + chain_loads + late_loads:
        copy.start()
    for copy in first_loads:
        copy.wait()
    strict, _, _ = block_masks()
    lane_index = lax.broadcasted_iota(jnp.int32, (BLOCK, PACK - LOGIT), 1)
    grad_taps[...] = jnp.zeros_like(grad_taps)
    grad_gain[...] = jnp.zeros_like(grad_gain)
    d_mixed[blocks * BLOCK :, :] = jnp.zeros((8, MIXED), F32)

    def prepare(group, _):
        for lane in range(UNROLL):
            b = group * UNROLL + lane
            here = rows_of(b)
            there = rows_of(place[b])
            grad = d_gated[there, :].astype(F32)
            gate = pre[there, MIXED:LOGIT].astype(F32)
            produced = mixer_out[here, :]
            scale = lax.rsqrt(jnp.mean(produced * produced, axis=-1, keepdims=True) + EPSILON)
            normed = produced * scale
            sig = jax.nn.sigmoid(gate)
            act = gate * sig
            weighted = grad * head_gain[0:1]
            pulled = weighted * act
            along = jnp.mean(pulled * normed, axis=-1, keepdims=True)
            low = (scale * (pulled - normed * along)).astype(BF16)
            grad_gain[...] += row_sums(grad * normed * act)
            d_gating[there, :] = (
                weighted * normed * (sig * (1.0 + gate * (1.0 - sig)))
            ).astype(BF16)
            d_out[here, :] = low
            pull_part[b] = mm(read_in[here, :], low, TN)
        return 0

    lax.fori_loop(0, blocks // UNROLL, prepare, 0)
    for copy in gating_stores:
        copy.start()
    for copy in chain_loads:
        copy.wait()

    def chain(step, state):
        b = blocks - 1 - step
        end_state[b] = state.astype(BF16)
        return mm_both(carry_in[b], state, TN) + pull_part[b]

    lax.fori_loop(0, blocks, chain, jnp.zeros((KEY_SIZE, DV), F32))
    for copy in late_loads:
        copy.wait()

    def finish(group, _):
        for lane in range(UNROLL):
            b = group * UNROLL + lane
            here = rows_of(b)
            there = rows_of(place[b])
            mixed = mixed_in[here, :]
            gate, act, query_unit, key_unit, query_scale, key_scale = units_of(mixed)
            query, key = query_unit.astype(BF16), key_unit.astype(BF16)
            beta, beta_row = beta_columns(pre[there, LOGIT:])
            link = decay_grid[b] * beta_row
            mixing = (SCALE * mm(query, key, NT)) * link
            carry = cols[here, 0:1]
            tail = cols[here, 1:2] * beta
            low = d_out[here, :]
            end = end_state[b]
            start = state_in[b]
            fresh = fresh_in[here, :]
            d_fresh = mm(mixing.astype(BF16), low, TN) + tail * mm(key, end)
            d_right = mm_left(inverse_in[here, :], d_fresh.astype(BF16), TN)
            d_right_low = d_right.astype(BF16)
            d_logit = (1.0 - beta) * jnp.sum(fresh.astype(F32) * d_right, axis=-1, keepdims=True)
            pair = jnp.concatenate([low, d_right_low], axis=0)
            on_state = mm(pair, start, NT)
            on_fresh = mm(pair, fresh, NT)
            read_grad = (SCALE * on_fresh[:BLOCK]) * link
            system_grad = jnp.where(strict, -on_fresh[BLOCK:] * link, 0.0)
            d_query = (SCALE * carry) * on_state[:BLOCK] + mm(read_grad.astype(BF16), key)
            d_key = (
                mm((system_grad + system_grad.T).astype(BF16), key)
                + mm(read_grad.astype(BF16), query, TN)
                + tail * mm(fresh, end, NT)
                - carry * on_state[BLOCK:]
            )
            d_query = d_query.astype(BF16).astype(F32)
            d_key = d_key.astype(BF16).astype(F32)
            slope = gate * (1.0 + mixed * (1.0 - gate))
            d_mixed[here, :KEY_SIZE] = (
                d_query - query_unit * jnp.sum(query_unit * d_query, axis=-1, keepdims=True)
            ) * (query_scale * slope[:, :KEY_SIZE])
            d_mixed[here, KEY_SIZE : 2 * KEY_SIZE] = (
                d_key - key_unit * jnp.sum(key_unit * d_key, axis=-1, keepdims=True)
            ) * (key_scale * slope[:, KEY_SIZE : 2 * KEY_SIZE])
            d_mixed[here, 2 * KEY_SIZE :] = d_right_low.astype(F32) * slope[:, 2 * KEY_SIZE :]
            d_logits[there, :] = jnp.where(lane_index == 0, d_logit, 0.0).astype(BF16)
        return 0

    lax.fori_loop(0, blocks // UNROLL, finish, 0)
    for copy in logit_stores:
        copy.start()

    def unmix(group, _):
        for lane in range(UNROLL):
            b = group * UNROLL + lane
            there = rows_of(place[b])
            longer = pl.ds(pl.multiple_of(b * BLOCK, BLOCK), BLOCK + 8)
            extended = d_mixed[longer, :]
            current = pre[there, :MIXED].astype(F32)
            total = taps[0:1] * extended[:BLOCK]
            grad_taps[0] += row_sums(current * extended[:BLOCK])
            for lag in range(1, CONV):
                kept = cols[longer, 1 + lag : 2 + lag] * extended
                moved = pltpu.roll(kept, BLOCK + 8 - lag, 0)[:BLOCK]
                total = total + taps[lag : lag + 1] * moved
                grad_taps[lag] += row_sums(current * moved)
            d_main[there, :] = total.astype(BF16)
        return 0

    lax.fori_loop(0, blocks // UNROLL, unmix, 0)
    for copy in main_stores:
        copy.start()
    for copy in gating_stores + logit_stores + main_stores:
        copy.wait()


VMEM_SPEC = pl.BlockSpec(memory_space=pltpu.VMEM)
SMEM_SPEC = pl.BlockSpec(memory_space=pltpu.SMEM)
ANY_SPEC = pl.BlockSpec(memory_space=pl.ANY)
FORWARD_COST = pl.CostEstimate(flops=30_000_000_000, bytes_accessed=100_000_000, transcendentals=0)
SMALL_COST = pl.CostEstimate(flops=1_000_000, bytes_accessed=1_000, transcendentals=0)


def mixer_forward(place, pre_own, pre_other, decay_grid, cols, rows, taps, head_gain):
    blocks = decay_grid.shape[0]
    half, tokens = pre_own.shape[0], blocks * BLOCK
    shape = jax.ShapeDtypeStruct
    return pl.pallas_call(
        forward_kernel,
        out_shape=(
            shape((half, DV), BF16),
            shape((half, DV), BF16),
            shape((tokens, DV), F32),
            shape((tokens, MIXED), F32),
            shape((tokens, BLOCK), F32),
            shape((blocks, KEY_SIZE, DV), BF16),
            shape((tokens, DV), BF16),
            shape((blocks, KEY_SIZE, KEY_SIZE), F32),
            shape((tokens, KEY_SIZE), BF16),
        ),
        in_specs=[SMEM_SPEC] + [ANY_SPEC] * 2 + [VMEM_SPEC] * 5,
        out_specs=[ANY_SPEC] * 9,
        scratch_shapes=[
            pltpu.VMEM((tokens, DV), F32),
            pltpu.VMEM((tokens, MIXED), F32),
            pltpu.VMEM((tokens, BLOCK), F32),
            pltpu.VMEM((blocks, KEY_SIZE, DV), BF16),
            pltpu.VMEM((tokens, DV), BF16),
            pltpu.VMEM((blocks, KEY_SIZE, KEY_SIZE), F32),
            pltpu.VMEM((tokens, KEY_SIZE), BF16),
            pltpu.VMEM((blocks, 2 * BLOCK, KEY_SIZE), BF16),
            pltpu.VMEM((tokens, DV), F32),
            pltpu.VMEM((tokens, DV), F32),
            pltpu.VMEM((blocks, KEY_SIZE, DV), F32),
            pltpu.VMEM((tokens, PACK), BF16),
            pltpu.VMEM((tokens, DV), BF16),
            pltpu.SemaphoreType.DMA((11,)),
        ],
        compiler_params=pltpu.CompilerParams(vmem_limit_bytes=52 * 1024 * 1024),
        cost_estimate=FORWARD_COST,
        name="mixer_forward",
    )(place, pre_own, pre_other, decay_grid, cols, rows, taps, head_gain)


def mixer_backward(place, d_gated, pre, decay_grid, cols, taps, head_gain, kept):
    blocks = decay_grid.shape[0]
    half, tokens = pre[0].shape[0], blocks * BLOCK
    shape = jax.ShapeDtypeStruct
    return pl.pallas_call(
        backward_kernel,
        out_shape=(
            shape((half, PACK), BF16),
            shape((half, PACK), BF16),
            shape((CONV, 8, MIXED), F32),
            shape((8, DV), F32),
        ),
        in_specs=[SMEM_SPEC] + [ANY_SPEC] * 4 + [VMEM_SPEC] * 4 + [ANY_SPEC] * 7,
        out_specs=[ANY_SPEC] * 2 + [VMEM_SPEC] * 2,
        scratch_shapes=[
            pltpu.VMEM((tokens, DV), F32),
            pltpu.VMEM((tokens, MIXED), F32),
            pltpu.VMEM((tokens, BLOCK), F32),
            pltpu.VMEM((blocks, KEY_SIZE, DV), BF16),
            pltpu.VMEM((tokens, DV), BF16),
            pltpu.VMEM((blocks, KEY_SIZE, KEY_SIZE), F32),
            pltpu.VMEM((tokens, KEY_SIZE), BF16),
            pltpu.VMEM((tokens, DV), BF16),
            pltpu.VMEM((blocks, KEY_SIZE, DV), F32),
            pltpu.VMEM((blocks, KEY_SIZE, DV), BF16),
            pltpu.VMEM((tokens + 8, MIXED), F32),
            pltpu.VMEM((tokens, DV), BF16),
            pltpu.VMEM((tokens, PACK), BF16),
            pltpu.VMEM((tokens, MIXED), BF16),
            pltpu.VMEM((tokens, DV), BF16),
            pltpu.VMEM((tokens, PACK - LOGIT), BF16),
            pltpu.SemaphoreType.DMA((17,)),
        ],
        compiler_params=pltpu.CompilerParams(vmem_limit_bytes=52 * 1024 * 1024),
        cost_estimate=SMALL_COST,
        name="mixer_backward",
    )(place, *d_gated, *pre, decay_grid, cols, taps, head_gain, *kept)


def stream_tables(rate, starts):
    blocks = rate.shape[0] // BLOCK
    level = jnp.cumsum(jnp.log(rate).reshape(blocks, BLOCK), axis=-1)
    segment = jnp.cumsum(starts.reshape(blocks, BLOCK), axis=-1)
    positions = jnp.arange(BLOCK)
    causal = positions[:, None] >= positions[None, :]
    linked = (segment[:, :, None] == segment[:, None, :]) & causal
    spread = jnp.where(causal, level[:, :, None] - level[:, None, :], 0.0)
    decay_grid = jnp.where(linked, jnp.exp(spread), 0.0)
    carry = jnp.where(segment == 0, jnp.exp(level), 0.0)
    tail = decay_grid[:, BLOCK - 1, :]
    keep = 1.0 - starts
    padded = jnp.concatenate([jnp.zeros((2,), F32), keep])
    keep_two = keep * padded[1:-1]
    keep_three = keep_two * padded[:-2]
    zero = jnp.zeros_like(keep)
    cols = jnp.stack([carry.reshape(-1), tail.reshape(-1), keep, keep_two, keep_three, zero, zero, zero], axis=1)
    cols = jnp.concatenate([cols, jnp.zeros((8, 8), F32)], axis=0)
    rows = jnp.broadcast_to(carry[:, None, :], (blocks, 8, BLOCK))
    return decay_grid, cols, rows


def unpack_kernel(
    grads, gain, w_query, w_key, w_value, w_gating, w_beta, query, key, value, gating, beta, gain_part
):
    heads = grads.shape[0]
    scale = gain[...]
    total = jnp.zeros((grads.shape[1], 128), F32)

    def lane_sums(values):
        part = values[:, :128]
        for start in range(128, values.shape[1], 128):
            part = part + values[:, start : start + 128]
        return part

    columns = []
    for head in range(heads):
        start = 0
        for out, weights, size in (
            (query, w_query, KEY_SIZE),
            (key, w_key, KEY_SIZE),
            (value, w_value, DV),
            (gating, w_gating, DV),
        ):
            place = slice(head * size, (head + 1) * size)
            part = grads[head, :, start : start + size].astype(F32)
            out[:, place] = part * scale
            total = total + lane_sums(part * weights[:, place].astype(F32))
            start += size
        columns.append(grads[head, :, LOGIT : LOGIT + 1].astype(F32))
    columns = jnp.concatenate(columns, axis=1)
    beta[...] = columns * scale
    gain_part[...] = jnp.sum(total, axis=1, keepdims=True) + jnp.sum(
        columns * w_beta[...].astype(F32), axis=1, keepdims=True
    )


def unpack_heads(grads, gain, w_query, w_key, w_value, w_gating, w_beta):
    shape = jax.ShapeDtypeStruct
    weights = (w_query, w_key, w_value, w_gating, w_beta)
    query, key, value, gating, beta, gain_part = pl.pallas_call(
        unpack_kernel,
        out_shape=tuple(shape(w.shape, F32) for w in weights) + (shape((gain.shape[0], 1), F32),),
        in_specs=[VMEM_SPEC] * 7,
        out_specs=[VMEM_SPEC] * 6,
        compiler_params=pltpu.CompilerParams(vmem_limit_bytes=32 * 1024 * 1024),
        cost_estimate=SMALL_COST,
        name="unpack_heads",
    )(grads, gain, *weights)
    return query, key, value, gating, beta, gain_part[:, 0]


def pack_kernel(
    core, gain, w_beta, rates, starts, *refs
):
    sources, (kept, given), copies, marks = refs[:5], refs[5:7], refs[7:12], refs[12]
    loads = [
        pltpu.make_async_copy(source, copy, marks.at[index])
        for index, (source, copy) in enumerate(zip(sources, copies))
    ]
    for load in loads:
        load.start()
    for load in loads:
        load.wait()
    w_query, w_key, w_value, w_gating, w_output = copies
    heads = kept.shape[0]
    half = kept.shape[1]
    first = core[0] == 0
    scale = gain[...]
    lanes = lax.broadcasted_iota(jnp.int32, (2 * half, 128), 1)
    blank = jnp.zeros((half - 8, 128), F32)

    def two_rows(values):
        right = lanes[: values.shape[0]] >= half
        return jnp.where(right, pltpu.roll(values, half, 1), 0.0), jnp.where(right, values, 0.0)

    rate = rates[...]
    high = rate.astype(BF16).astype(F32)
    middle = (rate - high).astype(BF16).astype(F32)
    notes = [*two_rows(high), *two_rows(middle), *two_rows(rate - high - middle)]
    start_rows = two_rows(jnp.broadcast_to(starts[...], (8, 2 * half)))

    def place(head, columns, values):
        low, high = values[:half], values[half:]
        kept[head, :, columns] = jnp.where(first, low, high).astype(BF16)
        given[head, :, columns] = jnp.where(first, high, low).astype(BF16)

    for head in range(heads):
        start = 0
        for weights, size in ((w_query, KEY_SIZE), (w_key, KEY_SIZE), (w_value, DV), (w_gating, DV)):
            part = weights[:, head * size : (head + 1) * size].astype(F32) * scale
            place(head, slice(start, start + size), part)
            start += size
        beta = w_beta[:, head : head + 1].astype(F32) * scale
        place(
            head, slice(PACK, PACK + DV), w_output[head * DV : (head + 1) * DV, :].astype(F32).T
        )
        note = [part[head : head + 1] for part in notes] + [part[:1] for part in start_rows]
        note = jnp.concatenate(note + [blank], axis=0)
        place(
            head, slice(LOGIT, PACK), jnp.where(lanes < 2, beta, 0.0) + jnp.concatenate([note, note], axis=0)
        )


def pack_heads(core, gain, w_query, w_key, w_value, w_gating, w_beta, w_output, rates, starts):
    rows = gain.shape[0]
    heads = w_query.shape[1] // KEY_SIZE
    wide = (w_query, w_key, w_value, w_gating, w_output)
    shape = jax.ShapeDtypeStruct((heads, rows // 2, PACK + DV), BF16)
    return pl.pallas_call(
        pack_kernel,
        out_shape=(shape, shape),
        in_specs=[SMEM_SPEC] + [VMEM_SPEC] * 4 + [ANY_SPEC] * 5,
        out_specs=[VMEM_SPEC] * 2,
        scratch_shapes=[pltpu.VMEM(w.shape, BF16) for w in wide] + [pltpu.SemaphoreType.DMA((5,))],
        compiler_params=pltpu.CompilerParams(vmem_limit_bytes=58 * 1024 * 1024),
        cost_estimate=SMALL_COST,
        name="pack_heads",
    )(core, gain, w_beta, rates, starts, *wide)


def join_kernel(*refs):
    *pieces, out = refs
    start = 0
    for piece in pieces:
        out[start : start + piece.shape[0]] = piece[...]
        start += piece.shape[0]


def joined_rows(pieces):
    rows, width = sum(piece.shape[0] for piece in pieces), pieces[0].shape[1]
    steps = 2

    def block(size):
        return pl.BlockSpec((size, width // steps), lambda step: (0, step))

    return pl.pallas_call(
        join_kernel,
        out_shape=jax.ShapeDtypeStruct((rows, width), pieces[0].dtype),
        grid=(steps,),
        in_specs=[block(piece.shape[0]) for piece in pieces],
        out_specs=block(rows),
        name="joined_rows",
    )(*pieces)


CHIPS = 16
CORES = 2
BOTH = ("seq", "head")


def along_x(index):
    return index ^ 1


def along_y(index):
    return index ^ 2


def along_z(steps):
    return lambda index: (index + 4 * steps) % CHIPS


def send(value, target):
    return lax.ppermute(value, "seq", [(index, target(index)) for index in range(CHIPS)])


def swap_cores(value):
    return lax.ppermute(value, "head", [(0, 1), (1, 0)])


def exchange(pieces):
    return lax.all_to_all(pieces, "seq", split_axis=0, concat_axis=0, tiled=True)


def after(values, *earlier):
    return lax.optimization_barrier((values, earlier))[0]


def stacked(values):
    return jnp.concatenate(values, axis=0)


def total_of(*values):
    total = values[0].astype(F32)
    for value in values[1:]:
        total = total + value.astype(F32)
    return total


def gather_levels(block):
    return [block] + [send(block, along_z(steps)) for steps in (1, 2, 3)]


def send_near(block):
    return block, send(block, along_x), send(block, along_y)


def far_halves(near):
    _, from_x, from_y = near
    half = from_x.shape[0] // 2
    return from_y[:half], from_x[half:]


def send_far(halves):
    return send(halves[0], along_x), send(halves[1], along_y)


def far_parts(parts):
    rows = parts.shape[0] // 8
    return parts[6 * rows : 7 * rows], parts[7 * rows :]


def near_parts(parts, low, high):
    rows = parts.shape[0] // 8
    for_x = stacked([parts[2 * rows : 3 * rows], total_of(parts[3 * rows : 4 * rows], high).astype(BF16)])
    for_y = stacked([total_of(parts[4 * rows : 5 * rows], low).astype(BF16), parts[5 * rows : 6 * rows]])
    return for_x, for_y


def send_parts(parts):
    return send(parts[0], along_x), send(parts[1], along_y)


def level_parts(parts, from_x, from_y):
    total = total_of(parts[: parts.shape[0] // 4], from_x, from_y)
    rows = total.shape[0] // 4
    return [total[:rows]] + [total[j * rows : (j + 1) * rows].astype(BF16) for j in (1, 2, 3)]


def send_levels(levels):
    return levels[:1] + [send(level, along_z(-j)) for j, level in zip((1, 2, 3), levels[1:])]


def nn(a, b):
    return mm(a, b)


def nt(a, b):
    return mm(a, b, NT)


def tn(a, b):
    return mm(a, b, TN)


def head_plan(
    inputs,
    doc_starts,
    decay_rate,
    mixer_gain,
    w_query,
    w_key,
    w_value,
    w_beta,
    w_gating,
    conv_query,
    conv_key,
    conv_value,
    head_gain,
    w_output,
    feed_gain,
    w_gate,
    w_up,
    w_down,
    cotangent,
):
    chip, core = lax.axis_index("seq"), lax.axis_index("head")
    first = core == 0
    tok_rows, width = inputs.shape
    half_rows = tok_rows // CORES
    row_count = w_query.shape[0]
    half_count = row_count // CORES
    head_count = w_query.shape[1] // KEY_SIZE
    units = w_gate.shape[1] // CHIPS
    own_count = CHIPS * half_rows

    def own_rows(values):
        return lax.dynamic_slice_in_dim(values, core * half_rows, half_rows, 0)

    def in_order(own, other, axis):
        return jnp.concatenate([jnp.where(first, own, other), jnp.where(first, other, own)], axis=axis)

    def split_by_core(pieces):
        kept = lax.dynamic_slice_in_dim(pieces, core * half_count, half_count, 1)
        given = lax.dynamic_slice_in_dim(pieces, (1 - core) * half_count, half_count, 1)
        return in_order(kept, swap_cores(given), 0)

    def joined_by_core(mine):
        both = in_order(mine[:, None], swap_cores(mine)[:, None], 1)
        return both.reshape(width, mine.shape[-1])

    inputs_own = own_rows(inputs).astype(F32)
    scale_one = lax.rsqrt(jnp.mean(inputs_own * inputs_own, axis=-1, keepdims=True) + EPSILON)
    normed_one = inputs_own * scale_one
    gain_one = mixer_gain.astype(F32)[:, None]
    gain_two = feed_gain.astype(F32)[:, None]

    in_kept, in_given = pack_heads(
        core.astype(jnp.int32)[None],
        gain_one,
        w_query,
        w_key,
        w_value,
        w_gating,
        w_beta,
        w_output,
        decay_rate.T,
        doc_starts.astype(F32)[None],
    )
    in_payload = in_order(in_kept, swap_cores(in_given), 0)
    one_levels = gather_levels(normed_one.astype(BF16))
    in_mine = exchange(after(in_payload, one_levels))
    one_near = send_near(stacked(one_levels))
    in_mine = after(in_mine, one_near)
    normed_all = stacked(one_near + send_far(far_halves(one_near)))
    weights_all = joined_by_core(in_mine)
    weights_in, weights_out = weights_all[:, :PACK], weights_all[:, PACK:]

    taps_here = jnp.concatenate(
        [
            conv_query.reshape(CONV, head_count, KEY_SIZE),
            conv_key.reshape(CONV, head_count, KEY_SIZE),
            conv_value.reshape(CONV, head_count, DV),
        ],
        axis=2,
    ).transpose(1, 0, 2)
    taps_there = swap_cores(taps_here)
    taps = lax.dynamic_index_in_dim(
        jnp.where(chip // head_count == core, taps_here, taps_there), chip % head_count, 0, False
    ).astype(F32)
    taps = stacked([taps, jnp.zeros_like(taps)])
    gain_head = jnp.broadcast_to(head_gain.astype(F32)[None], (8, DV))
    seen = in_mine[:, :8, PACK - tok_rows // 2 : PACK].astype(F32).reshape(CHIPS, 4, tok_rows)
    rate = (seen[:, 0] + seen[:, 1] + seen[:, 2]).reshape(-1)
    starts = seen[:, 3].reshape(-1)
    decay_grid, cols, rows = stream_tables(rate, starts)

    blocks = jnp.arange(CHIPS * CORES)
    far = blocks // CORES
    place = (
        4 * ((far ^ chip) % 4) + (chip // 4 - far // 4) % 4 + CHIPS * (blocks % CORES != core)
    ).astype(jnp.int32)

    raw = nn(normed_all, weights_in)
    column = lax.broadcasted_iota(jnp.int32, raw.shape, 1)
    pre_own = jnp.where(
        column == LOGIT + 1,
        raw - lax.reduce_precision(raw, exponent_bits=8, mantissa_bits=7),
        raw,
    ).astype(BF16)
    pre = (pre_own, swap_cores(pre_own))

    feed = jnp.concatenate(
        [
            (w_gate.astype(F32) * gain_two).astype(BF16).T.reshape(CHIPS, units, row_count),
            (w_up.astype(F32) * gain_two).astype(BF16).T.reshape(CHIPS, units, row_count),
            w_down.reshape(CHIPS, units, row_count),
        ],
        axis=1,
    )
    feed = after(feed, in_mine)
    feed_mine = exchange(feed)
    gated_own, gated_other, *kept = mixer_forward(place, *pre, decay_grid, cols, rows, taps, gain_head)
    mixed_parts = nt(gated_own, weights_out).astype(BF16)
    far = send_far(far_parts(mixed_parts))

    cot_own = own_rows(cotangent)
    far, feed_mine = after((far, feed_mine))
    near = near_parts(mixed_parts, *far)
    near, cot = send_parts(near), gather_levels(after(cot_own, near))
    feed_other = swap_cores(feed_mine)
    near, cot = after((near, cot))
    levels = level_parts(mixed_parts, *near)
    levels, cot = send_levels(levels), send_near(stacked(after(cot, levels)))

    levels, cot = after((levels, cot))
    middle = inputs_own + total_of(*levels)
    scale_two = lax.rsqrt(jnp.mean(middle * middle, axis=-1, keepdims=True) + EPSILON)
    normed_mid = middle * scale_two
    mid = normed_mid.astype(BF16)
    mid_sent, cot_far = gather_levels(mid), send_far(far_halves(after(cot, mid)))
    feed_mine, feed_other = after((feed_mine, feed_other), mid)

    def unit_rows(position):
        return stacked(
            [
                part[:, position * units : (position + 1) * units].transpose(1, 0, 2).reshape(units, width)
                for part in (feed_mine, feed_other)
            ]
        )

    gate_rows, up_rows, down_rows = unit_rows(0), unit_rows(1), unit_rows(2)
    mid = mid_sent
    mid, cot_far, gate_rows, up_rows, down_rows = after((mid, cot_far, gate_rows, up_rows, down_rows))
    mid = stacked(mid)
    cot_all = stacked(after(cot, mid) + cot_far)
    cut = after(normed_all, mid).reshape(own_count, CHIPS, CORES, half_count)
    cut_mine = lax.dynamic_index_in_dim(cut, core, 2, False).reshape(own_count, width // CORES)
    cut_given = lax.dynamic_index_in_dim(cut, 1 - core, 2, False).reshape(own_count, width // CORES)
    mid = send_near(mid)
    d_hidden = nt(cot_all, down_rows).astype(BF16)
    mid, d_hidden, cut_mine, cut_given = after((mid, d_hidden, cut_mine, cut_given))
    cut_other = swap_cores(cut_given)
    mid_all = stacked(mid + send_far(far_halves(mid)))

    gate_lin = nt(mid_all, gate_rows)
    up_lin = nt(mid_all, up_rows)
    d_hidden = d_hidden.astype(F32)
    sig = jax.nn.sigmoid(gate_lin)
    act = gate_lin * sig
    hidden = (act * up_lin).astype(BF16)
    d_gate = (d_hidden * up_lin * (sig * (1.0 + gate_lin * (1.0 - sig)))).astype(BF16)
    d_up = (d_hidden * act).astype(BF16)
    e_parts = (nn(d_gate, gate_rows) + nn(d_up, up_rows)).astype(BF16)
    far = send_far(far_parts(e_parts))
    feed_parts = nn(after(hidden, e_parts), down_rows).astype(BF16)
    far, feed_parts = after((far, feed_parts))
    near = send_parts(near_parts(e_parts, *far))

    parts = [tn(d_gate, mid_all), tn(d_up, mid_all), tn(hidden, cot_all)]
    keep_part = stacked([part[:units] for part in parts])
    give_part = stacked([part[units:] for part in parts]).astype(BF16)
    near, feed_parts, keep_part, give_part = after((near, feed_parts, keep_part, give_part))
    levels = level_parts(e_parts, *near)
    levels, feed_far = send_levels(levels), send_far(far_parts(after(feed_parts, levels)))
    levels, feed_far = after((levels, feed_far))
    e_two = total_of(*levels)
    d_middle = cot_own.astype(F32) + scale_two * (
        e_two - normed_mid * jnp.mean(e_two * normed_mid, axis=-1, keepdims=True)
    )
    d_mid = d_middle.astype(BF16)
    d_mid, feed_near = gather_levels(d_mid), send_parts(near_parts(feed_parts, *after(feed_far, d_mid)))
    feed_grad = (keep_part + swap_cores(give_part).astype(F32)).astype(BF16)
    feed_grad = feed_grad.reshape(3 * units, CHIPS, row_count).transpose(1, 0, 2)
    feed_grad = jnp.pad(feed_grad, ((0, 0), (0, half_count * DV // row_count), (0, 0)))
    d_mid, feed_near, feed_grad = after((d_mid, feed_near, feed_grad))
    d_mid = stacked(d_mid)
    feed_levels = level_parts(feed_parts, *after(feed_near, d_mid))
    d_mid, feed_levels = send_near(d_mid), send_levels(feed_levels)
    d_mid, feed_levels = after((d_mid, feed_levels))
    d_mid_all = stacked(d_mid + send_far(far_halves(d_mid)))

    d_gated_own = nn(d_mid_all, weights_out).astype(BF16)
    d_gated = (d_gated_own, swap_cores(d_gated_own))
    grad_out = tn(d_mid_all, gated_own).astype(BF16).reshape(CHIPS, CORES, half_count, DV)
    grad_out = total_of(
        lax.dynamic_index_in_dim(grad_out, core, 1, False),
        swap_cores(lax.dynamic_index_in_dim(grad_out, 1 - core, 1, False)),
    ).astype(BF16)
    feed_grad = lax.dynamic_update_slice(
        feed_grad, grad_out.reshape(CHIPS, half_count * DV // row_count, row_count), (0, 3 * units, 0)
    )
    feed_back = exchange(feed_grad)
    d_pre_own, d_pre_other, grad_taps, grad_gain = mixer_backward(
        place, d_gated, pre, decay_grid, cols, taps, gain_head, kept
    )


    small = jnp.concatenate([jnp.sum(grad_taps, axis=1).reshape(-1), jnp.sum(grad_gain, axis=0)])
    small = small.reshape(-1, 64)
    small_rows = small.shape[0]
    grad_in = tn(cut_mine, d_pre_own) + tn(cut_other, d_pre_other)
    small = jnp.pad(small, ((0, half_count - small_rows), (PACK - 64, 0)))
    grad_in = (grad_in.reshape(CHIPS, half_count, PACK) + small).astype(BF16)
    grad_in, feed_back = after((grad_in, feed_back))
    e_parts = nt(after(d_pre_own, grad_in), weights_in).astype(BF16)
    grad_in = exchange(grad_in)
    near = send_parts(near_parts(e_parts, *send_far(far_parts(e_parts))))
    near, grad_in = after((near, grad_in))
    levels = level_parts(e_parts, *near)
    grad_in, feed_back = after((grad_in, feed_back), levels)
    e_levels = send_levels(levels)
    small = grad_in[:, :small_rows, PACK - 64 :].astype(F32).reshape(CHIPS, -1)
    taps_all = lax.dynamic_slice_in_dim(small[:, : CONV * MIXED], core * head_count, head_count, 0)
    taps_all = taps_all.reshape(head_count, CONV, MIXED).transpose(1, 0, 2)

    def heads_here(back):
        mine = lax.dynamic_slice_in_dim(back, core * head_count, head_count, 0)
        given = lax.dynamic_slice_in_dim(back, (1 - core) * head_count, head_count, 0)
        return in_order(mine, swap_cores(given), 1)

    grad_in = heads_here(grad_in)
    block_out_own = (middle + total_of(*feed_levels)).astype(BF16)
    block_out = in_order(block_out_own, swap_cores(block_out_own), 0)
    grad_out = heads_here(feed_back[:, 3 * units :].reshape(CHIPS, half_count, DV))
    grad_output = grad_out.astype(F32).transpose(0, 2, 1).reshape(head_count * DV, row_count)
    feed_back = feed_back[:, : 3 * units].astype(F32)
    raw_gate = feed_back[:, :units].reshape(CHIPS * units, row_count).T
    raw_up = feed_back[:, units : 2 * units].reshape(CHIPS * units, row_count).T
    grad_down = feed_back[:, 2 * units :].reshape(CHIPS * units, row_count)
    feed_gain_part = jnp.sum(raw_gate * w_gate.astype(F32) + raw_up * w_up.astype(F32), axis=1)

    raw_query, raw_key, raw_value, raw_gating, raw_beta, mixer_gain_part = unpack_heads(
        grad_in, gain_one, w_query, w_key, w_value, w_gating, w_beta
    )
    gain_parts = jnp.stack([mixer_gain_part, feed_gain_part])
    gain_totals = gain_parts + swap_cores(gain_parts)

    others = (
        gain_totals[0],
        raw_query,
        raw_key,
        raw_value,
        raw_beta,
        raw_gating,
        taps_all[:, :, :KEY_SIZE].reshape(CONV, head_count * KEY_SIZE),
        taps_all[:, :, KEY_SIZE : 2 * KEY_SIZE].reshape(CONV, head_count * KEY_SIZE),
        taps_all[:, :, 2 * KEY_SIZE :].reshape(CONV, head_count * DV),
        jnp.sum(small[:, CONV * MIXED :], axis=0),
        grad_output,
        gain_totals[1],
        raw_gate * gain_two,
        raw_up * gain_two,
        grad_down,
    )
    e_levels, block_out, others = after((e_levels, block_out, others))
    e_one = total_of(*e_levels)
    grad_own = d_middle + scale_one * (
        e_one - normed_one * jnp.mean(e_one * normed_one, axis=-1, keepdims=True)
    )
    grad_inputs = in_order(grad_own, swap_cores(grad_own), 0)
    return (block_out, grad_inputs) + others


EXACT_PRECISION = lax.Precision.HIGHEST


def passed_along(value, axis, steps):
    count = lax.axis_size(axis)
    first, last = (max(0, -steps), min(count, count - steps))
    return lax.ppermute(value, axis, [(source, source + steps) for source in range(first, last)])


def entering(value, axis, join, neutral):
    count, mine = (lax.axis_size(axis), lax.axis_index(axis))
    pieces = jax.tree.map(lambda part: lax.all_gather(part, axis), value)
    subtotal = jax.tree.map(
        lambda part, zero: jnp.full_like(part, 0) + jnp.asarray(zero, part.dtype), value, neutral
    )

    def lap(position, subtotal):
        longer = join(subtotal, jax.tree.map(lambda part: part[position], pieces))
        return jax.tree.map(lambda new, old: jnp.where(position < mine, new, old), longer, subtotal)

    return lax.fori_loop(0, count - 1, lap, subtotal)


def carried_in(shard, axis, join, neutral):
    count = lax.axis_size(axis)
    place = lax.axis_index(axis)
    ahead = count - 1 - place
    gathered = jax.tree.map(
        lambda a, kind: lax.all_gather(a.astype(kind), axis),
        shard,
        jax.tree.map(lambda a: jnp.bfloat16 if a.dtype == jnp.float32 else a.dtype, shard),
    )
    state = jax.tree.map(lambda a, e: jnp.zeros_like(a) + jnp.asarray(e, a.dtype), shard, neutral)

    def one(lap, state):
        source = count - 1 - lap
        return join(
            state,
            jax.tree.map(
                lambda a, own: lax.dynamic_index_in_dim(a, source, 0, False).astype(own.dtype),
                gathered,
                shard,
            ),
        )

    return lax.fori_loop(0, ahead, one, state)


def high_einsum(einsum_form, *arrays):
    return jnp.einsum(
        einsum_form, *arrays, precision=EXACT_PRECISION, preferred_element_type=jnp.float32
    )


def low_dot(left_side, right_side):
    return jnp.dot(left_side, right_side, preferred_element_type=jnp.float32)


def inner_dot(left_side, right_side):
    return lax.dot_general(
        left_side, right_side, (((0,), (0,)), ((), ())), preferred_element_type=jnp.float32
    )


def outer_dot(left_side, right_side):
    return lax.dot_general(
        left_side, right_side, (((1,), (1,)), ((), ())), preferred_element_type=jnp.float32
    )


def rounded(values):
    return lax.optimization_barrier(values.astype(jnp.bfloat16)).astype(jnp.float32)


def scale_norm(values, gain_vec):
    return (
        values * lax.rsqrt(jnp.mean(values * values, axis=-1, keepdims=True) + EPSILON) * gain_vec
    )


def unit_rows(values):
    return values * lax.rsqrt(jnp.sum(values * values, axis=-1, keepdims=True) + EPSILON)


def swiglu(gate_lin, up_lin):
    return jax.nn.silu(gate_lin) * up_lin


def compose_maps(earlier_map, later_map):
    return (
        high_einsum("hde,hef->hdf", later_map[0], earlier_map[0]),
        high_einsum("hde,hef->hdf", later_map[0], earlier_map[1]) + later_map[1],
    )


def gather_plan(
    inputs,
    doc_starts,
    decay_rate,
    mixer_gain,
    w_query,
    w_key,
    w_value,
    w_beta,
    w_gating,
    conv_query,
    conv_key,
    conv_value,
    head_gain,
    w_output,
    feed_gain,
    w_gate,
    w_up,
    w_down,
    cotangent,
):
    tok_rows = inputs.shape[0]
    head_count = decay_rate.shape[1]
    key_width = w_query.shape[1]
    value_width = w_value.shape[1]
    edge_count = CONV - 1
    block_count = tok_rows // BLOCK
    gathered = (
        lax.all_gather(mixer_gain, "seq", axis=0, tiled=True),
        lax.all_gather(w_query, "seq", axis=0, tiled=True),
        lax.all_gather(w_key, "seq", axis=0, tiled=True),
        lax.all_gather(w_value, "seq", axis=0, tiled=True),
        lax.all_gather(w_beta, "seq", axis=0, tiled=True),
        lax.all_gather(w_gating, "seq", axis=0, tiled=True),
        lax.all_gather(w_output, "seq", axis=1, tiled=True),
        lax.all_gather(feed_gain, "seq", axis=0, tiled=True),
        lax.all_gather(w_gate, "seq", axis=0, tiled=True),
        lax.all_gather(w_up, "seq", axis=0, tiled=True),
        lax.all_gather(w_down, "seq", axis=1, tiled=True),
    )
    (
        gain_one,
        full_query,
        full_key,
        full_value,
        full_beta,
        full_gating,
        full_output,
        gain_two,
        full_gate,
        full_up,
        full_down,
    ) = gathered
    inputs_float = inputs.astype(jnp.float32)
    normed_float, norm_one_back = jax.vjp(scale_norm, inputs_float, gain_one.astype(jnp.float32))
    normed_one = normed_float.astype(jnp.bfloat16)
    query_pre = low_dot(normed_one, full_query).astype(jnp.bfloat16)
    key_pre = low_dot(normed_one, full_key).astype(jnp.bfloat16)
    value_pre = low_dot(normed_one, full_value).astype(jnp.bfloat16)
    gating_pre = low_dot(normed_one, full_gating).astype(jnp.bfloat16)
    beta_logit = low_dot(normed_one, full_beta)
    joined = jnp.concatenate([query_pre, key_pre, value_pre], axis=1)
    tail_starts = doc_starts[tok_rows - edge_count :]
    later_starts = jnp.cumsum(tail_starts[::-1])[::-1] - tail_starts
    sender_keep = (later_starts == 0).astype(jnp.bfloat16)[:, None]
    edge_in = passed_along(joined[tok_rows - edge_count :] * sender_keep, "seq", 1)
    local_doc = jnp.cumsum(doc_starts)
    padded_doc = jnp.concatenate([jnp.zeros((edge_count,), local_doc.dtype), local_doc])
    keep_masks = [
        (
            padded_doc[edge_count - shift_lag : edge_count - shift_lag + tok_rows] == local_doc
        ).astype(jnp.float32)[:, None]
        for shift_lag in range(CONV)
    ]

    def conv_piece(extended, conv_weights):
        mixed = keep_masks[0] * conv_weights[0] * extended[edge_count:]
        for shift_lag in range(1, CONV):
            mixed = (
                mixed
                + keep_masks[shift_lag]
                * conv_weights[shift_lag]
                * extended[edge_count - shift_lag : edge_count - shift_lag + tok_rows]
            )
        activated = jax.nn.silu(mixed)
        query_unit = unit_rows(activated[:, :key_width].reshape(tok_rows, head_count, KEY_SIZE))
        key_unit = unit_rows(
            activated[:, key_width : 2 * key_width].reshape(tok_rows, head_count, KEY_SIZE)
        )
        value_act = activated[:, 2 * key_width :].reshape(tok_rows, head_count, DV)
        return (query_unit, key_unit, value_act)

    extended = jnp.concatenate([edge_in, joined], axis=0).astype(jnp.float32)
    conv_weights = jnp.concatenate([conv_query, conv_key, conv_value], axis=1).astype(jnp.float32)
    (query_unit, key_unit, value_act), conv_back = jax.vjp(conv_piece, extended, conv_weights)

    def to_blocks(values):
        return values.reshape(block_count, BLOCK, head_count, values.shape[-1]).transpose(
            0, 2, 1, 3
        )

    def from_blocks(values):
        return values.transpose(0, 2, 1, 3).reshape(tok_rows, head_count, values.shape[-1])

    log_rate = jnp.log(decay_rate).reshape(block_count, BLOCK, head_count).transpose(0, 2, 1)
    log_level = jnp.cumsum(log_rate, axis=-1)
    segment = jnp.cumsum(doc_starts.reshape(block_count, BLOCK), axis=-1)
    positions = jnp.arange(BLOCK)
    causal = positions[:, None] >= positions[None, :]
    strict = positions[:, None] > positions[None, :]
    linked = (segment[:, None, :, None] == segment[:, None, None, :]) & causal
    spread = jnp.where(causal, log_level[..., :, None] - log_level[..., None, :], 0.0)
    decay_grid = jnp.where(linked, jnp.exp(spread), 0.0)
    carry_in = jnp.where(segment[:, None, :] == 0, jnp.exp(log_level), 0.0)
    tail_decay = decay_grid[..., BLOCK - 1, :]
    key_eye = jnp.eye(KEY_SIZE, dtype=jnp.float32)
    block_eye = jnp.eye(BLOCK, dtype=jnp.float32)

    def block_terms(query_blocks, key_blocks, value_blocks, logit_blocks):
        beta_gate = jax.nn.sigmoid(logit_blocks)
        key_gram = high_einsum("nhcd,nhmd->nhcm", key_blocks, key_blocks)
        system = block_eye + jnp.where(strict, decay_grid * key_gram * beta_gate[..., None, :], 0.0)
        right_side = jnp.concatenate([value_blocks, carry_in[..., None] * key_blocks], axis=-1)
        solved = jax.scipy.linalg.solve_triangular(
            system, right_side, lower=True, unit_diagonal=True
        )
        fresh_values = solved[..., :DV]
        fresh_keys = solved[..., DV:]
        mixing = (
            high_einsum("nhcd,nhmd->nhcm", query_blocks, key_blocks)
            * decay_grid
            * beta_gate[..., None, :]
        )
        weighted = key_blocks * (tail_decay * beta_gate)[..., None]
        block_maps = carry_in[..., BLOCK - 1, None, None] * key_eye - high_einsum(
            "nhcd,nhce->nhde", weighted, fresh_keys
        )
        block_adds = high_einsum("nhcd,nhce->nhde", weighted, fresh_values)

        def chain_step(current, element):
            return (compose_maps(current, element), None)

        start_map = (
            jnp.broadcast_to(key_eye, (head_count, KEY_SIZE, KEY_SIZE)),
            jnp.zeros((head_count, KEY_SIZE, DV), jnp.float32),
        )
        device_pair, _ = lax.scan(chain_step, start_map, (block_maps, block_adds))
        return (
            (fresh_values, fresh_keys, mixing, block_maps, block_adds),
            device_pair[0],
            device_pair[1],
        )

    def block_outputs(block_parts, query_blocks, start_state):

        def step_block(current, element):
            fresh_values, fresh_keys, mixing, block_map, block_add, query_part, carry_part = element
            updated = fresh_values - high_einsum("hcd,hde->hce", fresh_keys, current)
            produced_output = (
                carry_part[..., None] * high_einsum("hcd,hde->hce", query_part, current)
                + high_einsum("hcm,hme->hce", mixing, updated)
            ) * KEY_SIZE ** (-0.5)
            return (high_einsum("hde,hef->hdf", block_map, current) + block_add, produced_output)

        _, emitted_all = lax.scan(step_block, start_state, block_parts + (query_blocks, carry_in))
        return emitted_all

    query_blocks = to_blocks(rounded(query_unit))
    key_blocks = to_blocks(rounded(key_unit))
    value_blocks = to_blocks(rounded(value_act))
    logit_blocks = beta_logit.reshape(block_count, BLOCK, head_count).transpose(0, 2, 1)
    (block_parts, device_map, device_add), terms_back = jax.vjp(
        block_terms, query_blocks, key_blocks, value_blocks, logit_blocks
    )
    identity = (jnp.broadcast_to(key_eye, device_map.shape), jnp.zeros_like(device_add))
    prefix = entering((device_map, device_add), "seq", compose_maps, identity)
    start_state = prefix[1]
    produced_output, emitted_back = jax.vjp(block_outputs, block_parts, query_blocks, start_state)

    def gated_norm(values, gating_values, gain_vec):
        normed_out = values * lax.rsqrt(jnp.mean(values * values, axis=-1, keepdims=True) + EPSILON)
        return (normed_out * gain_vec * jax.nn.silu(gating_values)).reshape(tok_rows, value_width)

    mixer_out = from_blocks(produced_output)
    gated_float, gated_back = jax.vjp(
        gated_norm,
        mixer_out,
        gating_pre.astype(jnp.float32).reshape(tok_rows, head_count, DV),
        head_gain.astype(jnp.float32),
    )
    gated_out = gated_float.astype(jnp.bfloat16)
    middle = inputs_float + lax.psum(
        low_dot(gated_out, full_output).astype(jnp.bfloat16), "head"
    ).astype(jnp.float32)
    normed_middle, norm_two_back = jax.vjp(scale_norm, middle, gain_two.astype(jnp.float32))
    normed_two = normed_middle.astype(jnp.bfloat16)
    gate_lin = low_dot(normed_two, full_gate)
    up_lin = low_dot(normed_two, full_up)
    hidden_float, swiglu_back = jax.vjp(swiglu, gate_lin, up_lin)
    hidden = hidden_float.astype(jnp.bfloat16)
    feed_out = lax.psum(low_dot(hidden, full_down).astype(jnp.bfloat16), "head").astype(jnp.float32)
    block_out = (middle + feed_out).astype(jnp.bfloat16)
    regathered = (
        lax.all_gather(w_query, "seq", axis=0, tiled=True),
        lax.all_gather(w_key, "seq", axis=0, tiled=True),
        lax.all_gather(w_value, "seq", axis=0, tiled=True),
        lax.all_gather(w_beta, "seq", axis=0, tiled=True),
        lax.all_gather(w_gating, "seq", axis=0, tiled=True),
        lax.all_gather(w_output, "seq", axis=1, tiled=True),
        lax.all_gather(w_gate, "seq", axis=0, tiled=True),
        lax.all_gather(w_up, "seq", axis=0, tiled=True),
        lax.all_gather(w_down, "seq", axis=1, tiled=True),
    )
    (
        full_query,
        full_key,
        full_value,
        full_beta,
        full_gating,
        full_output,
        full_gate,
        full_up,
        full_down,
    ) = regathered
    cotangent_float = cotangent.astype(jnp.float32)
    grad_down = inner_dot(hidden, cotangent)
    d_hidden = rounded(outer_dot(cotangent, full_down))
    d_gate_float, d_up_float = swiglu_back(d_hidden)
    d_gate = d_gate_float.astype(jnp.bfloat16)
    d_up = d_up_float.astype(jnp.bfloat16)
    grad_gate = inner_dot(normed_two, d_gate)
    grad_up = inner_dot(normed_two, d_up)
    d_normed_two = lax.psum(
        (outer_dot(d_gate, full_gate) + outer_dot(d_up, full_up)).astype(jnp.bfloat16), "head"
    ).astype(jnp.float32)
    d_middle_norm, grad_gain_two = norm_two_back(d_normed_two)
    d_middle = cotangent_float + d_middle_norm
    d_middle_low = d_middle.astype(jnp.bfloat16)
    grad_output = inner_dot(gated_out, d_middle_low)
    d_gated = rounded(outer_dot(d_middle_low, full_output))
    d_mixer_out, d_gating_float, grad_head_part = gated_back(d_gated)
    d_gating = d_gating_float.reshape(tok_rows, value_width).astype(jnp.bfloat16)
    d_parts, d_query_late, d_start = emitted_back(to_blocks(d_mixer_out))
    chained = carried_in((jnp.swapaxes(device_map, 1, 2), d_start), "seq", compose_maps, identity)
    d_end = chained[1]
    d_map = high_einsum("hde,hfe->hdf", d_end, start_state)
    d_query_early, d_key_blocks, d_value_blocks, d_logit_blocks = terms_back(
        (d_parts, d_map, d_end)
    )
    d_query_unit = rounded(from_blocks(d_query_early + d_query_late))
    d_key_unit = rounded(from_blocks(d_key_blocks))
    d_value_act = rounded(from_blocks(d_value_blocks))
    d_beta_logit = (
        d_logit_blocks.transpose(0, 2, 1).reshape(tok_rows, head_count).astype(jnp.bfloat16)
    )
    d_extended, grad_conv_all = conv_back((d_query_unit, d_key_unit, d_value_act))
    returned = passed_along(d_extended[:edge_count].astype(jnp.bfloat16), "seq", -1).astype(
        jnp.float32
    )
    d_rows = d_extended[edge_count:]
    d_rows = jnp.concatenate(
        [
            d_rows[: tok_rows - edge_count],
            d_rows[tok_rows - edge_count :] + returned * sender_keep.astype(jnp.float32),
        ],
        axis=0,
    )
    d_joined = d_rows.astype(jnp.bfloat16)
    d_query_pre = d_joined[:, :key_width]
    d_key_pre = d_joined[:, key_width : 2 * key_width]
    d_value_pre = d_joined[:, 2 * key_width :]
    grad_query = inner_dot(normed_one, d_query_pre)
    grad_key = inner_dot(normed_one, d_key_pre)
    grad_value = inner_dot(normed_one, d_value_pre)
    grad_gating = inner_dot(normed_one, d_gating)
    grad_beta = inner_dot(normed_one, d_beta_logit)
    d_normed_part = (
        outer_dot(d_query_pre, full_query)
        + outer_dot(d_key_pre, full_key)
        + outer_dot(d_value_pre, full_value)
        + outer_dot(d_gating, full_gating)
        + outer_dot(d_beta_logit, full_beta)
    )
    d_normed_one, head_total = (
        lax.psum(d_normed_part.astype(jnp.bfloat16), "head").astype(jnp.float32),
        lax.psum(grad_head_part.astype(jnp.bfloat16), "head").astype(jnp.float32),
    )
    d_inputs_norm, grad_gain_one = norm_one_back(d_normed_one)
    grad_inputs = d_middle + d_inputs_norm
    small_totals = lax.psum((grad_conv_all, head_total), "seq")
    conv_total = small_totals[0]
    totals = (
        lax.psum_scatter(grad_gain_one, "seq", scatter_dimension=0, tiled=True),
        lax.psum_scatter(grad_query, "seq", scatter_dimension=0, tiled=True),
        lax.psum_scatter(grad_key, "seq", scatter_dimension=0, tiled=True),
        lax.psum_scatter(grad_value, "seq", scatter_dimension=0, tiled=True),
        lax.psum_scatter(grad_beta, "seq", scatter_dimension=0, tiled=True),
        lax.psum_scatter(grad_gating, "seq", scatter_dimension=0, tiled=True),
        lax.psum_scatter(grad_output, "seq", scatter_dimension=1, tiled=True),
        lax.psum_scatter(grad_gain_two, "seq", scatter_dimension=0, tiled=True),
        lax.psum_scatter(grad_gate, "seq", scatter_dimension=0, tiled=True),
        lax.psum_scatter(grad_up, "seq", scatter_dimension=0, tiled=True),
        lax.psum_scatter(grad_down, "seq", scatter_dimension=1, tiled=True),
    )
    return (
        block_out,
        grad_inputs,
        totals[0],
        totals[1],
        totals[2],
        totals[3],
        totals[4],
        totals[5],
        conv_total[:, :key_width],
        conv_total[:, key_width : 2 * key_width],
        conv_total[:, 2 * key_width :],
        small_totals[1],
        totals[6],
        totals[7],
        totals[8],
        totals[9],
        totals[10],
    )


def solution(mesh):
    in_specs = (
        P("seq", None),
        P("seq"),
        P("seq", "head"),
        P("seq"),
        P("seq", "head"),
        P("seq", "head"),
        P("seq", "head"),
        P("seq", "head"),
        P("seq", "head"),
        P(None, "head"),
        P(None, "head"),
        P(None, "head"),
        P(),
        P("head", "seq"),
        P("seq"),
        P("seq", "head"),
        P("seq", "head"),
        P("head", "seq"),
        P("seq", None),
    )
    out_specs = (
        P("seq", None),
        P("seq", None),
        P("seq"),
        P("seq", "head"),
        P("seq", "head"),
        P("seq", "head"),
        P("seq", "head"),
        P("seq", "head"),
        P(None, "head"),
        P(None, "head"),
        P(None, "head"),
        P(),
        P("head", "seq"),
        P("seq"),
        P("seq", "head"),
        P("seq", "head"),
        P("head", "seq"),
    )
    whole_heads = mesh.shape["seq"] == CHIPS and mesh.shape["head"] == CORES
    per_device = head_plan if whole_heads else gather_plan
    return jax.shard_map(
        per_device, mesh=mesh, in_specs=in_specs, out_specs=out_specs, check_vma=False
    )
```

```python
import jax
import jax.numpy as jnp
from jax import lax
from jax.sharding import PartitionSpec as P
from jax.experimental import pallas as pl
from jax.experimental.pallas import tpu as pltpu

KEY_SIZE = 128
DV = 256
CONV = 4
BLOCK = 64
EPSILON = 1e-06
F32 = jnp.float32
BF16 = jnp.bfloat16
LOGIT = 2 * KEY_SIZE + 2 * DV
PACK = LOGIT + 128
MIXED = 2 * KEY_SIZE + DV
SCALE = KEY_SIZE**-0.5
UNROLL = 16


def mm(a, b, dims=((1,), (0,))):
    return lax.dot_general(a, b, (dims, ((), ())), preferred_element_type=F32)


NT = ((1,), (1,))
TN = ((0,), (0,))


def halves(a):
    high = a.astype(BF16)
    return high, (a - high.astype(F32)).astype(BF16)


def mm_left(a, b, dims=((1,), (0,))):
    high, low = halves(a)
    return mm(high, b, dims) + mm(low, b, dims)


def mm_right(a, b, dims=((1,), (0,))):
    high, low = halves(b)
    return mm(a, high, dims) + mm(a, low, dims)


def mm_both(a, b, dims=((1,), (0,))):
    a_high, a_low = halves(a)
    b_high, b_low = halves(b)
    return mm(a_high, b_high, dims) + (mm(a_high, b_low, dims) + mm(a_low, b_high, dims))


def block_masks():
    row = lax.broadcasted_iota(jnp.int32, (BLOCK, BLOCK), 0)
    col = lax.broadcasted_iota(jnp.int32, (BLOCK, BLOCK), 1)
    strict = row > col
    levels = []
    size = 1
    while size < BLOCK:
        levels.append(
            (row // (2 * size) == col // (2 * size)) & (row // size % 2 == 1) & (col // size % 2 == 0)
        )
        size *= 2
    return strict, levels, (row == col).astype(F32)


def unit_lower_inverses(systems, levels, eye):
    inverses = [eye - jnp.where(levels[0], system, 0.0) for system in systems]
    for level in levels[1:]:
        inner = [
            mm_both(jnp.where(level, system, 0.0), inverse)
            for system, inverse in zip(systems, inverses)
        ]
        inverses = [
            inverse - mm_both(inverse, part) for inverse, part in zip(inverses, inner)
        ]
    return inverses


def rows_of(index):
    return pl.ds(pl.multiple_of(index * BLOCK, BLOCK), BLOCK)


def row_sums(values):
    return jnp.sum(values.reshape(values.shape[0] // 8, 8, values.shape[1]), axis=0)


def beta_columns(packed):
    logit = packed[:, :1].astype(F32) + packed[:, 1:2].astype(F32)
    beta = jax.nn.sigmoid(logit)
    return beta, jnp.broadcast_to(beta, (BLOCK, 128)).T[:BLOCK]


def units_of(mixed):
    gate = jax.nn.sigmoid(mixed)
    act = mixed * gate
    query, key = act[:, :KEY_SIZE], act[:, KEY_SIZE : 2 * KEY_SIZE]
    query_scale = lax.rsqrt(jnp.sum(query * query, axis=-1, keepdims=True) + EPSILON)
    key_scale = lax.rsqrt(jnp.sum(key * key, axis=-1, keepdims=True) + EPSILON)
    return gate, act, query * query_scale, key * key_scale, query_scale, key_scale


def forward_kernel(
    place,
    pre_own,
    pre_other,
    decay_grid,
    cols,
    rows,
    taps,
    head_gain,
    gated_own,
    gated_other,
    mixer_to,
    mixed_to,
    inverse_to,
    state_to,
    fresh_to,
    carry_to,
    read_to,
    mixer_out,
    mixed_out,
    inverse_out,
    state_out,
    fresh_out,
    carry_out,
    read_out,
    both_maps,
    value_part,
    out_part,
    add_part,
    pre,
    gated,
    marks,
):
    blocks = decay_grid.shape[0]
    half = pre_own.shape[0]
    loads = [
        pltpu.make_async_copy(pre_own, pre.at[:half], marks.at[0]),
        pltpu.make_async_copy(pre_other, pre.at[half:], marks.at[1]),
    ]
    prepared = [
        pltpu.make_async_copy(mixed_out, mixed_to, marks.at[2]),
        pltpu.make_async_copy(inverse_out, inverse_to, marks.at[3]),
        pltpu.make_async_copy(carry_out, carry_to, marks.at[4]),
        pltpu.make_async_copy(read_out, read_to, marks.at[5]),
    ]
    chained = [pltpu.make_async_copy(state_out, state_to, marks.at[6])]
    finished = [
        pltpu.make_async_copy(gated.at[:half], gated_own, marks.at[7]),
        pltpu.make_async_copy(gated.at[half:], gated_other, marks.at[8]),
        pltpu.make_async_copy(mixer_out, mixer_to, marks.at[9]),
        pltpu.make_async_copy(fresh_out, fresh_to, marks.at[10]),
    ]
    for copy in loads:
        copy.start()
    for copy in loads:
        copy.wait()
    strict, levels, eye = block_masks()
    def prepare(group, _):
        work = []
        for lane in range(UNROLL):
            b = group * UNROLL + lane
            here = rows_of(b)
            source = place[b]
            before = place[jnp.maximum(b - 1, 0)]
            current = pre[rows_of(source), :MIXED].astype(F32)
            edge = pre[
                pl.ds(pl.multiple_of(before * BLOCK + BLOCK - 16, 16), 16), :MIXED
            ].astype(F32)
            extended = jnp.concatenate([edge[8:], current], axis=0)
            mixed = taps[0:1] * current
            for lag in range(1, CONV):
                mixed = mixed + (taps[lag : lag + 1] * cols[here, 1 + lag : 2 + lag]) * pltpu.roll(
                    extended, lag, 0
                )[8:]
            mixed_out[here, :] = mixed
            _, act, query, key, _, _ = units_of(mixed)
            query, key, value = query.astype(BF16), key.astype(BF16), act[:, 2 * KEY_SIZE :].astype(BF16)
            beta, beta_row = beta_columns(pre[rows_of(source), LOGIT:])
            link = decay_grid[b] * beta_row
            system = jnp.where(strict, link * mm(key, key, NT), 0.0)
            mixing = (SCALE * mm(query, key, NT)) * link
            work.append((b, here, query, key, value, beta, system, mixing))
        inverses = unit_lower_inverses([item[6] for item in work], levels, eye)
        for (b, here, query, key, value, beta, system, mixing), inverse in zip(work, inverses):
            inverse_out[here, :] = inverse
            carry = cols[here, 0:1]
            tail = cols[here, 1:2] * beta
            fresh_values = mm_left(inverse, value)
            fresh_keys = mm_left(inverse * rows[b, 0:1, :], key)
            low_mixing = mixing.astype(BF16)
            read = (SCALE * carry) * query.astype(F32) - mm(low_mixing, fresh_keys.astype(BF16))
            value_part[here, :] = fresh_values
            out_part[here, :] = mm(low_mixing, fresh_values.astype(BF16))
            read_out[here, :] = read.astype(BF16)
            both_maps[b, :BLOCK] = read.astype(BF16)
            both_maps[b, BLOCK:] = fresh_keys.astype(BF16)
            carry_out[b] = mm_right(key, tail * fresh_keys, TN).astype(BF16)
            add_part[b] = mm_right(key, tail * fresh_values, TN)
        return 0

    lax.fori_loop(0, blocks // UNROLL, prepare, 0)
    for copy in prepared:
        copy.start()

    def chain(b, state):
        low = state.astype(BF16)
        state_out[b] = low
        carry = cols[pl.ds(pl.multiple_of(b * BLOCK + BLOCK - 8, 8), 8), 0:1][7:]
        return carry * state + (add_part[b] - mm(carry_out[b], low))

    lax.fori_loop(0, blocks, chain, jnp.zeros((KEY_SIZE, DV), F32), unroll=8)
    for copy in chained:
        copy.start()

    def finish(group, _):
        for lane in range(UNROLL):
            b = group * UNROLL + lane
            here = rows_of(b)
            source = place[b]
            both = mm(both_maps[b], state_out[b])
            produced = both[:BLOCK] + out_part[here, :]
            fresh_out[here, :] = (value_part[here, :] - both[BLOCK:]).astype(BF16)
            mixer_out[here, :] = produced
            scale = lax.rsqrt(jnp.mean(produced * produced, axis=-1, keepdims=True) + EPSILON)
            gate = pre[rows_of(source), MIXED:LOGIT].astype(F32)
            gated[rows_of(source), :] = (
                produced * scale * head_gain[0:1] * (gate * jax.nn.sigmoid(gate))
            ).astype(BF16)
        return 0

    lax.fori_loop(0, blocks // UNROLL, finish, 0)
    for copy in finished:
        copy.start()
    for copy in prepared + chained + finished:
        copy.wait()


def backward_kernel(
    place,
    d_gated_own,
    d_gated_other,
    pre_own,
    pre_other,
    decay_grid,
    cols,
    taps,
    head_gain,
    mixer_from,
    mixed_from,
    inverse_from,
    state_from,
    fresh_from,
    carry_from,
    read_from,
    d_pre_own,
    d_pre_other,
    grad_taps,
    grad_gain,
    mixer_out,
    mixed_in,
    inverse_in,
    state_in,
    fresh_in,
    carry_in,
    read_in,
    d_out,
    pull_part,
    end_state,
    d_mixed,
    d_gated,
    pre,
    d_main,
    d_gating,
    d_logits,
    marks,
):
    blocks = decay_grid.shape[0]
    half = pre_own.shape[0]
    first_loads = [
        pltpu.make_async_copy(pre_own, pre.at[:half], marks.at[0]),
        pltpu.make_async_copy(pre_other, pre.at[half:], marks.at[1]),
        pltpu.make_async_copy(d_gated_own, d_gated.at[:half], marks.at[2]),
        pltpu.make_async_copy(d_gated_other, d_gated.at[half:], marks.at[3]),
        pltpu.make_async_copy(mixer_from, mixer_out, marks.at[4]),
        pltpu.make_async_copy(read_from, read_in, marks.at[5]),
    ]
    chain_loads = [pltpu.make_async_copy(carry_from, carry_in, marks.at[6])]
    late_loads = [
        pltpu.make_async_copy(mixed_from, mixed_in, marks.at[7]),
        pltpu.make_async_copy(inverse_from, inverse_in, marks.at[8]),
        pltpu.make_async_copy(state_from, state_in, marks.at[9]),
        pltpu.make_async_copy(fresh_from, fresh_in, marks.at[10]),
    ]

    def stores(source, columns, mark):
        return [
            pltpu.make_async_copy(source.at[:half], d_pre_own.at[:, columns], marks.at[mark]),
            pltpu.make_async_copy(source.at[half:], d_pre_other.at[:, columns], marks.at[mark + 1]),
        ]

    gating_stores = stores(d_gating, slice(MIXED, LOGIT), 11)
    logit_stores = stores(d_logits, slice(LOGIT, PACK), 13)
    main_stores = stores(d_main, slice(0, MIXED), 15)
    for copy in first_loads + chain_loads + late_loads:
        copy.start()
    for copy in first_loads:
        copy.wait()
    strict, _, _ = block_masks()
    lane_index = lax.broadcasted_iota(jnp.int32, (BLOCK, PACK - LOGIT), 1)
    grad_taps[...] = jnp.zeros_like(grad_taps)
    grad_gain[...] = jnp.zeros_like(grad_gain)
    d_mixed[blocks * BLOCK :, :] = jnp.zeros((8, MIXED), F32)

    def prepare(group, _):
        for lane in range(UNROLL):
            b = group * UNROLL + lane
            here = rows_of(b)
            there = rows_of(place[b])
            grad = d_gated[there, :].astype(F32)
            gate = pre[there, MIXED:LOGIT].astype(F32)
            produced = mixer_out[here, :]
            scale = lax.rsqrt(jnp.mean(produced * produced, axis=-1, keepdims=True) + EPSILON)
            normed = produced * scale
            sig = jax.nn.sigmoid(gate)
            act = gate * sig
            weighted = grad * head_gain[0:1]
            pulled = weighted * act
            along = jnp.mean(pulled * normed, axis=-1, keepdims=True)
            low = (scale * (pulled - normed * along)).astype(BF16)
            grad_gain[...] += row_sums(grad * normed * act)
            d_gating[there, :] = (
                weighted * normed * (sig * (1.0 + gate * (1.0 - sig)))
            ).astype(BF16)
            d_out[here, :] = low
            pull_part[b] = mm(read_in[here, :], low, TN)
        return 0

    lax.fori_loop(0, blocks // UNROLL, prepare, 0)
    for copy in gating_stores:
        copy.start()
    for copy in chain_loads:
        copy.wait()

    def chain(step, state):
        b = blocks - 1 - step
        low = state.astype(BF16)
        end_state[b] = low
        carry = cols[pl.ds(pl.multiple_of(b * BLOCK + BLOCK - 8, 8), 8), 0:1][7:]
        return carry * state + (pull_part[b] - mm(carry_in[b], low, TN))

    lax.fori_loop(0, blocks, chain, jnp.zeros((KEY_SIZE, DV), F32), unroll=8)
    for copy in late_loads:
        copy.wait()

    def finish(group, _):
        for lane in range(UNROLL):
            b = group * UNROLL + lane
            here = rows_of(b)
            there = rows_of(place[b])
            mixed = mixed_in[here, :]
            gate, act, query_unit, key_unit, query_scale, key_scale = units_of(mixed)
            query, key = query_unit.astype(BF16), key_unit.astype(BF16)
            beta, beta_row = beta_columns(pre[there, LOGIT:])
            link = decay_grid[b] * beta_row
            mixing = (SCALE * mm(query, key, NT)) * link
            carry = cols[here, 0:1]
            tail = cols[here, 1:2] * beta
            low = d_out[here, :]
            end = end_state[b]
            start = state_in[b]
            fresh = fresh_in[here, :]
            d_fresh = mm(mixing.astype(BF16), low, TN) + tail * mm(key, end)
            d_right = mm_left(inverse_in[here, :], d_fresh.astype(BF16), TN)
            d_right_low = d_right.astype(BF16)
            d_logit = (1.0 - beta) * jnp.sum(fresh.astype(F32) * d_right, axis=-1, keepdims=True)
            pair = jnp.concatenate([low, d_right_low], axis=0)
            on_state = mm(pair, start, NT)
            on_fresh = mm(pair, fresh, NT)
            read_grad = (SCALE * on_fresh[:BLOCK]) * link
            system_grad = jnp.where(strict, -on_fresh[BLOCK:] * link, 0.0)
            d_query = (SCALE * carry) * on_state[:BLOCK] + mm(read_grad.astype(BF16), key)
            d_key = (
                mm((system_grad + system_grad.T).astype(BF16), key)
                + mm(read_grad.astype(BF16), query, TN)
                + tail * mm(fresh, end, NT)
                - carry * on_state[BLOCK:]
            )
            d_query = d_query.astype(BF16).astype(F32)
            d_key = d_key.astype(BF16).astype(F32)
            slope = gate * (1.0 + mixed * (1.0 - gate))
            d_mixed[here, :KEY_SIZE] = (
                d_query - query_unit * jnp.sum(query_unit * d_query, axis=-1, keepdims=True)
            ) * (query_scale * slope[:, :KEY_SIZE])
            d_mixed[here, KEY_SIZE : 2 * KEY_SIZE] = (
                d_key - key_unit * jnp.sum(key_unit * d_key, axis=-1, keepdims=True)
            ) * (key_scale * slope[:, KEY_SIZE : 2 * KEY_SIZE])
            d_mixed[here, 2 * KEY_SIZE :] = d_right_low.astype(F32) * slope[:, 2 * KEY_SIZE :]
            d_logits[there, :] = jnp.where(lane_index == 0, d_logit, 0.0).astype(BF16)
        return 0

    lax.fori_loop(0, blocks // UNROLL, finish, 0)
    for copy in logit_stores:
        copy.start()

    def unmix(group, _):
        for lane in range(UNROLL):
            b = group * UNROLL + lane
            there = rows_of(place[b])
            longer = pl.ds(pl.multiple_of(b * BLOCK, BLOCK), BLOCK + 8)
            extended = d_mixed[longer, :]
            current = pre[there, :MIXED].astype(F32)
            total = taps[0:1] * extended[:BLOCK]
            grad_taps[0] += row_sums(current * extended[:BLOCK])
            for lag in range(1, CONV):
                kept = cols[longer, 1 + lag : 2 + lag] * extended
                moved = pltpu.roll(kept, BLOCK + 8 - lag, 0)[:BLOCK]
                total = total + taps[lag : lag + 1] * moved
                grad_taps[lag] += row_sums(current * moved)
            d_main[there, :] = total.astype(BF16)
        return 0

    lax.fori_loop(0, blocks // UNROLL, unmix, 0)
    for copy in main_stores:
        copy.start()
    for copy in gating_stores + logit_stores + main_stores:
        copy.wait()


VMEM_SPEC = pl.BlockSpec(memory_space=pltpu.VMEM)
SMEM_SPEC = pl.BlockSpec(memory_space=pltpu.SMEM)
ANY_SPEC = pl.BlockSpec(memory_space=pl.ANY)
FORWARD_COST = pl.CostEstimate(flops=30_000_000_000, bytes_accessed=100_000_000, transcendentals=0)
SMALL_COST = pl.CostEstimate(flops=1_000_000, bytes_accessed=1_000, transcendentals=0)


def mixer_forward(place, pre_own, pre_other, decay_grid, cols, rows, taps, head_gain):
    blocks = decay_grid.shape[0]
    half, tokens = pre_own.shape[0], blocks * BLOCK
    shape = jax.ShapeDtypeStruct
    return pl.pallas_call(
        forward_kernel,
        out_shape=(
            shape((half, DV), BF16),
            shape((half, DV), BF16),
            shape((tokens, DV), F32),
            shape((tokens, MIXED), F32),
            shape((tokens, BLOCK), F32),
            shape((blocks, KEY_SIZE, DV), BF16),
            shape((tokens, DV), BF16),
            shape((blocks, KEY_SIZE, KEY_SIZE), BF16),
            shape((tokens, KEY_SIZE), BF16),
        ),
        in_specs=[SMEM_SPEC] + [ANY_SPEC] * 2 + [VMEM_SPEC] * 5,
        out_specs=[ANY_SPEC] * 9,
        scratch_shapes=[
            pltpu.VMEM((tokens, DV), F32),
            pltpu.VMEM((tokens, MIXED), F32),
            pltpu.VMEM((tokens, BLOCK), F32),
            pltpu.VMEM((blocks, KEY_SIZE, DV), BF16),
            pltpu.VMEM((tokens, DV), BF16),
            pltpu.VMEM((blocks, KEY_SIZE, KEY_SIZE), BF16),
            pltpu.VMEM((tokens, KEY_SIZE), BF16),
            pltpu.VMEM((blocks, 2 * BLOCK, KEY_SIZE), BF16),
            pltpu.VMEM((tokens, DV), F32),
            pltpu.VMEM((tokens, DV), F32),
            pltpu.VMEM((blocks, KEY_SIZE, DV), F32),
            pltpu.VMEM((tokens, PACK), BF16),
            pltpu.VMEM((tokens, DV), BF16),
            pltpu.SemaphoreType.DMA((11,)),
        ],
        compiler_params=pltpu.CompilerParams(vmem_limit_bytes=52 * 1024 * 1024),
        cost_estimate=FORWARD_COST,
        name="mixer_forward",
    )(place, pre_own, pre_other, decay_grid, cols, rows, taps, head_gain)


def mixer_backward(place, d_gated, pre, decay_grid, cols, taps, head_gain, kept):
    blocks = decay_grid.shape[0]
    half, tokens = pre[0].shape[0], blocks * BLOCK
    shape = jax.ShapeDtypeStruct
    return pl.pallas_call(
        backward_kernel,
        out_shape=(
            shape((half, PACK), BF16),
            shape((half, PACK), BF16),
            shape((CONV, 8, MIXED), F32),
            shape((8, DV), F32),
        ),
        in_specs=[SMEM_SPEC] + [ANY_SPEC] * 4 + [VMEM_SPEC] * 4 + [ANY_SPEC] * 7,
        out_specs=[ANY_SPEC] * 2 + [VMEM_SPEC] * 2,
        scratch_shapes=[
            pltpu.VMEM((tokens, DV), F32),
            pltpu.VMEM((tokens, MIXED), F32),
            pltpu.VMEM((tokens, BLOCK), F32),
            pltpu.VMEM((blocks, KEY_SIZE, DV), BF16),
            pltpu.VMEM((tokens, DV), BF16),
            pltpu.VMEM((blocks, KEY_SIZE, KEY_SIZE), BF16),
            pltpu.VMEM((tokens, KEY_SIZE), BF16),
            pltpu.VMEM((tokens, DV), BF16),
            pltpu.VMEM((blocks, KEY_SIZE, DV), F32),
            pltpu.VMEM((blocks, KEY_SIZE, DV), BF16),
            pltpu.VMEM((tokens + 8, MIXED), F32),
            pltpu.VMEM((tokens, DV), BF16),
            pltpu.VMEM((tokens, PACK), BF16),
            pltpu.VMEM((tokens, MIXED), BF16),
            pltpu.VMEM((tokens, DV), BF16),
            pltpu.VMEM((tokens, PACK - LOGIT), BF16),
            pltpu.SemaphoreType.DMA((17,)),
        ],
        compiler_params=pltpu.CompilerParams(vmem_limit_bytes=52 * 1024 * 1024),
        cost_estimate=SMALL_COST,
        name="mixer_backward",
    )(place, *d_gated, *pre, decay_grid, cols, taps, head_gain, *kept)


def stream_tables(rate, starts):
    blocks = rate.shape[0] // BLOCK
    level = jnp.cumsum(jnp.log(rate).reshape(blocks, BLOCK), axis=-1)
    segment = jnp.cumsum(starts.reshape(blocks, BLOCK), axis=-1)
    positions = jnp.arange(BLOCK)
    causal = positions[:, None] >= positions[None, :]
    linked = (segment[:, :, None] == segment[:, None, :]) & causal
    spread = jnp.where(causal, level[:, :, None] - level[:, None, :], 0.0)
    decay_grid = jnp.where(linked, jnp.exp(spread), 0.0)
    carry = jnp.where(segment == 0, jnp.exp(level), 0.0)
    tail = decay_grid[:, BLOCK - 1, :]
    keep = 1.0 - starts
    padded = jnp.concatenate([jnp.zeros((2,), F32), keep])
    keep_two = keep * padded[1:-1]
    keep_three = keep_two * padded[:-2]
    zero = jnp.zeros_like(keep)
    cols = jnp.stack([carry.reshape(-1), tail.reshape(-1), keep, keep_two, keep_three, zero, zero, zero], axis=1)
    cols = jnp.concatenate([cols, jnp.zeros((8, 8), F32)], axis=0)
    rows = jnp.broadcast_to(carry[:, None, :], (blocks, 8, BLOCK))
    return decay_grid, cols, rows


def unpack_kernel(
    grads, gain, w_query, w_key, w_value, w_gating, w_beta, query, key, value, gating, beta, gain_part
):
    heads = grads.shape[0]
    scale = gain[...]
    total = jnp.zeros((grads.shape[1], 128), F32)

    def lane_sums(values):
        part = values[:, :128]
        for start in range(128, values.shape[1], 128):
            part = part + values[:, start : start + 128]
        return part

    columns = []
    for head in range(heads):
        start = 0
        for out, weights, size in (
            (query, w_query, KEY_SIZE),
            (key, w_key, KEY_SIZE),
            (value, w_value, DV),
            (gating, w_gating, DV),
        ):
            place = slice(head * size, (head + 1) * size)
            part = grads[head, :, start : start + size].astype(F32)
            out[:, place] = part * scale
            total = total + lane_sums(part * weights[:, place].astype(F32))
            start += size
        columns.append(grads[head, :, LOGIT : LOGIT + 1].astype(F32))
    columns = jnp.concatenate(columns, axis=1)
    beta[...] = columns * scale
    gain_part[...] = jnp.sum(total, axis=1, keepdims=True) + jnp.sum(
        columns * w_beta[...].astype(F32), axis=1, keepdims=True
    )


def unpack_heads(grads, gain, w_query, w_key, w_value, w_gating, w_beta):
    shape = jax.ShapeDtypeStruct
    weights = (w_query, w_key, w_value, w_gating, w_beta)
    query, key, value, gating, beta, gain_part = pl.pallas_call(
        unpack_kernel,
        out_shape=tuple(shape(w.shape, F32) for w in weights) + (shape((gain.shape[0], 1), F32),),
        in_specs=[VMEM_SPEC] * 7,
        out_specs=[VMEM_SPEC] * 6,
        compiler_params=pltpu.CompilerParams(vmem_limit_bytes=32 * 1024 * 1024),
        cost_estimate=SMALL_COST,
        name="unpack_heads",
    )(grads, gain, *weights)
    return query, key, value, gating, beta, gain_part[:, 0]


def pack_kernel(
    core, gain, w_beta, rates, starts, *refs
):
    sources, (kept, given), copies, marks = refs[:5], refs[5:7], refs[7:12], refs[12]
    loads = [
        pltpu.make_async_copy(source, copy, marks.at[index])
        for index, (source, copy) in enumerate(zip(sources, copies))
    ]
    for load in loads:
        load.start()
    for load in loads:
        load.wait()
    w_query, w_key, w_value, w_gating, w_output = copies
    heads = kept.shape[0]
    half = kept.shape[1]
    first = core[0] == 0
    scale = gain[...]
    lanes = lax.broadcasted_iota(jnp.int32, (2 * half, 128), 1)
    blank = jnp.zeros((half - 8, 128), F32)

    def two_rows(values):
        right = lanes[: values.shape[0]] >= half
        return jnp.where(right, pltpu.roll(values, half, 1), 0.0), jnp.where(right, values, 0.0)

    rate = rates[...]
    high = rate.astype(BF16).astype(F32)
    middle = (rate - high).astype(BF16).astype(F32)
    notes = [*two_rows(high), *two_rows(middle), *two_rows(rate - high - middle)]
    start_rows = two_rows(jnp.broadcast_to(starts[...], (8, 2 * half)))

    def place(head, columns, values):
        low, high = values[:half], values[half:]
        kept[head, :, columns] = jnp.where(first, low, high).astype(BF16)
        given[head, :, columns] = jnp.where(first, high, low).astype(BF16)

    for head in range(heads):
        start = 0
        for weights, size in ((w_query, KEY_SIZE), (w_key, KEY_SIZE), (w_value, DV), (w_gating, DV)):
            part = weights[:, head * size : (head + 1) * size].astype(F32) * scale
            place(head, slice(start, start + size), part)
            start += size
        beta = w_beta[:, head : head + 1].astype(F32) * scale
        place(
            head, slice(PACK, PACK + DV), w_output[head * DV : (head + 1) * DV, :].astype(F32).T
        )
        note = [part[head : head + 1] for part in notes] + [part[:1] for part in start_rows]
        note = jnp.concatenate(note + [blank], axis=0)
        place(
            head, slice(LOGIT, PACK), jnp.where(lanes < 2, beta, 0.0) + jnp.concatenate([note, note], axis=0)
        )


def pack_heads(core, gain, w_query, w_key, w_value, w_gating, w_beta, w_output, rates, starts):
    rows = gain.shape[0]
    heads = w_query.shape[1] // KEY_SIZE
    wide = (w_query, w_key, w_value, w_gating, w_output)
    shape = jax.ShapeDtypeStruct((heads, rows // 2, PACK + DV), BF16)
    return pl.pallas_call(
        pack_kernel,
        out_shape=(shape, shape),
        in_specs=[SMEM_SPEC] + [VMEM_SPEC] * 4 + [ANY_SPEC] * 5,
        out_specs=[VMEM_SPEC] * 2,
        scratch_shapes=[pltpu.VMEM(w.shape, BF16) for w in wide] + [pltpu.SemaphoreType.DMA((5,))],
        compiler_params=pltpu.CompilerParams(vmem_limit_bytes=58 * 1024 * 1024),
        cost_estimate=SMALL_COST,
        name="pack_heads",
    )(core, gain, w_beta, rates, starts, *wide)


def join_kernel(*refs):
    *pieces, out = refs
    start = 0
    for piece in pieces:
        out[start : start + piece.shape[0]] = piece[...]
        start += piece.shape[0]


def joined_rows(pieces):
    rows, width = sum(piece.shape[0] for piece in pieces), pieces[0].shape[1]
    steps = 2

    def block(size):
        return pl.BlockSpec((size, width // steps), lambda step: (0, step))

    return pl.pallas_call(
        join_kernel,
        out_shape=jax.ShapeDtypeStruct((rows, width), pieces[0].dtype),
        grid=(steps,),
        in_specs=[block(piece.shape[0]) for piece in pieces],
        out_specs=block(rows),
        name="joined_rows",
    )(*pieces)


CHIPS = 16
CORES = 2
BOTH = ("seq", "head")


def along_x(index):
    return index ^ 1


def along_y(index):
    return index ^ 2


def along_z(steps):
    return lambda index: (index + 4 * steps) % CHIPS


def send(value, target):
    return lax.ppermute(value, "seq", [(index, target(index)) for index in range(CHIPS)])


def swap_cores(value):
    return lax.ppermute(value, "head", [(0, 1), (1, 0)])


def exchange(pieces):
    return lax.all_to_all(pieces, "seq", split_axis=0, concat_axis=0, tiled=True)


def after(values, *earlier):
    return lax.optimization_barrier((values, earlier))[0]


def stacked(values):
    return jnp.concatenate(values, axis=0)


def total_of(*values):
    total = values[0].astype(F32)
    for value in values[1:]:
        total = total + value.astype(F32)
    return total


def gather_levels(block):
    return [block] + [send(block, along_z(steps)) for steps in (1, 2, 3)]


def send_near(block):
    return block, send(block, along_x), send(block, along_y)


def far_halves(near):
    _, from_x, from_y = near
    half = from_x.shape[0] // 2
    return from_y[:half], from_x[half:]


def send_far(halves):
    return send(halves[0], along_x), send(halves[1], along_y)


def by_planes(own, others):
    return stacked([piece for pair in zip(own, others) for part in pair for piece in part])


def four_blocks(near, far):
    return [near[0]], [near[1]], [near[2]], list(far)


def far_parts(parts):
    rows = parts.shape[0] // 8
    return parts[6 * rows : 7 * rows], parts[7 * rows :]


def near_parts(parts, low, high):
    rows = parts.shape[0] // 8
    for_x = stacked([parts[2 * rows : 3 * rows], total_of(parts[3 * rows : 4 * rows], high).astype(BF16)])
    for_y = stacked([total_of(parts[4 * rows : 5 * rows], low).astype(BF16), parts[5 * rows : 6 * rows]])
    return for_x, for_y


def send_parts(parts):
    return send(parts[0], along_x), send(parts[1], along_y)


def level_parts(parts, from_x, from_y):
    total = total_of(parts[: parts.shape[0] // 4], from_x, from_y)
    rows = total.shape[0] // 4
    return [total[:rows]] + [total[j * rows : (j + 1) * rows].astype(BF16) for j in (1, 2, 3)]


def send_levels(levels):
    return levels[:1] + [send(level, along_z(-j)) for j, level in zip((1, 2, 3), levels[1:])]


def nn(a, b):
    return mm(a, b)


def nt(a, b):
    return mm(a, b, NT)


def tn(a, b):
    return mm(a, b, TN)


def head_plan(
    inputs,
    doc_starts,
    decay_rate,
    mixer_gain,
    w_query,
    w_key,
    w_value,
    w_beta,
    w_gating,
    conv_query,
    conv_key,
    conv_value,
    head_gain,
    w_output,
    feed_gain,
    w_gate,
    w_up,
    w_down,
    cotangent,
):
    chip, core = lax.axis_index("seq"), lax.axis_index("head")
    first = core == 0
    tok_rows, width = inputs.shape
    half_rows = tok_rows // CORES
    row_count = w_query.shape[0]
    half_count = row_count // CORES
    head_count = w_query.shape[1] // KEY_SIZE
    units = w_gate.shape[1] // CHIPS
    own_count = CHIPS * half_rows

    def own_rows(values):
        return lax.dynamic_slice_in_dim(values, core * half_rows, half_rows, 0)

    def in_order(own, other, axis):
        return jnp.concatenate([jnp.where(first, own, other), jnp.where(first, other, own)], axis=axis)

    def split_by_core(pieces):
        kept = lax.dynamic_slice_in_dim(pieces, core * half_count, half_count, 1)
        given = lax.dynamic_slice_in_dim(pieces, (1 - core) * half_count, half_count, 1)
        return in_order(kept, swap_cores(given), 0)

    def joined_by_core(mine):
        both = in_order(mine[:, None], swap_cores(mine)[:, None], 1)
        return both.reshape(width, mine.shape[-1])

    inputs_own = own_rows(inputs).astype(F32)
    scale_one = lax.rsqrt(jnp.mean(inputs_own * inputs_own, axis=-1, keepdims=True) + EPSILON)
    normed_one = inputs_own * scale_one
    gain_one = mixer_gain.astype(F32)[:, None]
    gain_two = feed_gain.astype(F32)[:, None]

    in_kept, in_given = pack_heads(
        core.astype(jnp.int32)[None],
        gain_one,
        w_query,
        w_key,
        w_value,
        w_gating,
        w_beta,
        w_output,
        decay_rate.T,
        doc_starts.astype(F32)[None],
    )
    in_payload = in_order(in_kept, swap_cores(in_given), 0)
    one_levels = gather_levels(normed_one.astype(BF16))
    one_own = send_near(one_levels[0])
    one_own, one_levels = after((one_own, one_levels))
    in_mine = exchange(after(in_payload, one_levels))
    one_near, one_own_far = send_near(stacked(one_levels[1:])), send_far(far_halves(one_own))
    one_near, one_own_far, in_mine = after((one_near, one_own_far, in_mine))
    normed_all = by_planes(
        four_blocks(one_own, one_own_far), four_blocks(one_near, send_far(far_halves(one_near)))
    )
    weights_all = joined_by_core(in_mine)
    weights_in, weights_out = weights_all[:, :PACK], weights_all[:, PACK:]

    taps_here = jnp.concatenate(
        [
            conv_query.reshape(CONV, head_count, KEY_SIZE),
            conv_key.reshape(CONV, head_count, KEY_SIZE),
            conv_value.reshape(CONV, head_count, DV),
        ],
        axis=2,
    ).transpose(1, 0, 2)
    taps_there = swap_cores(taps_here)
    taps = lax.dynamic_index_in_dim(
        jnp.where(chip // head_count == core, taps_here, taps_there), chip % head_count, 0, False
    ).astype(F32)
    taps = stacked([taps, jnp.zeros_like(taps)])
    gain_head = jnp.broadcast_to(head_gain.astype(F32)[None], (8, DV))
    seen = in_mine[:, :8, PACK - tok_rows // 2 : PACK].astype(F32).reshape(CHIPS, 4, tok_rows)
    rate = (seen[:, 0] + seen[:, 1] + seen[:, 2]).reshape(-1)
    starts = seen[:, 3].reshape(-1)
    decay_grid, cols, rows = stream_tables(rate, starts)

    blocks = jnp.arange(CHIPS * CORES)
    far = blocks // CORES
    place = (
        4 * ((far ^ chip) % 4) + (chip // 4 - far // 4) % 4 + CHIPS * (blocks % CORES != core)
    ).astype(jnp.int32)

    raw = nn(normed_all, weights_in)
    column = lax.broadcasted_iota(jnp.int32, raw.shape, 1)
    pre_own = jnp.where(
        column == LOGIT + 1,
        raw - lax.reduce_precision(raw, exponent_bits=8, mantissa_bits=7),
        raw,
    ).astype(BF16)
    pre = (pre_own, swap_cores(pre_own))

    feed = jnp.concatenate(
        [
            (w_gate.astype(F32) * gain_two).astype(BF16).T.reshape(CHIPS, units, row_count),
            (w_up.astype(F32) * gain_two).astype(BF16).T.reshape(CHIPS, units, row_count),
            w_down.reshape(CHIPS, units, row_count),
        ],
        axis=1,
    )
    feed = after(feed, in_mine)
    feed_mine = exchange(feed)
    gated_own, gated_other, *kept = mixer_forward(place, *pre, decay_grid, cols, rows, taps, gain_head)
    mixed_parts = nt(gated_own, weights_out).astype(BF16)
    far = send_far(far_parts(mixed_parts))

    cot_own = own_rows(cotangent)
    far, feed_mine = after((far, feed_mine))
    near = near_parts(mixed_parts, *far)
    near, cot = send_parts(near), gather_levels(after(cot_own, near))
    feed_other = swap_cores(feed_mine)
    near, cot = after((near, cot))
    levels = level_parts(mixed_parts, *near)
    levels, cot = send_levels(levels), send_near(stacked(after(cot, levels)))

    levels, cot = after((levels, cot))
    middle = inputs_own + total_of(*levels)
    scale_two = lax.rsqrt(jnp.mean(middle * middle, axis=-1, keepdims=True) + EPSILON)
    normed_mid = middle * scale_two
    mid = normed_mid.astype(BF16)
    mid_sent, mid_own, cot_far = gather_levels(mid), send_near(mid), send_far(far_halves(after(cot, mid)))
    feed_mine, feed_other = after((feed_mine, feed_other), mid)

    def unit_rows(position):
        return stacked(
            [
                part[:, position * units : (position + 1) * units].transpose(1, 0, 2).reshape(units, width)
                for part in (feed_mine, feed_other)
            ]
        )

    gate_rows, up_rows, down_rows = unit_rows(0), unit_rows(1), unit_rows(2)
    mid = mid_sent
    mid, mid_own, cot_far, gate_rows, up_rows, down_rows = after(
        (mid, mid_own, cot_far, gate_rows, up_rows, down_rows)
    )
    mid = stacked(mid[1:])
    cot_all = stacked(after(cot, mid) + cot_far)
    mid, mid_own_far = send_near(mid), send_far(far_halves(mid_own))
    d_hidden = nt(cot_all, down_rows).astype(BF16)
    mid, mid_own_far, d_hidden = after((mid, mid_own_far, d_hidden))
    mid_all = by_planes(four_blocks(mid_own, mid_own_far), four_blocks(mid, send_far(far_halves(mid))))

    gate_lin = nt(mid_all, gate_rows)
    up_lin = nt(mid_all, up_rows)
    d_hidden = d_hidden.astype(F32)
    sig = jax.nn.sigmoid(gate_lin)
    act = gate_lin * sig
    hidden = (act * up_lin).astype(BF16)
    d_gate = (d_hidden * up_lin * (sig * (1.0 + gate_lin * (1.0 - sig)))).astype(BF16)
    d_up = (d_hidden * act).astype(BF16)
    e_parts = (nn(d_gate, gate_rows) + nn(d_up, up_rows)).astype(BF16)
    far = send_far(far_parts(e_parts))
    feed_parts = nn(after(hidden, e_parts), down_rows).astype(BF16)
    far, feed_parts = after((far, feed_parts))
    near = send_parts(near_parts(e_parts, *far))

    parts = [tn(d_gate, mid_all), tn(d_up, mid_all), tn(hidden, cot_all)]
    keep_part = stacked([part[:units] for part in parts])
    give_part = stacked([part[units:] for part in parts]).astype(BF16)
    cut = after(normed_all, e_parts).reshape(own_count, CHIPS, CORES, half_count)
    cut_mine = lax.dynamic_index_in_dim(cut, core, 2, False).reshape(own_count, width // CORES)
    cut_given = lax.dynamic_index_in_dim(cut, 1 - core, 2, False).reshape(own_count, width // CORES)
    near, feed_parts, keep_part, give_part, cut_mine, cut_given = after(
        (near, feed_parts, keep_part, give_part, cut_mine, cut_given)
    )
    cut_other = swap_cores(cut_given)
    levels = level_parts(e_parts, *near)
    levels, feed_far = send_levels(levels), send_far(far_parts(after(feed_parts, levels)))
    levels, feed_far = after((levels, feed_far))
    e_two = total_of(*levels)
    d_middle = cot_own.astype(F32) + scale_two * (
        e_two - normed_mid * jnp.mean(e_two * normed_mid, axis=-1, keepdims=True)
    )
    d_mid = d_middle.astype(BF16)
    d_mid, feed_near = gather_levels(d_mid), send_parts(near_parts(feed_parts, *after(feed_far, d_mid)))
    feed_grad = (keep_part + swap_cores(give_part).astype(F32)).astype(BF16)
    feed_grad = feed_grad.reshape(3 * units, CHIPS, row_count).transpose(1, 0, 2)
    feed_grad = jnp.pad(feed_grad, ((0, 0), (0, half_count * DV // row_count), (0, 0)))
    d_mid, feed_near, feed_grad = after((d_mid, feed_near, feed_grad))
    d_mid = stacked(d_mid)
    feed_levels = level_parts(feed_parts, *after(feed_near, d_mid))
    d_mid, feed_levels = send_near(d_mid), send_levels(feed_levels)
    d_mid, feed_levels = after((d_mid, feed_levels))
    d_mid_all = stacked(d_mid + send_far(far_halves(d_mid)))

    d_gated_own = nn(d_mid_all, weights_out).astype(BF16)
    d_gated = (d_gated_own, swap_cores(d_gated_own))
    grad_out = tn(d_mid_all, gated_own).astype(BF16).reshape(CHIPS, CORES, half_count, DV)
    grad_out = total_of(
        lax.dynamic_index_in_dim(grad_out, core, 1, False),
        swap_cores(lax.dynamic_index_in_dim(grad_out, 1 - core, 1, False)),
    ).astype(BF16)
    feed_grad = lax.dynamic_update_slice(
        feed_grad, grad_out.reshape(CHIPS, half_count * DV // row_count, row_count), (0, 3 * units, 0)
    )
    feed_back = exchange(feed_grad)
    d_pre_own, d_pre_other, grad_taps, grad_gain = mixer_backward(
        place, d_gated, pre, decay_grid, cols, taps, gain_head, kept
    )


    small = jnp.concatenate([jnp.sum(grad_taps, axis=1).reshape(-1), jnp.sum(grad_gain, axis=0)])
    small = small.reshape(-1, 64)
    small_rows = small.shape[0]
    grad_in = tn(cut_mine, d_pre_own) + tn(cut_other, d_pre_other)
    small = jnp.pad(small, ((0, half_count - small_rows), (PACK - 64, 0)))
    grad_in = (grad_in.reshape(CHIPS, half_count, PACK) + small).astype(BF16)
    grad_in, feed_back = after((grad_in, feed_back))
    e_parts = nt(after(d_pre_own, grad_in), weights_in).astype(BF16)
    grad_in = exchange(grad_in)
    near = send_parts(near_parts(e_parts, *send_far(far_parts(e_parts))))
    near, grad_in = after((near, grad_in))
    levels = level_parts(e_parts, *near)
    grad_in, feed_back = after((grad_in, feed_back), levels)
    e_levels = send_levels(levels)
    small = grad_in[:, :small_rows, PACK - 64 :].astype(F32).reshape(CHIPS, -1)
    taps_all = lax.dynamic_slice_in_dim(small[:, : CONV * MIXED], core * head_count, head_count, 0)
    taps_all = taps_all.reshape(head_count, CONV, MIXED).transpose(1, 0, 2)

    def heads_here(back):
        mine = lax.dynamic_slice_in_dim(back, core * head_count, head_count, 0)
        given = lax.dynamic_slice_in_dim(back, (1 - core) * head_count, head_count, 0)
        return in_order(mine, swap_cores(given), 1)

    grad_in = heads_here(grad_in)
    block_out_own = (middle + total_of(*feed_levels)).astype(BF16)
    block_out = in_order(block_out_own, swap_cores(block_out_own), 0)
    grad_out = heads_here(feed_back[:, 3 * units :].reshape(CHIPS, half_count, DV))
    grad_output = grad_out.astype(F32).transpose(0, 2, 1).reshape(head_count * DV, row_count)
    feed_back = feed_back[:, : 3 * units].astype(F32)
    raw_gate = feed_back[:, :units].reshape(CHIPS * units, row_count).T
    raw_up = feed_back[:, units : 2 * units].reshape(CHIPS * units, row_count).T
    grad_down = feed_back[:, 2 * units :].reshape(CHIPS * units, row_count)
    feed_gain_part = jnp.sum(raw_gate * w_gate.astype(F32) + raw_up * w_up.astype(F32), axis=1)

    raw_query, raw_key, raw_value, raw_gating, raw_beta, mixer_gain_part = unpack_heads(
        grad_in, gain_one, w_query, w_key, w_value, w_gating, w_beta
    )
    gain_parts = jnp.stack([mixer_gain_part, feed_gain_part])
    gain_totals = gain_parts + swap_cores(gain_parts)

    others = (
        gain_totals[0],
        raw_query,
        raw_key,
        raw_value,
        raw_beta,
        raw_gating,
        taps_all[:, :, :KEY_SIZE].reshape(CONV, head_count * KEY_SIZE),
        taps_all[:, :, KEY_SIZE : 2 * KEY_SIZE].reshape(CONV, head_count * KEY_SIZE),
        taps_all[:, :, 2 * KEY_SIZE :].reshape(CONV, head_count * DV),
        jnp.sum(small[:, CONV * MIXED :], axis=0),
        grad_output,
        gain_totals[1],
        raw_gate * gain_two,
        raw_up * gain_two,
        grad_down,
    )
    e_levels, block_out, others = after((e_levels, block_out, others))
    e_one = total_of(*e_levels)
    grad_own = d_middle + scale_one * (
        e_one - normed_one * jnp.mean(e_one * normed_one, axis=-1, keepdims=True)
    )
    grad_inputs = in_order(grad_own, swap_cores(grad_own), 0)
    return (block_out, grad_inputs) + others


EXACT_PRECISION = lax.Precision.HIGHEST


def passed_along(value, axis, steps):
    count = lax.axis_size(axis)
    first, last = (max(0, -steps), min(count, count - steps))
    return lax.ppermute(value, axis, [(source, source + steps) for source in range(first, last)])


def entering(value, axis, join, neutral):
    count, mine = (lax.axis_size(axis), lax.axis_index(axis))
    pieces = jax.tree.map(lambda part: lax.all_gather(part, axis), value)
    subtotal = jax.tree.map(
        lambda part, zero: jnp.full_like(part, 0) + jnp.asarray(zero, part.dtype), value, neutral
    )

    def lap(position, subtotal):
        longer = join(subtotal, jax.tree.map(lambda part: part[position], pieces))
        return jax.tree.map(lambda new, old: jnp.where(position < mine, new, old), longer, subtotal)

    return lax.fori_loop(0, count - 1, lap, subtotal)


def carried_in(shard, axis, join, neutral):
    count = lax.axis_size(axis)
    place = lax.axis_index(axis)
    ahead = count - 1 - place
    gathered = jax.tree.map(
        lambda a, kind: lax.all_gather(a.astype(kind), axis),
        shard,
        jax.tree.map(lambda a: jnp.bfloat16 if a.dtype == jnp.float32 else a.dtype, shard),
    )
    state = jax.tree.map(lambda a, e: jnp.zeros_like(a) + jnp.asarray(e, a.dtype), shard, neutral)

    def one(lap, state):
        source = count - 1 - lap
        return join(
            state,
            jax.tree.map(
                lambda a, own: lax.dynamic_index_in_dim(a, source, 0, False).astype(own.dtype),
                gathered,
                shard,
            ),
        )

    return lax.fori_loop(0, ahead, one, state)


def high_einsum(einsum_form, *arrays):
    return jnp.einsum(
        einsum_form, *arrays, precision=EXACT_PRECISION, preferred_element_type=jnp.float32
    )


def low_dot(left_side, right_side):
    return jnp.dot(left_side, right_side, preferred_element_type=jnp.float32)


def inner_dot(left_side, right_side):
    return lax.dot_general(
        left_side, right_side, (((0,), (0,)), ((), ())), preferred_element_type=jnp.float32
    )


def outer_dot(left_side, right_side):
    return lax.dot_general(
        left_side, right_side, (((1,), (1,)), ((), ())), preferred_element_type=jnp.float32
    )


def rounded(values):
    return lax.optimization_barrier(values.astype(jnp.bfloat16)).astype(jnp.float32)


def scale_norm(values, gain_vec):
    return (
        values * lax.rsqrt(jnp.mean(values * values, axis=-1, keepdims=True) + EPSILON) * gain_vec
    )


def unit_rows(values):
    return values * lax.rsqrt(jnp.sum(values * values, axis=-1, keepdims=True) + EPSILON)


def swiglu(gate_lin, up_lin):
    return jax.nn.silu(gate_lin) * up_lin


def compose_maps(earlier_map, later_map):
    return (
        high_einsum("hde,hef->hdf", later_map[0], earlier_map[0]),
        high_einsum("hde,hef->hdf", later_map[0], earlier_map[1]) + later_map[1],
    )


def gather_plan(
    inputs,
    doc_starts,
    decay_rate,
    mixer_gain,
    w_query,
    w_key,
    w_value,
    w_beta,
    w_gating,
    conv_query,
    conv_key,
    conv_value,
    head_gain,
    w_output,
    feed_gain,
    w_gate,
    w_up,
    w_down,
    cotangent,
):
    tok_rows = inputs.shape[0]
    head_count = decay_rate.shape[1]
    key_width = w_query.shape[1]
    value_width = w_value.shape[1]
    edge_count = CONV - 1
    block_count = tok_rows // BLOCK
    gathered = (
        lax.all_gather(mixer_gain, "seq", axis=0, tiled=True),
        lax.all_gather(w_query, "seq", axis=0, tiled=True),
        lax.all_gather(w_key, "seq", axis=0, tiled=True),
        lax.all_gather(w_value, "seq", axis=0, tiled=True),
        lax.all_gather(w_beta, "seq", axis=0, tiled=True),
        lax.all_gather(w_gating, "seq", axis=0, tiled=True),
        lax.all_gather(w_output, "seq", axis=1, tiled=True),
        lax.all_gather(feed_gain, "seq", axis=0, tiled=True),
        lax.all_gather(w_gate, "seq", axis=0, tiled=True),
        lax.all_gather(w_up, "seq", axis=0, tiled=True),
        lax.all_gather(w_down, "seq", axis=1, tiled=True),
    )
    (
        gain_one,
        full_query,
        full_key,
        full_value,
        full_beta,
        full_gating,
        full_output,
        gain_two,
        full_gate,
        full_up,
        full_down,
    ) = gathered
    inputs_float = inputs.astype(jnp.float32)
    normed_float, norm_one_back = jax.vjp(scale_norm, inputs_float, gain_one.astype(jnp.float32))
    normed_one = normed_float.astype(jnp.bfloat16)
    query_pre = low_dot(normed_one, full_query).astype(jnp.bfloat16)
    key_pre = low_dot(normed_one, full_key).astype(jnp.bfloat16)
    value_pre = low_dot(normed_one, full_value).astype(jnp.bfloat16)
    gating_pre = low_dot(normed_one, full_gating).astype(jnp.bfloat16)
    beta_logit = low_dot(normed_one, full_beta)
    joined = jnp.concatenate([query_pre, key_pre, value_pre], axis=1)
    tail_starts = doc_starts[tok_rows - edge_count :]
    later_starts = jnp.cumsum(tail_starts[::-1])[::-1] - tail_starts
    sender_keep = (later_starts == 0).astype(jnp.bfloat16)[:, None]
    edge_in = passed_along(joined[tok_rows - edge_count :] * sender_keep, "seq", 1)
    local_doc = jnp.cumsum(doc_starts)
    padded_doc = jnp.concatenate([jnp.zeros((edge_count,), local_doc.dtype), local_doc])
    keep_masks = [
        (
            padded_doc[edge_count - shift_lag : edge_count - shift_lag + tok_rows] == local_doc
        ).astype(jnp.float32)[:, None]
        for shift_lag in range(CONV)
    ]

    def conv_piece(extended, conv_weights):
        mixed = keep_masks[0] * conv_weights[0] * extended[edge_count:]
        for shift_lag in range(1, CONV):
            mixed = (
                mixed
                + keep_masks[shift_lag]
                * conv_weights[shift_lag]
                * extended[edge_count - shift_lag : edge_count - shift_lag + tok_rows]
            )
        activated = jax.nn.silu(mixed)
        query_unit = unit_rows(activated[:, :key_width].reshape(tok_rows, head_count, KEY_SIZE))
        key_unit = unit_rows(
            activated[:, key_width : 2 * key_width].reshape(tok_rows, head_count, KEY_SIZE)
        )
        value_act = activated[:, 2 * key_width :].reshape(tok_rows, head_count, DV)
        return (query_unit, key_unit, value_act)

    extended = jnp.concatenate([edge_in, joined], axis=0).astype(jnp.float32)
    conv_weights = jnp.concatenate([conv_query, conv_key, conv_value], axis=1).astype(jnp.float32)
    (query_unit, key_unit, value_act), conv_back = jax.vjp(conv_piece, extended, conv_weights)

    def to_blocks(values):
        return values.reshape(block_count, BLOCK, head_count, values.shape[-1]).transpose(
            0, 2, 1, 3
        )

    def from_blocks(values):
        return values.transpose(0, 2, 1, 3).reshape(tok_rows, head_count, values.shape[-1])

    log_rate = jnp.log(decay_rate).reshape(block_count, BLOCK, head_count).transpose(0, 2, 1)
    log_level = jnp.cumsum(log_rate, axis=-1)
    segment = jnp.cumsum(doc_starts.reshape(block_count, BLOCK), axis=-1)
    positions = jnp.arange(BLOCK)
    causal = positions[:, None] >= positions[None, :]
    strict = positions[:, None] > positions[None, :]
    linked = (segment[:, None, :, None] == segment[:, None, None, :]) & causal
    spread = jnp.where(causal, log_level[..., :, None] - log_level[..., None, :], 0.0)
    decay_grid = jnp.where(linked, jnp.exp(spread), 0.0)
    carry_in = jnp.where(segment[:, None, :] == 0, jnp.exp(log_level), 0.0)
    tail_decay = decay_grid[..., BLOCK - 1, :]
    key_eye = jnp.eye(KEY_SIZE, dtype=jnp.float32)
    block_eye = jnp.eye(BLOCK, dtype=jnp.float32)

    def block_terms(query_blocks, key_blocks, value_blocks, logit_blocks):
        beta_gate = jax.nn.sigmoid(logit_blocks)
        key_gram = high_einsum("nhcd,nhmd->nhcm", key_blocks, key_blocks)
        system = block_eye + jnp.where(strict, decay_grid * key_gram * beta_gate[..., None, :], 0.0)
        right_side = jnp.concatenate([value_blocks, carry_in[..., None] * key_blocks], axis=-1)
        solved = jax.scipy.linalg.solve_triangular(
            system, right_side, lower=True, unit_diagonal=True
        )
        fresh_values = solved[..., :DV]
        fresh_keys = solved[..., DV:]
        mixing = (
            high_einsum("nhcd,nhmd->nhcm", query_blocks, key_blocks)
            * decay_grid
            * beta_gate[..., None, :]
        )
        weighted = key_blocks * (tail_decay * beta_gate)[..., None]
        block_maps = carry_in[..., BLOCK - 1, None, None] * key_eye - high_einsum(
            "nhcd,nhce->nhde", weighted, fresh_keys
        )
        block_adds = high_einsum("nhcd,nhce->nhde", weighted, fresh_values)

        def chain_step(current, element):
            return (compose_maps(current, element), None)

        start_map = (
            jnp.broadcast_to(key_eye, (head_count, KEY_SIZE, KEY_SIZE)),
            jnp.zeros((head_count, KEY_SIZE, DV), jnp.float32),
        )
        device_pair, _ = lax.scan(chain_step, start_map, (block_maps, block_adds))
        return (
            (fresh_values, fresh_keys, mixing, block_maps, block_adds),
            device_pair[0],
            device_pair[1],
        )

    def block_outputs(block_parts, query_blocks, start_state):

        def step_block(current, element):
            fresh_values, fresh_keys, mixing, block_map, block_add, query_part, carry_part = element
            updated = fresh_values - high_einsum("hcd,hde->hce", fresh_keys, current)
            produced_output = (
                carry_part[..., None] * high_einsum("hcd,hde->hce", query_part, current)
                + high_einsum("hcm,hme->hce", mixing, updated)
            ) * KEY_SIZE ** (-0.5)
            return (high_einsum("hde,hef->hdf", block_map, current) + block_add, produced_output)

        _, emitted_all = lax.scan(step_block, start_state, block_parts + (query_blocks, carry_in))
        return emitted_all

    query_blocks = to_blocks(rounded(query_unit))
    key_blocks = to_blocks(rounded(key_unit))
    value_blocks = to_blocks(rounded(value_act))
    logit_blocks = beta_logit.reshape(block_count, BLOCK, head_count).transpose(0, 2, 1)
    (block_parts, device_map, device_add), terms_back = jax.vjp(
        block_terms, query_blocks, key_blocks, value_blocks, logit_blocks
    )
    identity = (jnp.broadcast_to(key_eye, device_map.shape), jnp.zeros_like(device_add))
    prefix = entering((device_map, device_add), "seq", compose_maps, identity)
    start_state = prefix[1]
    produced_output, emitted_back = jax.vjp(block_outputs, block_parts, query_blocks, start_state)

    def gated_norm(values, gating_values, gain_vec):
        normed_out = values * lax.rsqrt(jnp.mean(values * values, axis=-1, keepdims=True) + EPSILON)
        return (normed_out * gain_vec * jax.nn.silu(gating_values)).reshape(tok_rows, value_width)

    mixer_out = from_blocks(produced_output)
    gated_float, gated_back = jax.vjp(
        gated_norm,
        mixer_out,
        gating_pre.astype(jnp.float32).reshape(tok_rows, head_count, DV),
        head_gain.astype(jnp.float32),
    )
    gated_out = gated_float.astype(jnp.bfloat16)
    middle = inputs_float + lax.psum(
        low_dot(gated_out, full_output).astype(jnp.bfloat16), "head"
    ).astype(jnp.float32)
    normed_middle, norm_two_back = jax.vjp(scale_norm, middle, gain_two.astype(jnp.float32))
    normed_two = normed_middle.astype(jnp.bfloat16)
    gate_lin = low_dot(normed_two, full_gate)
    up_lin = low_dot(normed_two, full_up)
    hidden_float, swiglu_back = jax.vjp(swiglu, gate_lin, up_lin)
    hidden = hidden_float.astype(jnp.bfloat16)
    feed_out = lax.psum(low_dot(hidden, full_down).astype(jnp.bfloat16), "head").astype(jnp.float32)
    block_out = (middle + feed_out).astype(jnp.bfloat16)
    regathered = (
        lax.all_gather(w_query, "seq", axis=0, tiled=True),
        lax.all_gather(w_key, "seq", axis=0, tiled=True),
        lax.all_gather(w_value, "seq", axis=0, tiled=True),
        lax.all_gather(w_beta, "seq", axis=0, tiled=True),
        lax.all_gather(w_gating, "seq", axis=0, tiled=True),
        lax.all_gather(w_output, "seq", axis=1, tiled=True),
        lax.all_gather(w_gate, "seq", axis=0, tiled=True),
        lax.all_gather(w_up, "seq", axis=0, tiled=True),
        lax.all_gather(w_down, "seq", axis=1, tiled=True),
    )
    (
        full_query,
        full_key,
        full_value,
        full_beta,
        full_gating,
        full_output,
        full_gate,
        full_up,
        full_down,
    ) = regathered
    cotangent_float = cotangent.astype(jnp.float32)
    grad_down = inner_dot(hidden, cotangent)
    d_hidden = rounded(outer_dot(cotangent, full_down))
    d_gate_float, d_up_float = swiglu_back(d_hidden)
    d_gate = d_gate_float.astype(jnp.bfloat16)
    d_up = d_up_float.astype(jnp.bfloat16)
    grad_gate = inner_dot(normed_two, d_gate)
    grad_up = inner_dot(normed_two, d_up)
    d_normed_two = lax.psum(
        (outer_dot(d_gate, full_gate) + outer_dot(d_up, full_up)).astype(jnp.bfloat16), "head"
    ).astype(jnp.float32)
    d_middle_norm, grad_gain_two = norm_two_back(d_normed_two)
    d_middle = cotangent_float + d_middle_norm
    d_middle_low = d_middle.astype(jnp.bfloat16)
    grad_output = inner_dot(gated_out, d_middle_low)
    d_gated = rounded(outer_dot(d_middle_low, full_output))
    d_mixer_out, d_gating_float, grad_head_part = gated_back(d_gated)
    d_gating = d_gating_float.reshape(tok_rows, value_width).astype(jnp.bfloat16)
    d_parts, d_query_late, d_start = emitted_back(to_blocks(d_mixer_out))
    chained = carried_in((jnp.swapaxes(device_map, 1, 2), d_start), "seq", compose_maps, identity)
    d_end = chained[1]
    d_map = high_einsum("hde,hfe->hdf", d_end, start_state)
    d_query_early, d_key_blocks, d_value_blocks, d_logit_blocks = terms_back(
        (d_parts, d_map, d_end)
    )
    d_query_unit = rounded(from_blocks(d_query_early + d_query_late))
    d_key_unit = rounded(from_blocks(d_key_blocks))
    d_value_act = rounded(from_blocks(d_value_blocks))
    d_beta_logit = (
        d_logit_blocks.transpose(0, 2, 1).reshape(tok_rows, head_count).astype(jnp.bfloat16)
    )
    d_extended, grad_conv_all = conv_back((d_query_unit, d_key_unit, d_value_act))
    returned = passed_along(d_extended[:edge_count].astype(jnp.bfloat16), "seq", -1).astype(
        jnp.float32
    )
    d_rows = d_extended[edge_count:]
    d_rows = jnp.concatenate(
        [
            d_rows[: tok_rows - edge_count],
            d_rows[tok_rows - edge_count :] + returned * sender_keep.astype(jnp.float32),
        ],
        axis=0,
    )
    d_joined = d_rows.astype(jnp.bfloat16)
    d_query_pre = d_joined[:, :key_width]
    d_key_pre = d_joined[:, key_width : 2 * key_width]
    d_value_pre = d_joined[:, 2 * key_width :]
    grad_query = inner_dot(normed_one, d_query_pre)
    grad_key = inner_dot(normed_one, d_key_pre)
    grad_value = inner_dot(normed_one, d_value_pre)
    grad_gating = inner_dot(normed_one, d_gating)
    grad_beta = inner_dot(normed_one, d_beta_logit)
    d_normed_part = (
        outer_dot(d_query_pre, full_query)
        + outer_dot(d_key_pre, full_key)
        + outer_dot(d_value_pre, full_value)
        + outer_dot(d_gating, full_gating)
        + outer_dot(d_beta_logit, full_beta)
    )
    d_normed_one, head_total = (
        lax.psum(d_normed_part.astype(jnp.bfloat16), "head").astype(jnp.float32),
        lax.psum(grad_head_part.astype(jnp.bfloat16), "head").astype(jnp.float32),
    )
    d_inputs_norm, grad_gain_one = norm_one_back(d_normed_one)
    grad_inputs = d_middle + d_inputs_norm
    small_totals = lax.psum((grad_conv_all, head_total), "seq")
    conv_total = small_totals[0]
    totals = (
        lax.psum_scatter(grad_gain_one, "seq", scatter_dimension=0, tiled=True),
        lax.psum_scatter(grad_query, "seq", scatter_dimension=0, tiled=True),
        lax.psum_scatter(grad_key, "seq", scatter_dimension=0, tiled=True),
        lax.psum_scatter(grad_value, "seq", scatter_dimension=0, tiled=True),
        lax.psum_scatter(grad_beta, "seq", scatter_dimension=0, tiled=True),
        lax.psum_scatter(grad_gating, "seq", scatter_dimension=0, tiled=True),
        lax.psum_scatter(grad_output, "seq", scatter_dimension=1, tiled=True),
        lax.psum_scatter(grad_gain_two, "seq", scatter_dimension=0, tiled=True),
        lax.psum_scatter(grad_gate, "seq", scatter_dimension=0, tiled=True),
        lax.psum_scatter(grad_up, "seq", scatter_dimension=0, tiled=True),
        lax.psum_scatter(grad_down, "seq", scatter_dimension=1, tiled=True),
    )
    return (
        block_out,
        grad_inputs,
        totals[0],
        totals[1],
        totals[2],
        totals[3],
        totals[4],
        totals[5],
        conv_total[:, :key_width],
        conv_total[:, key_width : 2 * key_width],
        conv_total[:, 2 * key_width :],
        small_totals[1],
        totals[6],
        totals[7],
        totals[8],
        totals[9],
        totals[10],
    )


def solution(mesh):
    in_specs = (
        P("seq", None),
        P("seq"),
        P("seq", "head"),
        P("seq"),
        P("seq", "head"),
        P("seq", "head"),
        P("seq", "head"),
        P("seq", "head"),
        P("seq", "head"),
        P(None, "head"),
        P(None, "head"),
        P(None, "head"),
        P(),
        P("head", "seq"),
        P("seq"),
        P("seq", "head"),
        P("seq", "head"),
        P("head", "seq"),
        P("seq", None),
    )
    out_specs = (
        P("seq", None),
        P("seq", None),
        P("seq"),
        P("seq", "head"),
        P("seq", "head"),
        P("seq", "head"),
        P("seq", "head"),
        P("seq", "head"),
        P(None, "head"),
        P(None, "head"),
        P(None, "head"),
        P(),
        P("head", "seq"),
        P("seq"),
        P("seq", "head"),
        P("seq", "head"),
        P("head", "seq"),
    )
    whole_heads = mesh.shape["seq"] == CHIPS and mesh.shape["head"] == CORES
    per_device = head_plan if whole_heads else gather_plan
    return jax.shard_map(
        per_device, mesh=mesh, in_specs=in_specs, out_specs=out_specs, check_vma=False
    )
```

```python
import jax
import jax.numpy as jnp
from jax import lax
from jax.sharding import PartitionSpec as P
from jax.experimental import pallas as pl
from jax.experimental.pallas import tpu as pltpu

KEY_SIZE = 128
DV = 256
CONV = 4
BLOCK = 64
EPSILON = 1e-06
F32 = jnp.float32
BF16 = jnp.bfloat16
LOGIT = 2 * KEY_SIZE + 2 * DV
PACK = LOGIT + 128
MIXED = 2 * KEY_SIZE + DV
SCALE = KEY_SIZE**-0.5
UNROLL = 16


def mm(a, b, dims=((1,), (0,))):
    return lax.dot_general(a, b, (dims, ((), ())), preferred_element_type=F32)


NT = ((1,), (1,))
TN = ((0,), (0,))


def halves(a):
    high = a.astype(BF16)
    return high, (a - high.astype(F32)).astype(BF16)


def mm_left(a, b, dims=((1,), (0,))):
    high, low = halves(a)
    return mm(high, b, dims) + mm(low, b, dims)


def mm_right(a, b, dims=((1,), (0,))):
    high, low = halves(b)
    return mm(a, high, dims) + mm(a, low, dims)


def mm_both(a, b, dims=((1,), (0,))):
    a_high, a_low = halves(a)
    b_high, b_low = halves(b)
    return mm(a_high, b_high, dims) + (mm(a_high, b_low, dims) + mm(a_low, b_high, dims))


def block_masks():
    row = lax.broadcasted_iota(jnp.int32, (BLOCK, BLOCK), 0)
    col = lax.broadcasted_iota(jnp.int32, (BLOCK, BLOCK), 1)
    strict = row > col
    levels = []
    size = 1
    while size < BLOCK:
        levels.append(
            (row // (2 * size) == col // (2 * size)) & (row // size % 2 == 1) & (col // size % 2 == 0)
        )
        size *= 2
    return strict, levels, (row == col).astype(F32)


def unit_lower_inverses(systems, levels, eye):
    inverses = [eye - jnp.where(levels[0], system, 0.0) for system in systems]
    for level in levels[1:]:
        inner = [
            mm_both(jnp.where(level, system, 0.0), inverse)
            for system, inverse in zip(systems, inverses)
        ]
        inverses = [
            inverse - mm_both(inverse, part) for inverse, part in zip(inverses, inner)
        ]
    return inverses


def rows_of(index):
    return pl.ds(pl.multiple_of(index * BLOCK, BLOCK), BLOCK)


def row_sums(values):
    return jnp.sum(values.reshape(values.shape[0] // 8, 8, values.shape[1]), axis=0)


def beta_columns(packed):
    logit = packed[:, :1].astype(F32) + packed[:, 1:2].astype(F32)
    beta = jax.nn.sigmoid(logit)
    return beta, jnp.broadcast_to(beta, (BLOCK, 128)).T[:BLOCK]


def units_of(mixed):
    gate = jax.nn.sigmoid(mixed)
    act = mixed * gate
    query, key = act[:, :KEY_SIZE], act[:, KEY_SIZE : 2 * KEY_SIZE]
    query_scale = lax.rsqrt(jnp.sum(query * query, axis=-1, keepdims=True) + EPSILON)
    key_scale = lax.rsqrt(jnp.sum(key * key, axis=-1, keepdims=True) + EPSILON)
    return gate, act, query * query_scale, key * key_scale, query_scale, key_scale


def forward_kernel(
    place,
    pre_own,
    pre_other,
    decay_grid,
    cols,
    rows,
    taps,
    head_gain,
    gated_own,
    gated_other,
    mixer_to,
    mixed_to,
    inverse_to,
    state_to,
    fresh_to,
    carry_to,
    read_to,
    mixer_out,
    mixed_out,
    inverse_out,
    state_out,
    fresh_out,
    carry_out,
    read_out,
    both_maps,
    value_part,
    out_part,
    add_part,
    pre,
    gated,
    marks,
):
    blocks = decay_grid.shape[0]
    half = pre_own.shape[0]
    loads = [
        pltpu.make_async_copy(pre_own, pre.at[:half], marks.at[0]),
        pltpu.make_async_copy(pre_other, pre.at[half:], marks.at[1]),
    ]
    prepared = [
        pltpu.make_async_copy(mixed_out, mixed_to, marks.at[2]),
        pltpu.make_async_copy(inverse_out, inverse_to, marks.at[3]),
        pltpu.make_async_copy(carry_out, carry_to, marks.at[4]),
        pltpu.make_async_copy(read_out, read_to, marks.at[5]),
    ]
    chained = [pltpu.make_async_copy(state_out, state_to, marks.at[6])]
    finished = [
        pltpu.make_async_copy(gated.at[:half], gated_own, marks.at[7]),
        pltpu.make_async_copy(gated.at[half:], gated_other, marks.at[8]),
        pltpu.make_async_copy(mixer_out, mixer_to, marks.at[9]),
        pltpu.make_async_copy(fresh_out, fresh_to, marks.at[10]),
    ]
    for copy in loads:
        copy.start()
    for copy in loads:
        copy.wait()
    strict, levels, eye = block_masks()
    def prepare(group, _):
        work = []
        for lane in range(UNROLL):
            b = group * UNROLL + lane
            here = rows_of(b)
            source = place[b]
            before = place[jnp.maximum(b - 1, 0)]
            current = pre[rows_of(source), :MIXED].astype(F32)
            edge = pre[
                pl.ds(pl.multiple_of(before * BLOCK + BLOCK - 16, 16), 16), :MIXED
            ].astype(F32)
            extended = jnp.concatenate([edge[8:], current], axis=0)
            mixed = taps[0:1] * current
            for lag in range(1, CONV):
                mixed = mixed + (taps[lag : lag + 1] * cols[here, 1 + lag : 2 + lag]) * pltpu.roll(
                    extended, lag, 0
                )[8:]
            mixed_out[here, :] = mixed
            _, act, query, key, _, _ = units_of(mixed)
            query, key, value = query.astype(BF16), key.astype(BF16), act[:, 2 * KEY_SIZE :].astype(BF16)
            beta, beta_row = beta_columns(pre[rows_of(source), LOGIT:])
            link = decay_grid[b] * beta_row
            system = jnp.where(strict, link * mm(key, key, NT), 0.0)
            mixing = (SCALE * mm(query, key, NT)) * link
            work.append((b, here, query, key, value, beta, system, mixing))
        inverses = unit_lower_inverses([item[6] for item in work], levels, eye)
        for (b, here, query, key, value, beta, system, mixing), inverse in zip(work, inverses):
            inverse_out[here, :] = inverse
            carry = cols[here, 0:1]
            tail = cols[here, 1:2] * beta
            fresh_values = mm_left(inverse, value)
            fresh_keys = mm_left(inverse * rows[b, 0:1, :], key)
            low_mixing = mixing.astype(BF16)
            read = (SCALE * carry) * query.astype(F32) - mm(low_mixing, fresh_keys.astype(BF16))
            value_part[here, :] = fresh_values
            out_part[here, :] = mm(low_mixing, fresh_values.astype(BF16))
            read_out[here, :] = read.astype(BF16)
            both_maps[b, :BLOCK] = read.astype(BF16)
            both_maps[b, BLOCK:] = fresh_keys.astype(BF16)
            carry_out[b] = mm_right(key, tail * fresh_keys, TN).astype(BF16)
            add_part[b] = mm_right(key, tail * fresh_values, TN)
        return 0

    lax.fori_loop(0, blocks // UNROLL, prepare, 0)
    for copy in prepared:
        copy.start()

    def chain(b, state):
        low = state.astype(BF16)
        state_out[b] = low
        carry = cols[pl.ds(pl.multiple_of(b * BLOCK + BLOCK - 8, 8), 8), 0:1][7:]
        return carry * state + (add_part[b] - mm(carry_out[b], low))

    lax.fori_loop(0, blocks, chain, jnp.zeros((KEY_SIZE, DV), F32), unroll=8)
    for copy in chained:
        copy.start()

    def finish(group, _):
        for lane in range(UNROLL):
            b = group * UNROLL + lane
            here = rows_of(b)
            source = place[b]
            both = mm(both_maps[b], state_out[b])
            produced = both[:BLOCK] + out_part[here, :]
            fresh_out[here, :] = (value_part[here, :] - both[BLOCK:]).astype(BF16)
            mixer_out[here, :] = produced
            scale = lax.rsqrt(jnp.mean(produced * produced, axis=-1, keepdims=True) + EPSILON)
            gate = pre[rows_of(source), MIXED:LOGIT].astype(F32)
            gated[rows_of(source), :] = (
                produced * scale * head_gain[0:1] * (gate * jax.nn.sigmoid(gate))
            ).astype(BF16)
        return 0

    lax.fori_loop(0, blocks // UNROLL, finish, 0)
    for copy in finished:
        copy.start()
    for copy in prepared + chained + finished:
        copy.wait()


def backward_kernel(
    place,
    d_gated_own,
    d_gated_other,
    pre_own,
    pre_other,
    decay_grid,
    cols,
    taps,
    head_gain,
    mixer_from,
    mixed_from,
    inverse_from,
    state_from,
    fresh_from,
    carry_from,
    read_from,
    d_pre_own,
    d_pre_other,
    grad_taps,
    grad_gain,
    mixer_out,
    mixed_in,
    inverse_in,
    state_in,
    fresh_in,
    carry_in,
    read_in,
    d_out,
    pull_part,
    end_state,
    d_mixed,
    d_gated,
    pre,
    d_main,
    d_gating,
    d_logits,
    marks,
):
    blocks = decay_grid.shape[0]
    half = pre_own.shape[0]
    first_loads = [
        pltpu.make_async_copy(pre_own, pre.at[:half], marks.at[0]),
        pltpu.make_async_copy(pre_other, pre.at[half:], marks.at[1]),
        pltpu.make_async_copy(d_gated_own, d_gated.at[:half], marks.at[2]),
        pltpu.make_async_copy(d_gated_other, d_gated.at[half:], marks.at[3]),
        pltpu.make_async_copy(mixer_from, mixer_out, marks.at[4]),
        pltpu.make_async_copy(read_from, read_in, marks.at[5]),
    ]
    chain_loads = [pltpu.make_async_copy(carry_from, carry_in, marks.at[6])]
    late_loads = [
        pltpu.make_async_copy(mixed_from, mixed_in, marks.at[7]),
        pltpu.make_async_copy(inverse_from, inverse_in, marks.at[8]),
        pltpu.make_async_copy(state_from, state_in, marks.at[9]),
        pltpu.make_async_copy(fresh_from, fresh_in, marks.at[10]),
    ]

    def stores(source, columns, mark):
        return [
            pltpu.make_async_copy(source.at[:half], d_pre_own.at[:, columns], marks.at[mark]),
            pltpu.make_async_copy(source.at[half:], d_pre_other.at[:, columns], marks.at[mark + 1]),
        ]

    gating_stores = stores(d_gating, slice(MIXED, LOGIT), 11)
    logit_stores = stores(d_logits, slice(LOGIT, PACK), 13)
    main_stores = stores(d_main, slice(0, MIXED), 15)
    for copy in first_loads + chain_loads + late_loads:
        copy.start()
    for copy in first_loads:
        copy.wait()
    strict, _, _ = block_masks()
    lane_index = lax.broadcasted_iota(jnp.int32, (BLOCK, PACK - LOGIT), 1)
    grad_taps[...] = jnp.zeros_like(grad_taps)
    grad_gain[...] = jnp.zeros_like(grad_gain)
    d_mixed[blocks * BLOCK :, :] = jnp.zeros((8, MIXED), F32)

    def prepare(group, _):
        for lane in range(UNROLL):
            b = group * UNROLL + lane
            here = rows_of(b)
            there = rows_of(place[b])
            grad = d_gated[there, :].astype(F32)
            gate = pre[there, MIXED:LOGIT].astype(F32)
            produced = mixer_out[here, :]
            scale = lax.rsqrt(jnp.mean(produced * produced, axis=-1, keepdims=True) + EPSILON)
            normed = produced * scale
            sig = jax.nn.sigmoid(gate)
            act = gate * sig
            weighted = grad * head_gain[0:1]
            pulled = weighted * act
            along = jnp.mean(pulled * normed, axis=-1, keepdims=True)
            low = (scale * (pulled - normed * along)).astype(BF16)
            grad_gain[...] += row_sums(grad * normed * act)
            d_gating[there, :] = (
                weighted * normed * (sig * (1.0 + gate * (1.0 - sig)))
            ).astype(BF16)
            d_out[here, :] = low
            pull_part[b] = mm(read_in[here, :], low, TN)
        return 0

    lax.fori_loop(0, blocks // UNROLL, prepare, 0)
    for copy in gating_stores:
        copy.start()
    for copy in chain_loads:
        copy.wait()

    def chain(step, state):
        b = blocks - 1 - step
        low = state.astype(BF16)
        end_state[b] = low
        carry = cols[pl.ds(pl.multiple_of(b * BLOCK + BLOCK - 8, 8), 8), 0:1][7:]
        return carry * state + (pull_part[b] - mm(carry_in[b], low, TN))

    lax.fori_loop(0, blocks, chain, jnp.zeros((KEY_SIZE, DV), F32), unroll=8)
    for copy in late_loads:
        copy.wait()

    def finish(group, _):
        for lane in range(UNROLL):
            b = group * UNROLL + lane
            here = rows_of(b)
            there = rows_of(place[b])
            mixed = mixed_in[here, :]
            gate, act, query_unit, key_unit, query_scale, key_scale = units_of(mixed)
            query, key = query_unit.astype(BF16), key_unit.astype(BF16)
            beta, beta_row = beta_columns(pre[there, LOGIT:])
            link = decay_grid[b] * beta_row
            mixing = (SCALE * mm(query, key, NT)) * link
            carry = cols[here, 0:1]
            tail = cols[here, 1:2] * beta
            low = d_out[here, :]
            end = end_state[b]
            start = state_in[b]
            fresh = fresh_in[here, :]
            d_fresh = mm(mixing.astype(BF16), low, TN) + tail * mm(key, end)
            d_right = mm_left(inverse_in[here, :], d_fresh.astype(BF16), TN)
            d_right_low = d_right.astype(BF16)
            d_logit = (1.0 - beta) * jnp.sum(fresh.astype(F32) * d_right, axis=-1, keepdims=True)
            pair = jnp.concatenate([low, d_right_low], axis=0)
            on_state = mm(pair, start, NT)
            on_fresh = mm(pair, fresh, NT)
            read_grad = (SCALE * on_fresh[:BLOCK]) * link
            system_grad = jnp.where(strict, -on_fresh[BLOCK:] * link, 0.0)
            d_query = (SCALE * carry) * on_state[:BLOCK] + mm(read_grad.astype(BF16), key)
            d_key = (
                mm((system_grad + system_grad.T).astype(BF16), key)
                + mm(read_grad.astype(BF16), query, TN)
                + tail * mm(fresh, end, NT)
                - carry * on_state[BLOCK:]
            )
            d_query = d_query.astype(BF16).astype(F32)
            d_key = d_key.astype(BF16).astype(F32)
            slope = gate * (1.0 + mixed * (1.0 - gate))
            d_mixed[here, :KEY_SIZE] = (
                d_query - query_unit * jnp.sum(query_unit * d_query, axis=-1, keepdims=True)
            ) * (query_scale * slope[:, :KEY_SIZE])
            d_mixed[here, KEY_SIZE : 2 * KEY_SIZE] = (
                d_key - key_unit * jnp.sum(key_unit * d_key, axis=-1, keepdims=True)
            ) * (key_scale * slope[:, KEY_SIZE : 2 * KEY_SIZE])
            d_mixed[here, 2 * KEY_SIZE :] = d_right_low.astype(F32) * slope[:, 2 * KEY_SIZE :]
            d_logits[there, :] = jnp.where(lane_index == 0, d_logit, 0.0).astype(BF16)
        return 0

    lax.fori_loop(0, blocks // UNROLL, finish, 0)
    for copy in logit_stores:
        copy.start()

    def unmix(group, _):
        for lane in range(UNROLL):
            b = group * UNROLL + lane
            there = rows_of(place[b])
            longer = pl.ds(pl.multiple_of(b * BLOCK, BLOCK), BLOCK + 8)
            extended = d_mixed[longer, :]
            current = pre[there, :MIXED].astype(F32)
            total = taps[0:1] * extended[:BLOCK]
            grad_taps[0] += row_sums(current * extended[:BLOCK])
            for lag in range(1, CONV):
                kept = cols[longer, 1 + lag : 2 + lag] * extended
                moved = pltpu.roll(kept, BLOCK + 8 - lag, 0)[:BLOCK]
                total = total + taps[lag : lag + 1] * moved
                grad_taps[lag] += row_sums(current * moved)
            d_main[there, :] = total.astype(BF16)
        return 0

    lax.fori_loop(0, blocks // UNROLL, unmix, 0)
    for copy in main_stores:
        copy.start()
    for copy in gating_stores + logit_stores + main_stores:
        copy.wait()


VMEM_SPEC = pl.BlockSpec(memory_space=pltpu.VMEM)
SMEM_SPEC = pl.BlockSpec(memory_space=pltpu.SMEM)
ANY_SPEC = pl.BlockSpec(memory_space=pl.ANY)
FORWARD_COST = pl.CostEstimate(flops=30_000_000_000, bytes_accessed=100_000_000, transcendentals=0)
SMALL_COST = pl.CostEstimate(flops=1_000_000, bytes_accessed=1_000, transcendentals=0)


def mixer_forward(place, pre_own, pre_other, decay_grid, cols, rows, taps, head_gain):
    blocks = decay_grid.shape[0]
    half, tokens = pre_own.shape[0], blocks * BLOCK
    shape = jax.ShapeDtypeStruct
    return pl.pallas_call(
        forward_kernel,
        out_shape=(
            shape((half, DV), BF16),
            shape((half, DV), BF16),
            shape((tokens, DV), F32),
            shape((tokens, MIXED), F32),
            shape((tokens, BLOCK), F32),
            shape((blocks, KEY_SIZE, DV), BF16),
            shape((tokens, DV), BF16),
            shape((blocks, KEY_SIZE, KEY_SIZE), BF16),
            shape((tokens, KEY_SIZE), BF16),
        ),
        in_specs=[SMEM_SPEC] + [ANY_SPEC] * 2 + [VMEM_SPEC] * 5,
        out_specs=[ANY_SPEC] * 9,
        scratch_shapes=[
            pltpu.VMEM((tokens, DV), F32),
            pltpu.VMEM((tokens, MIXED), F32),
            pltpu.VMEM((tokens, BLOCK), F32),
            pltpu.VMEM((blocks, KEY_SIZE, DV), BF16),
            pltpu.VMEM((tokens, DV), BF16),
            pltpu.VMEM((blocks, KEY_SIZE, KEY_SIZE), BF16),
            pltpu.VMEM((tokens, KEY_SIZE), BF16),
            pltpu.VMEM((blocks, 2 * BLOCK, KEY_SIZE), BF16),
            pltpu.VMEM((tokens, DV), F32),
            pltpu.VMEM((tokens, DV), F32),
            pltpu.VMEM((blocks, KEY_SIZE, DV), F32),
            pltpu.VMEM((tokens, PACK), BF16),
            pltpu.VMEM((tokens, DV), BF16),
            pltpu.SemaphoreType.DMA((11,)),
        ],
        compiler_params=pltpu.CompilerParams(vmem_limit_bytes=52 * 1024 * 1024),
        cost_estimate=FORWARD_COST,
        name="mixer_forward",
    )(place, pre_own, pre_other, decay_grid, cols, rows, taps, head_gain)


def mixer_backward(place, d_gated, pre, decay_grid, cols, taps, head_gain, kept):
    blocks = decay_grid.shape[0]
    half, tokens = pre[0].shape[0], blocks * BLOCK
    shape = jax.ShapeDtypeStruct
    return pl.pallas_call(
        backward_kernel,
        out_shape=(
            shape((half, PACK), BF16),
            shape((half, PACK), BF16),
            shape((CONV, 8, MIXED), F32),
            shape((8, DV), F32),
        ),
        in_specs=[SMEM_SPEC] + [ANY_SPEC] * 4 + [VMEM_SPEC] * 4 + [ANY_SPEC] * 7,
        out_specs=[ANY_SPEC] * 2 + [VMEM_SPEC] * 2,
        scratch_shapes=[
            pltpu.VMEM((tokens, DV), F32),
            pltpu.VMEM((tokens, MIXED), F32),
            pltpu.VMEM((tokens, BLOCK), F32),
            pltpu.VMEM((blocks, KEY_SIZE, DV), BF16),
            pltpu.VMEM((tokens, DV), BF16),
            pltpu.VMEM((blocks, KEY_SIZE, KEY_SIZE), BF16),
            pltpu.VMEM((tokens, KEY_SIZE), BF16),
            pltpu.VMEM((tokens, DV), BF16),
            pltpu.VMEM((blocks, KEY_SIZE, DV), F32),
            pltpu.VMEM((blocks, KEY_SIZE, DV), BF16),
            pltpu.VMEM((tokens + 8, MIXED), F32),
            pltpu.VMEM((tokens, DV), BF16),
            pltpu.VMEM((tokens, PACK), BF16),
            pltpu.VMEM((tokens, MIXED), BF16),
            pltpu.VMEM((tokens, DV), BF16),
            pltpu.VMEM((tokens, PACK - LOGIT), BF16),
            pltpu.SemaphoreType.DMA((17,)),
        ],
        compiler_params=pltpu.CompilerParams(vmem_limit_bytes=52 * 1024 * 1024),
        cost_estimate=SMALL_COST,
        name="mixer_backward",
    )(place, *d_gated, *pre, decay_grid, cols, taps, head_gain, *kept)


def stream_tables(rate, starts):
    blocks = rate.shape[0] // BLOCK
    level = jnp.cumsum(jnp.log(rate).reshape(blocks, BLOCK), axis=-1)
    segment = jnp.cumsum(starts.reshape(blocks, BLOCK), axis=-1)
    positions = jnp.arange(BLOCK)
    causal = positions[:, None] >= positions[None, :]
    linked = (segment[:, :, None] == segment[:, None, :]) & causal
    spread = jnp.where(causal, level[:, :, None] - level[:, None, :], 0.0)
    decay_grid = jnp.where(linked, jnp.exp(spread), 0.0)
    carry = jnp.where(segment == 0, jnp.exp(level), 0.0)
    tail = decay_grid[:, BLOCK - 1, :]
    keep = 1.0 - starts
    padded = jnp.concatenate([jnp.zeros((2,), F32), keep])
    keep_two = keep * padded[1:-1]
    keep_three = keep_two * padded[:-2]
    zero = jnp.zeros_like(keep)
    cols = jnp.stack([carry.reshape(-1), tail.reshape(-1), keep, keep_two, keep_three, zero, zero, zero], axis=1)
    cols = jnp.concatenate([cols, jnp.zeros((8, 8), F32)], axis=0)
    rows = jnp.broadcast_to(carry[:, None, :], (blocks, 8, BLOCK))
    return decay_grid, cols, rows


def unpack_kernel(
    grads, gain, w_query, w_key, w_value, w_gating, w_beta, query, key, value, gating, beta, gain_part
):
    heads = grads.shape[0]
    scale = gain[...]
    total = jnp.zeros((grads.shape[1], 128), F32)

    def lane_sums(values):
        part = values[:, :128]
        for start in range(128, values.shape[1], 128):
            part = part + values[:, start : start + 128]
        return part

    columns = []
    for head in range(heads):
        start = 0
        for out, weights, size in (
            (query, w_query, KEY_SIZE),
            (key, w_key, KEY_SIZE),
            (value, w_value, DV),
            (gating, w_gating, DV),
        ):
            place = slice(head * size, (head + 1) * size)
            part = grads[head, :, start : start + size].astype(F32)
            out[:, place] = part * scale
            total = total + lane_sums(part * weights[:, place].astype(F32))
            start += size
        columns.append(grads[head, :, LOGIT : LOGIT + 1].astype(F32))
    columns = jnp.concatenate(columns, axis=1)
    beta[...] = columns * scale
    gain_part[...] = jnp.sum(total, axis=1, keepdims=True) + jnp.sum(
        columns * w_beta[...].astype(F32), axis=1, keepdims=True
    )


def unpack_heads(grads, gain, w_query, w_key, w_value, w_gating, w_beta):
    shape = jax.ShapeDtypeStruct
    weights = (w_query, w_key, w_value, w_gating, w_beta)
    query, key, value, gating, beta, gain_part = pl.pallas_call(
        unpack_kernel,
        out_shape=tuple(shape(w.shape, F32) for w in weights) + (shape((gain.shape[0], 1), F32),),
        in_specs=[VMEM_SPEC] * 7,
        out_specs=[VMEM_SPEC] * 6,
        compiler_params=pltpu.CompilerParams(vmem_limit_bytes=32 * 1024 * 1024),
        cost_estimate=SMALL_COST,
        name="unpack_heads",
    )(grads, gain, *weights)
    return query, key, value, gating, beta, gain_part[:, 0]


def pack_kernel(
    core, gain, w_beta, rates, starts, *refs
):
    sources, (kept, given), copies, marks = refs[:5], refs[5:7], refs[7:12], refs[12]
    loads = [
        pltpu.make_async_copy(source, copy, marks.at[index])
        for index, (source, copy) in enumerate(zip(sources, copies))
    ]
    for load in loads:
        load.start()
    for load in loads:
        load.wait()
    w_query, w_key, w_value, w_gating, w_output = copies
    heads = kept.shape[0]
    half = kept.shape[1]
    first = core[0] == 0
    scale = gain[...]
    lanes = lax.broadcasted_iota(jnp.int32, (2 * half, 128), 1)
    blank = jnp.zeros((half - 8, 128), F32)

    def two_rows(values):
        right = lanes[: values.shape[0]] >= half
        return jnp.where(right, pltpu.roll(values, half, 1), 0.0), jnp.where(right, values, 0.0)

    rate = rates[...]
    high = rate.astype(BF16).astype(F32)
    middle = (rate - high).astype(BF16).astype(F32)
    notes = [*two_rows(high), *two_rows(middle), *two_rows(rate - high - middle)]
    start_rows = two_rows(jnp.broadcast_to(starts[...], (8, 2 * half)))

    def place(head, columns, values):
        low, high = values[:half], values[half:]
        kept[head, :, columns] = jnp.where(first, low, high).astype(BF16)
        given[head, :, columns] = jnp.where(first, high, low).astype(BF16)

    for head in range(heads):
        start = 0
        for weights, size in ((w_query, KEY_SIZE), (w_key, KEY_SIZE), (w_value, DV), (w_gating, DV)):
            part = weights[:, head * size : (head + 1) * size].astype(F32) * scale
            place(head, slice(start, start + size), part)
            start += size
        beta = w_beta[:, head : head + 1].astype(F32) * scale
        place(
            head, slice(PACK, PACK + DV), w_output[head * DV : (head + 1) * DV, :].astype(F32).T
        )
        note = [part[head : head + 1] for part in notes] + [part[:1] for part in start_rows]
        note = jnp.concatenate(note + [blank], axis=0)
        place(
            head, slice(LOGIT, PACK), jnp.where(lanes < 2, beta, 0.0) + jnp.concatenate([note, note], axis=0)
        )


def pack_heads(core, gain, w_query, w_key, w_value, w_gating, w_beta, w_output, rates, starts):
    rows = gain.shape[0]
    heads = w_query.shape[1] // KEY_SIZE
    wide = (w_query, w_key, w_value, w_gating, w_output)
    shape = jax.ShapeDtypeStruct((heads, rows // 2, PACK + DV), BF16)
    return pl.pallas_call(
        pack_kernel,
        out_shape=(shape, shape),
        in_specs=[SMEM_SPEC] + [VMEM_SPEC] * 4 + [ANY_SPEC] * 5,
        out_specs=[VMEM_SPEC] * 2,
        scratch_shapes=[pltpu.VMEM(w.shape, BF16) for w in wide] + [pltpu.SemaphoreType.DMA((5,))],
        compiler_params=pltpu.CompilerParams(vmem_limit_bytes=58 * 1024 * 1024),
        cost_estimate=SMALL_COST,
        name="pack_heads",
    )(core, gain, w_beta, rates, starts, *wide)


def join_kernel(*refs):
    *pieces, out = refs
    start = 0
    for piece in pieces:
        out[start : start + piece.shape[0]] = piece[...]
        start += piece.shape[0]


def joined_rows(pieces):
    rows, width = sum(piece.shape[0] for piece in pieces), pieces[0].shape[1]
    steps = 2

    def block(size):
        return pl.BlockSpec((size, width // steps), lambda step: (0, step))

    return pl.pallas_call(
        join_kernel,
        out_shape=jax.ShapeDtypeStruct((rows, width), pieces[0].dtype),
        grid=(steps,),
        in_specs=[block(piece.shape[0]) for piece in pieces],
        out_specs=block(rows),
        name="joined_rows",
    )(*pieces)


CHIPS = 16
CORES = 2
BOTH = ("seq", "head")


def along_x(index):
    return index ^ 1


def along_y(index):
    return index ^ 2


def along_z(steps):
    return lambda index: (index + 4 * steps) % CHIPS


def send(value, target):
    return lax.ppermute(value, "seq", [(index, target(index)) for index in range(CHIPS)])


def swap_cores(value):
    return lax.ppermute(value, "head", [(0, 1), (1, 0)])


def exchange(pieces):
    return lax.all_to_all(pieces, "seq", split_axis=0, concat_axis=0, tiled=True)


def after(values, *earlier):
    return lax.optimization_barrier((values, earlier))[0]


def stacked(values):
    return jnp.concatenate(values, axis=0)


def total_of(*values):
    total = values[0].astype(F32)
    for value in values[1:]:
        total = total + value.astype(F32)
    return total


def gather_levels(block):
    return [block] + [send(block, along_z(steps)) for steps in (1, 2, 3)]


def send_near(block):
    return block, send(block, along_x), send(block, along_y)


def far_halves(near):
    _, from_x, from_y = near
    half = from_x.shape[0] // 2
    return from_y[:half], from_x[half:]


def send_far(halves):
    return send(halves[0], along_x), send(halves[1], along_y)


def by_planes(own, others):
    return stacked([piece for pair in zip(own, others) for part in pair for piece in part])


def four_blocks(near, far):
    return [near[0]], [near[1]], [near[2]], list(far)


def far_parts(parts):
    rows = parts.shape[0] // 8
    return parts[6 * rows : 7 * rows], parts[7 * rows :]


def near_parts(parts, low, high):
    rows = parts.shape[0] // 8
    for_x = stacked([parts[2 * rows : 3 * rows], total_of(parts[3 * rows : 4 * rows], high).astype(BF16)])
    for_y = stacked([total_of(parts[4 * rows : 5 * rows], low).astype(BF16), parts[5 * rows : 6 * rows]])
    return for_x, for_y


def send_parts(parts):
    return send(parts[0], along_x), send(parts[1], along_y)


def level_parts(parts, from_x, from_y):
    total = total_of(parts[: parts.shape[0] // 4], from_x, from_y)
    rows = total.shape[0] // 4
    return [total[:rows]] + [total[j * rows : (j + 1) * rows].astype(BF16) for j in (1, 2, 3)]


def send_levels(levels):
    return levels[:1] + [send(level, along_z(-j)) for j, level in zip((1, 2, 3), levels[1:])]


def nn(a, b):
    return mm(a, b)


def nt(a, b):
    return mm(a, b, NT)


def tn(a, b):
    return mm(a, b, TN)


def head_plan(
    inputs,
    doc_starts,
    decay_rate,
    mixer_gain,
    w_query,
    w_key,
    w_value,
    w_beta,
    w_gating,
    conv_query,
    conv_key,
    conv_value,
    head_gain,
    w_output,
    feed_gain,
    w_gate,
    w_up,
    w_down,
    cotangent,
):
    chip, core = lax.axis_index("seq"), lax.axis_index("head")
    first = core == 0
    tok_rows, width = inputs.shape
    half_rows = tok_rows // CORES
    row_count = w_query.shape[0]
    half_count = row_count // CORES
    head_count = w_query.shape[1] // KEY_SIZE
    units = w_gate.shape[1] // CHIPS
    own_count = CHIPS * half_rows

    def own_rows(values):
        return lax.dynamic_slice_in_dim(values, core * half_rows, half_rows, 0)

    def in_order(own, other, axis):
        return jnp.concatenate([jnp.where(first, own, other), jnp.where(first, other, own)], axis=axis)

    def split_by_core(pieces):
        kept = lax.dynamic_slice_in_dim(pieces, core * half_count, half_count, 1)
        given = lax.dynamic_slice_in_dim(pieces, (1 - core) * half_count, half_count, 1)
        return in_order(kept, swap_cores(given), 0)

    def joined_by_core(mine):
        both = in_order(mine[:, None], swap_cores(mine)[:, None], 1)
        return both.reshape(width, mine.shape[-1])

    inputs_own = own_rows(inputs).astype(F32)
    scale_one = lax.rsqrt(jnp.mean(inputs_own * inputs_own, axis=-1, keepdims=True) + EPSILON)
    normed_one = inputs_own * scale_one
    gain_one = mixer_gain.astype(F32)[:, None]
    gain_two = feed_gain.astype(F32)[:, None]

    in_kept, in_given = pack_heads(
        core.astype(jnp.int32)[None],
        gain_one,
        w_query,
        w_key,
        w_value,
        w_gating,
        w_beta,
        w_output,
        decay_rate.T,
        doc_starts.astype(F32)[None],
    )
    in_payload = in_order(in_kept, swap_cores(in_given), 0)
    one_levels = gather_levels(normed_one.astype(BF16))
    one_own = send_near(one_levels[0])
    one_own, one_levels = after((one_own, one_levels))
    in_mine = exchange(after(in_payload, one_levels))
    one_near, one_own_far = send_near(stacked(one_levels[1:])), send_far(far_halves(one_own))
    one_near, one_own_far, in_mine = after((one_near, one_own_far, in_mine))
    normed_all = by_planes(
        four_blocks(one_own, one_own_far), four_blocks(one_near, send_far(far_halves(one_near)))
    )
    weights_all = joined_by_core(in_mine)
    weights_in, weights_out = weights_all[:, :PACK], weights_all[:, PACK:]

    taps_here = jnp.concatenate(
        [
            conv_query.reshape(CONV, head_count, KEY_SIZE),
            conv_key.reshape(CONV, head_count, KEY_SIZE),
            conv_value.reshape(CONV, head_count, DV),
        ],
        axis=2,
    ).transpose(1, 0, 2)
    taps_there = swap_cores(taps_here)
    taps = lax.dynamic_index_in_dim(
        jnp.where(chip // head_count == core, taps_here, taps_there), chip % head_count, 0, False
    ).astype(F32)
    taps = stacked([taps, jnp.zeros_like(taps)])
    gain_head = jnp.broadcast_to(head_gain.astype(F32)[None], (8, DV))
    seen = in_mine[:, :8, PACK - tok_rows // 2 : PACK].astype(F32).reshape(CHIPS, 4, tok_rows)
    rate = (seen[:, 0] + seen[:, 1] + seen[:, 2]).reshape(-1)
    starts = seen[:, 3].reshape(-1)
    decay_grid, cols, rows = stream_tables(rate, starts)

    blocks = jnp.arange(CHIPS * CORES)
    far = blocks // CORES
    place = (
        4 * ((far ^ chip) % 4) + (chip // 4 - far // 4) % 4 + CHIPS * (blocks % CORES != core)
    ).astype(jnp.int32)

    raw = nn(normed_all, weights_in)
    column = lax.broadcasted_iota(jnp.int32, raw.shape, 1)
    pre_own = jnp.where(
        column == LOGIT + 1,
        raw - lax.reduce_precision(raw, exponent_bits=8, mantissa_bits=7),
        raw,
    ).astype(BF16)
    pre = (pre_own, swap_cores(pre_own))

    feed = jnp.concatenate(
        [
            (w_gate.astype(F32) * gain_two).astype(BF16).T.reshape(CHIPS, units, row_count),
            (w_up.astype(F32) * gain_two).astype(BF16).T.reshape(CHIPS, units, row_count),
            w_down.reshape(CHIPS, units, row_count),
        ],
        axis=1,
    )
    feed = after(feed, in_mine)
    feed_mine = exchange(feed)
    gated_own, gated_other, *kept = mixer_forward(place, *pre, decay_grid, cols, rows, taps, gain_head)
    mixed_parts = nt(gated_own, weights_out).astype(BF16)
    far = send_far(far_parts(mixed_parts))

    cot_own = own_rows(cotangent)
    far, feed_mine = after((far, feed_mine))
    near = near_parts(mixed_parts, *far)
    near, cot = send_parts(near), gather_levels(after(cot_own, near))
    feed_other = swap_cores(feed_mine)
    near, cot = after((near, cot))
    levels = level_parts(mixed_parts, *near)
    levels, cot = send_levels(levels), send_near(stacked(after(cot, levels)))

    levels, cot = after((levels, cot))
    middle = inputs_own + total_of(*levels)
    scale_two = lax.rsqrt(jnp.mean(middle * middle, axis=-1, keepdims=True) + EPSILON)
    normed_mid = middle * scale_two
    mid = normed_mid.astype(BF16)
    mid_sent, mid_own, cot_far = gather_levels(mid), send_near(mid), send_far(far_halves(after(cot, mid)))
    feed_mine, feed_other = after((feed_mine, feed_other), mid)

    def unit_rows(position):
        return stacked(
            [
                part[:, position * units : (position + 1) * units].transpose(1, 0, 2).reshape(units, width)
                for part in (feed_mine, feed_other)
            ]
        )

    gate_rows, up_rows, down_rows = unit_rows(0), unit_rows(1), unit_rows(2)
    mid = mid_sent
    mid, mid_own, cot_far, gate_rows, up_rows, down_rows = after(
        (mid, mid_own, cot_far, gate_rows, up_rows, down_rows)
    )
    mid = stacked(mid[1:])
    cot_all = stacked(after(cot, mid) + cot_far)
    mid, mid_own_far = send_near(mid), send_far(far_halves(mid_own))
    d_hidden = nt(cot_all, down_rows).astype(BF16)
    mid, mid_own_far, d_hidden = after((mid, mid_own_far, d_hidden))
    mid_all = by_planes(four_blocks(mid_own, mid_own_far), four_blocks(mid, send_far(far_halves(mid))))

    gate_lin = nt(mid_all, gate_rows)
    up_lin = nt(mid_all, up_rows)
    d_hidden = d_hidden.astype(F32)
    sig = jax.nn.sigmoid(gate_lin)
    act = gate_lin * sig
    hidden = (act * up_lin).astype(BF16)
    d_gate = (d_hidden * up_lin * (sig * (1.0 + gate_lin * (1.0 - sig)))).astype(BF16)
    d_up = (d_hidden * act).astype(BF16)
    e_parts = (nn(d_gate, gate_rows) + nn(d_up, up_rows)).astype(BF16)
    far = send_far(far_parts(e_parts))
    feed_parts = nn(after(hidden, e_parts), down_rows).astype(BF16)
    far, feed_parts = after((far, feed_parts))
    near = send_parts(near_parts(e_parts, *far))

    parts = [tn(d_gate, mid_all), tn(d_up, mid_all), tn(hidden, cot_all)]
    keep_part = stacked([part[:units] for part in parts])
    give_part = stacked([part[units:] for part in parts]).astype(BF16)
    cut = after(normed_all, e_parts).reshape(own_count, CHIPS, CORES, half_count)
    cut_mine = lax.dynamic_index_in_dim(cut, core, 2, False).reshape(own_count, width // CORES)
    cut_given = lax.dynamic_index_in_dim(cut, 1 - core, 2, False).reshape(own_count, width // CORES)
    near, feed_parts, keep_part, give_part, cut_mine, cut_given = after(
        (near, feed_parts, keep_part, give_part, cut_mine, cut_given)
    )
    cut_other = swap_cores(cut_given)
    levels = level_parts(e_parts, *near)
    levels, feed_far = send_levels(levels), send_far(far_parts(after(feed_parts, levels)))
    levels, feed_far = after((levels, feed_far))
    e_two = total_of(*levels)
    d_middle = cot_own.astype(F32) + scale_two * (
        e_two - normed_mid * jnp.mean(e_two * normed_mid, axis=-1, keepdims=True)
    )
    d_mid = d_middle.astype(BF16)
    d_mid, feed_near = gather_levels(d_mid), send_parts(near_parts(feed_parts, *after(feed_far, d_mid)))
    feed_grad = (keep_part + swap_cores(give_part).astype(F32)).astype(BF16)
    feed_grad = feed_grad.reshape(3 * units, CHIPS, row_count).transpose(1, 0, 2)
    feed_grad = jnp.pad(feed_grad, ((0, 0), (0, half_count * DV // row_count), (0, 0)))
    d_mid, feed_near, feed_grad = after((d_mid, feed_near, feed_grad))
    d_mid = stacked(d_mid)
    feed_levels = level_parts(feed_parts, *after(feed_near, d_mid))
    d_mid, feed_levels = send_near(d_mid), send_levels(feed_levels)
    d_mid, feed_levels = after((d_mid, feed_levels))
    d_mid_all = stacked(d_mid + send_far(far_halves(d_mid)))

    d_gated_own = nn(d_mid_all, weights_out).astype(BF16)
    d_gated = (d_gated_own, swap_cores(d_gated_own))
    grad_out = tn(d_mid_all, gated_own).astype(BF16).reshape(CHIPS, CORES, half_count, DV)
    grad_out = total_of(
        lax.dynamic_index_in_dim(grad_out, core, 1, False),
        swap_cores(lax.dynamic_index_in_dim(grad_out, 1 - core, 1, False)),
    ).astype(BF16)
    feed_grad = lax.dynamic_update_slice(
        feed_grad, grad_out.reshape(CHIPS, half_count * DV // row_count, row_count), (0, 3 * units, 0)
    )
    feed_back = exchange(feed_grad)
    d_pre_own, d_pre_other, grad_taps, grad_gain = mixer_backward(
        place, d_gated, pre, decay_grid, cols, taps, gain_head, kept
    )


    small = jnp.concatenate([jnp.sum(grad_taps, axis=1).reshape(-1), jnp.sum(grad_gain, axis=0)])
    small = small.reshape(-1, 64)
    small_rows = small.shape[0]
    e_parts = nt(d_pre_own, weights_in).astype(BF16)
    far = far_parts(e_parts)
    late_own, late_other = after((d_pre_own, d_pre_other), far)
    far = send_far(far)
    grad_in = tn(cut_mine, late_own) + tn(cut_other, late_other)
    small = jnp.pad(small, ((0, half_count - small_rows), (PACK - 64, 0)))
    grad_in = (grad_in.reshape(CHIPS, half_count, PACK) + small).astype(BF16)
    grad_in, feed_back, far = after((grad_in, feed_back, far))
    grad_in = exchange(grad_in)
    near = send_parts(near_parts(e_parts, *far))
    near, grad_in = after((near, grad_in))
    levels = level_parts(e_parts, *near)
    grad_in, feed_back = after((grad_in, feed_back), levels)
    e_levels = send_levels(levels)
    small = grad_in[:, :small_rows, PACK - 64 :].astype(F32).reshape(CHIPS, -1)
    taps_all = lax.dynamic_slice_in_dim(small[:, : CONV * MIXED], core * head_count, head_count, 0)
    taps_all = taps_all.reshape(head_count, CONV, MIXED).transpose(1, 0, 2)

    def heads_here(back):
        mine = lax.dynamic_slice_in_dim(back, core * head_count, head_count, 0)
        given = lax.dynamic_slice_in_dim(back, (1 - core) * head_count, head_count, 0)
        return in_order(mine, swap_cores(given), 1)

    grad_in = heads_here(grad_in)
    block_out_own = (middle + total_of(*feed_levels)).astype(BF16)
    block_out = in_order(block_out_own, swap_cores(block_out_own), 0)
    grad_out = heads_here(feed_back[:, 3 * units :].reshape(CHIPS, half_count, DV))
    grad_output = grad_out.astype(F32).transpose(0, 2, 1).reshape(head_count * DV, row_count)
    feed_back = feed_back[:, : 3 * units].astype(F32)
    raw_gate = feed_back[:, :units].reshape(CHIPS * units, row_count).T
    raw_up = feed_back[:, units : 2 * units].reshape(CHIPS * units, row_count).T
    grad_down = feed_back[:, 2 * units :].reshape(CHIPS * units, row_count)
    feed_gain_part = jnp.sum(raw_gate * w_gate.astype(F32) + raw_up * w_up.astype(F32), axis=1)

    raw_query, raw_key, raw_value, raw_gating, raw_beta, mixer_gain_part = unpack_heads(
        grad_in, gain_one, w_query, w_key, w_value, w_gating, w_beta
    )
    gain_parts = jnp.stack([mixer_gain_part, feed_gain_part])
    gain_totals = gain_parts + swap_cores(gain_parts)

    others = (
        gain_totals[0],
        raw_query,
        raw_key,
        raw_value,
        raw_beta,
        raw_gating,
        taps_all[:, :, :KEY_SIZE].reshape(CONV, head_count * KEY_SIZE),
        taps_all[:, :, KEY_SIZE : 2 * KEY_SIZE].reshape(CONV, head_count * KEY_SIZE),
        taps_all[:, :, 2 * KEY_SIZE :].reshape(CONV, head_count * DV),
        jnp.sum(small[:, CONV * MIXED :], axis=0),
        grad_output,
        gain_totals[1],
        raw_gate * gain_two,
        raw_up * gain_two,
        grad_down,
    )
    e_levels, block_out, others = after((e_levels, block_out, others))
    e_one = total_of(*e_levels)
    grad_own = d_middle + scale_one * (
        e_one - normed_one * jnp.mean(e_one * normed_one, axis=-1, keepdims=True)
    )
    grad_inputs = in_order(grad_own, swap_cores(grad_own), 0)
    return (block_out, grad_inputs) + others


EXACT_PRECISION = lax.Precision.HIGHEST


def passed_along(value, axis, steps):
    count = lax.axis_size(axis)
    first, last = (max(0, -steps), min(count, count - steps))
    return lax.ppermute(value, axis, [(source, source + steps) for source in range(first, last)])


def entering(value, axis, join, neutral):
    count, mine = (lax.axis_size(axis), lax.axis_index(axis))
    pieces = jax.tree.map(lambda part: lax.all_gather(part, axis), value)
    subtotal = jax.tree.map(
        lambda part, zero: jnp.full_like(part, 0) + jnp.asarray(zero, part.dtype), value, neutral
    )

    def lap(position, subtotal):
        longer = join(subtotal, jax.tree.map(lambda part: part[position], pieces))
        return jax.tree.map(lambda new, old: jnp.where(position < mine, new, old), longer, subtotal)

    return lax.fori_loop(0, count - 1, lap, subtotal)


def carried_in(shard, axis, join, neutral):
    count = lax.axis_size(axis)
    place = lax.axis_index(axis)
    ahead = count - 1 - place
    gathered = jax.tree.map(
        lambda a, kind: lax.all_gather(a.astype(kind), axis),
        shard,
        jax.tree.map(lambda a: jnp.bfloat16 if a.dtype == jnp.float32 else a.dtype, shard),
    )
    state = jax.tree.map(lambda a, e: jnp.zeros_like(a) + jnp.asarray(e, a.dtype), shard, neutral)

    def one(lap, state):
        source = count - 1 - lap
        return join(
            state,
            jax.tree.map(
                lambda a, own: lax.dynamic_index_in_dim(a, source, 0, False).astype(own.dtype),
                gathered,
                shard,
            ),
        )

    return lax.fori_loop(0, ahead, one, state)


def high_einsum(einsum_form, *arrays):
    return jnp.einsum(
        einsum_form, *arrays, precision=EXACT_PRECISION, preferred_element_type=jnp.float32
    )


def low_dot(left_side, right_side):
    return jnp.dot(left_side, right_side, preferred_element_type=jnp.float32)


def inner_dot(left_side, right_side):
    return lax.dot_general(
        left_side, right_side, (((0,), (0,)), ((), ())), preferred_element_type=jnp.float32
    )


def outer_dot(left_side, right_side):
    return lax.dot_general(
        left_side, right_side, (((1,), (1,)), ((), ())), preferred_element_type=jnp.float32
    )


def rounded(values):
    return lax.optimization_barrier(values.astype(jnp.bfloat16)).astype(jnp.float32)


def scale_norm(values, gain_vec):
    return (
        values * lax.rsqrt(jnp.mean(values * values, axis=-1, keepdims=True) + EPSILON) * gain_vec
    )


def unit_rows(values):
    return values * lax.rsqrt(jnp.sum(values * values, axis=-1, keepdims=True) + EPSILON)


def swiglu(gate_lin, up_lin):
    return jax.nn.silu(gate_lin) * up_lin


def compose_maps(earlier_map, later_map):
    return (
        high_einsum("hde,hef->hdf", later_map[0], earlier_map[0]),
        high_einsum("hde,hef->hdf", later_map[0], earlier_map[1]) + later_map[1],
    )


def gather_plan(
    inputs,
    doc_starts,
    decay_rate,
    mixer_gain,
    w_query,
    w_key,
    w_value,
    w_beta,
    w_gating,
    conv_query,
    conv_key,
    conv_value,
    head_gain,
    w_output,
    feed_gain,
    w_gate,
    w_up,
    w_down,
    cotangent,
):
    tok_rows = inputs.shape[0]
    head_count = decay_rate.shape[1]
    key_width = w_query.shape[1]
    value_width = w_value.shape[1]
    edge_count = CONV - 1
    block_count = tok_rows // BLOCK
    gathered = (
        lax.all_gather(mixer_gain, "seq", axis=0, tiled=True),
        lax.all_gather(w_query, "seq", axis=0, tiled=True),
        lax.all_gather(w_key, "seq", axis=0, tiled=True),
        lax.all_gather(w_value, "seq", axis=0, tiled=True),
        lax.all_gather(w_beta, "seq", axis=0, tiled=True),
        lax.all_gather(w_gating, "seq", axis=0, tiled=True),
        lax.all_gather(w_output, "seq", axis=1, tiled=True),
        lax.all_gather(feed_gain, "seq", axis=0, tiled=True),
        lax.all_gather(w_gate, "seq", axis=0, tiled=True),
        lax.all_gather(w_up, "seq", axis=0, tiled=True),
        lax.all_gather(w_down, "seq", axis=1, tiled=True),
    )
    (
        gain_one,
        full_query,
        full_key,
        full_value,
        full_beta,
        full_gating,
        full_output,
        gain_two,
        full_gate,
        full_up,
        full_down,
    ) = gathered
    inputs_float = inputs.astype(jnp.float32)
    normed_float, norm_one_back = jax.vjp(scale_norm, inputs_float, gain_one.astype(jnp.float32))
    normed_one = normed_float.astype(jnp.bfloat16)
    query_pre = low_dot(normed_one, full_query).astype(jnp.bfloat16)
    key_pre = low_dot(normed_one, full_key).astype(jnp.bfloat16)
    value_pre = low_dot(normed_one, full_value).astype(jnp.bfloat16)
    gating_pre = low_dot(normed_one, full_gating).astype(jnp.bfloat16)
    beta_logit = low_dot(normed_one, full_beta)
    joined = jnp.concatenate([query_pre, key_pre, value_pre], axis=1)
    tail_starts = doc_starts[tok_rows - edge_count :]
    later_starts = jnp.cumsum(tail_starts[::-1])[::-1] - tail_starts
    sender_keep = (later_starts == 0).astype(jnp.bfloat16)[:, None]
    edge_in = passed_along(joined[tok_rows - edge_count :] * sender_keep, "seq", 1)
    local_doc = jnp.cumsum(doc_starts)
    padded_doc = jnp.concatenate([jnp.zeros((edge_count,), local_doc.dtype), local_doc])
    keep_masks = [
        (
            padded_doc[edge_count - shift_lag : edge_count - shift_lag + tok_rows] == local_doc
        ).astype(jnp.float32)[:, None]
        for shift_lag in range(CONV)
    ]

    def conv_piece(extended, conv_weights):
        mixed = keep_masks[0] * conv_weights[0] * extended[edge_count:]
        for shift_lag in range(1, CONV):
            mixed = (
                mixed
                + keep_masks[shift_lag]
                * conv_weights[shift_lag]
                * extended[edge_count - shift_lag : edge_count - shift_lag + tok_rows]
            )
        activated = jax.nn.silu(mixed)
        query_unit = unit_rows(activated[:, :key_width].reshape(tok_rows, head_count, KEY_SIZE))
        key_unit = unit_rows(
            activated[:, key_width : 2 * key_width].reshape(tok_rows, head_count, KEY_SIZE)
        )
        value_act = activated[:, 2 * key_width :].reshape(tok_rows, head_count, DV)
        return (query_unit, key_unit, value_act)

    extended = jnp.concatenate([edge_in, joined], axis=0).astype(jnp.float32)
    conv_weights = jnp.concatenate([conv_query, conv_key, conv_value], axis=1).astype(jnp.float32)
    (query_unit, key_unit, value_act), conv_back = jax.vjp(conv_piece, extended, conv_weights)

    def to_blocks(values):
        return values.reshape(block_count, BLOCK, head_count, values.shape[-1]).transpose(
            0, 2, 1, 3
        )

    def from_blocks(values):
        return values.transpose(0, 2, 1, 3).reshape(tok_rows, head_count, values.shape[-1])

    log_rate = jnp.log(decay_rate).reshape(block_count, BLOCK, head_count).transpose(0, 2, 1)
    log_level = jnp.cumsum(log_rate, axis=-1)
    segment = jnp.cumsum(doc_starts.reshape(block_count, BLOCK), axis=-1)
    positions = jnp.arange(BLOCK)
    causal = positions[:, None] >= positions[None, :]
    strict = positions[:, None] > positions[None, :]
    linked = (segment[:, None, :, None] == segment[:, None, None, :]) & causal
    spread = jnp.where(causal, log_level[..., :, None] - log_level[..., None, :], 0.0)
    decay_grid = jnp.where(linked, jnp.exp(spread), 0.0)
    carry_in = jnp.where(segment[:, None, :] == 0, jnp.exp(log_level), 0.0)
    tail_decay = decay_grid[..., BLOCK - 1, :]
    key_eye = jnp.eye(KEY_SIZE, dtype=jnp.float32)
    block_eye = jnp.eye(BLOCK, dtype=jnp.float32)

    def block_terms(query_blocks, key_blocks, value_blocks, logit_blocks):
        beta_gate = jax.nn.sigmoid(logit_blocks)
        key_gram = high_einsum("nhcd,nhmd->nhcm", key_blocks, key_blocks)
        system = block_eye + jnp.where(strict, decay_grid * key_gram * beta_gate[..., None, :], 0.0)
        right_side = jnp.concatenate([value_blocks, carry_in[..., None] * key_blocks], axis=-1)
        solved = jax.scipy.linalg.solve_triangular(
            system, right_side, lower=True, unit_diagonal=True
        )
        fresh_values = solved[..., :DV]
        fresh_keys = solved[..., DV:]
        mixing = (
            high_einsum("nhcd,nhmd->nhcm", query_blocks, key_blocks)
            * decay_grid
            * beta_gate[..., None, :]
        )
        weighted = key_blocks * (tail_decay * beta_gate)[..., None]
        block_maps = carry_in[..., BLOCK - 1, None, None] * key_eye - high_einsum(
            "nhcd,nhce->nhde", weighted, fresh_keys
        )
        block_adds = high_einsum("nhcd,nhce->nhde", weighted, fresh_values)

        def chain_step(current, element):
            return (compose_maps(current, element), None)

        start_map = (
            jnp.broadcast_to(key_eye, (head_count, KEY_SIZE, KEY_SIZE)),
            jnp.zeros((head_count, KEY_SIZE, DV), jnp.float32),
        )
        device_pair, _ = lax.scan(chain_step, start_map, (block_maps, block_adds))
        return (
            (fresh_values, fresh_keys, mixing, block_maps, block_adds),
            device_pair[0],
            device_pair[1],
        )

    def block_outputs(block_parts, query_blocks, start_state):

        def step_block(current, element):
            fresh_values, fresh_keys, mixing, block_map, block_add, query_part, carry_part = element
            updated = fresh_values - high_einsum("hcd,hde->hce", fresh_keys, current)
            produced_output = (
                carry_part[..., None] * high_einsum("hcd,hde->hce", query_part, current)
                + high_einsum("hcm,hme->hce", mixing, updated)
            ) * KEY_SIZE ** (-0.5)
            return (high_einsum("hde,hef->hdf", block_map, current) + block_add, produced_output)

        _, emitted_all = lax.scan(step_block, start_state, block_parts + (query_blocks, carry_in))
        return emitted_all

    query_blocks = to_blocks(rounded(query_unit))
    key_blocks = to_blocks(rounded(key_unit))
    value_blocks = to_blocks(rounded(value_act))
    logit_blocks = beta_logit.reshape(block_count, BLOCK, head_count).transpose(0, 2, 1)
    (block_parts, device_map, device_add), terms_back = jax.vjp(
        block_terms, query_blocks, key_blocks, value_blocks, logit_blocks
    )
    identity = (jnp.broadcast_to(key_eye, device_map.shape), jnp.zeros_like(device_add))
    prefix = entering((device_map, device_add), "seq", compose_maps, identity)
    start_state = prefix[1]
    produced_output, emitted_back = jax.vjp(block_outputs, block_parts, query_blocks, start_state)

    def gated_norm(values, gating_values, gain_vec):
        normed_out = values * lax.rsqrt(jnp.mean(values * values, axis=-1, keepdims=True) + EPSILON)
        return (normed_out * gain_vec * jax.nn.silu(gating_values)).reshape(tok_rows, value_width)

    mixer_out = from_blocks(produced_output)
    gated_float, gated_back = jax.vjp(
        gated_norm,
        mixer_out,
        gating_pre.astype(jnp.float32).reshape(tok_rows, head_count, DV),
        head_gain.astype(jnp.float32),
    )
    gated_out = gated_float.astype(jnp.bfloat16)
    middle = inputs_float + lax.psum(
        low_dot(gated_out, full_output).astype(jnp.bfloat16), "head"
    ).astype(jnp.float32)
    normed_middle, norm_two_back = jax.vjp(scale_norm, middle, gain_two.astype(jnp.float32))
    normed_two = normed_middle.astype(jnp.bfloat16)
    gate_lin = low_dot(normed_two, full_gate)
    up_lin = low_dot(normed_two, full_up)
    hidden_float, swiglu_back = jax.vjp(swiglu, gate_lin, up_lin)
    hidden = hidden_float.astype(jnp.bfloat16)
    feed_out = lax.psum(low_dot(hidden, full_down).astype(jnp.bfloat16), "head").astype(jnp.float32)
    block_out = (middle + feed_out).astype(jnp.bfloat16)
    regathered = (
        lax.all_gather(w_query, "seq", axis=0, tiled=True),
        lax.all_gather(w_key, "seq", axis=0, tiled=True),
        lax.all_gather(w_value, "seq", axis=0, tiled=True),
        lax.all_gather(w_beta, "seq", axis=0, tiled=True),
        lax.all_gather(w_gating, "seq", axis=0, tiled=True),
        lax.all_gather(w_output, "seq", axis=1, tiled=True),
        lax.all_gather(w_gate, "seq", axis=0, tiled=True),
        lax.all_gather(w_up, "seq", axis=0, tiled=True),
        lax.all_gather(w_down, "seq", axis=1, tiled=True),
    )
    (
        full_query,
        full_key,
        full_value,
        full_beta,
        full_gating,
        full_output,
        full_gate,
        full_up,
        full_down,
    ) = regathered
    cotangent_float = cotangent.astype(jnp.float32)
    grad_down = inner_dot(hidden, cotangent)
    d_hidden = rounded(outer_dot(cotangent, full_down))
    d_gate_float, d_up_float = swiglu_back(d_hidden)
    d_gate = d_gate_float.astype(jnp.bfloat16)
    d_up = d_up_float.astype(jnp.bfloat16)
    grad_gate = inner_dot(normed_two, d_gate)
    grad_up = inner_dot(normed_two, d_up)
    d_normed_two = lax.psum(
        (outer_dot(d_gate, full_gate) + outer_dot(d_up, full_up)).astype(jnp.bfloat16), "head"
    ).astype(jnp.float32)
    d_middle_norm, grad_gain_two = norm_two_back(d_normed_two)
    d_middle = cotangent_float + d_middle_norm
    d_middle_low = d_middle.astype(jnp.bfloat16)
    grad_output = inner_dot(gated_out, d_middle_low)
    d_gated = rounded(outer_dot(d_middle_low, full_output))
    d_mixer_out, d_gating_float, grad_head_part = gated_back(d_gated)
    d_gating = d_gating_float.reshape(tok_rows, value_width).astype(jnp.bfloat16)
    d_parts, d_query_late, d_start = emitted_back(to_blocks(d_mixer_out))
    chained = carried_in((jnp.swapaxes(device_map, 1, 2), d_start), "seq", compose_maps, identity)
    d_end = chained[1]
    d_map = high_einsum("hde,hfe->hdf", d_end, start_state)
    d_query_early, d_key_blocks, d_value_blocks, d_logit_blocks = terms_back(
        (d_parts, d_map, d_end)
    )
    d_query_unit = rounded(from_blocks(d_query_early + d_query_late))
    d_key_unit = rounded(from_blocks(d_key_blocks))
    d_value_act = rounded(from_blocks(d_value_blocks))
    d_beta_logit = (
        d_logit_blocks.transpose(0, 2, 1).reshape(tok_rows, head_count).astype(jnp.bfloat16)
    )
    d_extended, grad_conv_all = conv_back((d_query_unit, d_key_unit, d_value_act))
    returned = passed_along(d_extended[:edge_count].astype(jnp.bfloat16), "seq", -1).astype(
        jnp.float32
    )
    d_rows = d_extended[edge_count:]
    d_rows = jnp.concatenate(
        [
            d_rows[: tok_rows - edge_count],
            d_rows[tok_rows - edge_count :] + returned * sender_keep.astype(jnp.float32),
        ],
        axis=0,
    )
    d_joined = d_rows.astype(jnp.bfloat16)
    d_query_pre = d_joined[:, :key_width]
    d_key_pre = d_joined[:, key_width : 2 * key_width]
    d_value_pre = d_joined[:, 2 * key_width :]
    grad_query = inner_dot(normed_one, d_query_pre)
    grad_key = inner_dot(normed_one, d_key_pre)
    grad_value = inner_dot(normed_one, d_value_pre)
    grad_gating = inner_dot(normed_one, d_gating)
    grad_beta = inner_dot(normed_one, d_beta_logit)
    d_normed_part = (
        outer_dot(d_query_pre, full_query)
        + outer_dot(d_key_pre, full_key)
        + outer_dot(d_value_pre, full_value)
        + outer_dot(d_gating, full_gating)
        + outer_dot(d_beta_logit, full_beta)
    )
    d_normed_one, head_total = (
        lax.psum(d_normed_part.astype(jnp.bfloat16), "head").astype(jnp.float32),
        lax.psum(grad_head_part.astype(jnp.bfloat16), "head").astype(jnp.float32),
    )
    d_inputs_norm, grad_gain_one = norm_one_back(d_normed_one)
    grad_inputs = d_middle + d_inputs_norm
    small_totals = lax.psum((grad_conv_all, head_total), "seq")
    conv_total = small_totals[0]
    totals = (
        lax.psum_scatter(grad_gain_one, "seq", scatter_dimension=0, tiled=True),
        lax.psum_scatter(grad_query, "seq", scatter_dimension=0, tiled=True),
        lax.psum_scatter(grad_key, "seq", scatter_dimension=0, tiled=True),
        lax.psum_scatter(grad_value, "seq", scatter_dimension=0, tiled=True),
        lax.psum_scatter(grad_beta, "seq", scatter_dimension=0, tiled=True),
        lax.psum_scatter(grad_gating, "seq", scatter_dimension=0, tiled=True),
        lax.psum_scatter(grad_output, "seq", scatter_dimension=1, tiled=True),
        lax.psum_scatter(grad_gain_two, "seq", scatter_dimension=0, tiled=True),
        lax.psum_scatter(grad_gate, "seq", scatter_dimension=0, tiled=True),
        lax.psum_scatter(grad_up, "seq", scatter_dimension=0, tiled=True),
        lax.psum_scatter(grad_down, "seq", scatter_dimension=1, tiled=True),
    )
    return (
        block_out,
        grad_inputs,
        totals[0],
        totals[1],
        totals[2],
        totals[3],
        totals[4],
        totals[5],
        conv_total[:, :key_width],
        conv_total[:, key_width : 2 * key_width],
        conv_total[:, 2 * key_width :],
        small_totals[1],
        totals[6],
        totals[7],
        totals[8],
        totals[9],
        totals[10],
    )


def solution(mesh):
    in_specs = (
        P("seq", None),
        P("seq"),
        P("seq", "head"),
        P("seq"),
        P("seq", "head"),
        P("seq", "head"),
        P("seq", "head"),
        P("seq", "head"),
        P("seq", "head"),
        P(None, "head"),
        P(None, "head"),
        P(None, "head"),
        P(),
        P("head", "seq"),
        P("seq"),
        P("seq", "head"),
        P("seq", "head"),
        P("head", "seq"),
        P("seq", None),
    )
    out_specs = (
        P("seq", None),
        P("seq", None),
        P("seq"),
        P("seq", "head"),
        P("seq", "head"),
        P("seq", "head"),
        P("seq", "head"),
        P("seq", "head"),
        P(None, "head"),
        P(None, "head"),
        P(None, "head"),
        P(),
        P("head", "seq"),
        P("seq"),
        P("seq", "head"),
        P("seq", "head"),
        P("head", "seq"),
    )
    whole_heads = mesh.shape["seq"] == CHIPS and mesh.shape["head"] == CORES
    per_device = head_plan if whole_heads else gather_plan
    return jax.shard_map(
        per_device, mesh=mesh, in_specs=in_specs, out_specs=out_specs, check_vma=False
    )
```
